256 devices in a mesh: shard: 128 (over y, z, x), rep: 2 (over core).
Axes of the slice: x: 4, y: 4, z: 8, core: 2. Of those that a mesh axis runs over, the one named last changes fastest.
Arguments:
- queries: bfloat16 [1024, 768], P(('shard', 'rep')), may hold values from -2 to 2
- slab: bfloat16 [262144, 768], P('shard'), may hold values from -2 to 2
- cand_ids: int32 [1024, 16], P(('shard', 'rep')), may hold values from 0 to 260127, as said below
- patches: bfloat16 [4096, 40, 1024], P('shard'), may hold values from -92 to 92
- text_states: bfloat16 [1024, 16, 768], P(('shard', 'rep')), may hold values from -8 to 8
- w_query: bfloat16 [768, 768], P(None, 'rep'), may hold values from -0.21875 to 0.21875
- w_key: bfloat16 [1024, 768], P(None, 'rep'), may hold values from -0.1875 to 0.1875
- w_value: bfloat16 [1024, 768], P(None, 'rep'), may hold values from -0.1875 to 0.1875
- w_out: bfloat16 [768, 768], P(None, 'rep'), may hold values from -0.21875 to 0.21875
- norm_gain: float32 [768], replicated, may hold values from 0.1 to 1.9
Outputs:
- retrieval: float32 [1024, 16], P(('shard', 'rep'))
- attended: bfloat16 [1024, 16, 16, 768], P(('shard', 'rep'))
The draws below stay inside these ranges and needn't reach their ends.
Inputs may be any that keep to these rules, and one draw needn't show every extreme that they name: `cand_ids`: each id is c * 2048 + r with r below 32. Among the ids of one device's block of 4 queries (rows b * 4 to b * 4 + 3), at most 1 lie on any one shard c, and on some shard exactly 1.
All inputs are finite; a program needn't handle non-finite values.
Results may differ from the reference program's by a relative error of at most 0.0039.
The reference program's roundings to bfloat16 on the way count: a program that leaves them out, or rounds other values in their place, can miss the bound.
Values may be sent and summed in bfloat16 or wider, within the bound.
No kernel may reach another device: no remote copies, remote signals or barrier semaphores. Data moves between devices by JAX's collectives and lax.ppermute only.
A program may use at most 192 MiB of HBM per device.

```python
import math
import jax
import jax.numpy as jnp
from jax import lax

E = 768
D = 768
HEADS = 12
DP = 1024
TEXT = 16
PATCHES = 40
TOPK = 16
Q_DEV = 4
SLAB_DEV = 2048
STORE = 32
CAP = 1
QUERIES = 1024
SLAB_ROWS = 262144
STORED = 4096
N_SHARD = 128


def draw_queries(key, part):
    key = jax.random.fold_in(key, 11)
    values = jnp.clip(jax.random.normal(key, (QUERIES, E), jnp.float32), -6.0, 6.0) * E ** (-0.5)
    return values.astype(jnp.bfloat16)


def draw_slab(key, part):
    key = jax.random.fold_in(key, 12)
    rising = 0.83 + 0.1 * jnp.arange(SLAB_ROWS, dtype=jnp.float32) / SLAB_ROWS
    values = jnp.clip(jax.random.normal(key, (SLAB_ROWS, E), jnp.float32), -6.0, 6.0) * E ** (-0.5) * rising[:, None]
    return values.astype(jnp.bfloat16)


def draw_cand_ids(key, part):
    key = jax.random.fold_in(key, 13)
    owners = QUERIES // Q_DEV
    span = Q_DEV * TOPK
    owner_keys = jax.random.split(key, owners)
    order = jax.vmap(lambda each: jax.random.permutation(each, N_SHARD * CAP))(owner_keys)[:, :span]
    source = order // CAP
    local = jax.random.randint(jax.random.fold_in(key, 1), (owners, span), 0, STORE)
    ids = source * SLAB_DEV + local
    return ids.reshape(QUERIES, TOPK).astype(jnp.int32)


def draw_patches(key, part):
    key = jax.random.fold_in(key, 14)
    first = jax.random.fold_in(key, 0)
    values = jnp.clip(jax.random.normal(first, (STORED, PATCHES, DP), jnp.float32), -6.0, 6.0)
    return values.astype(jnp.bfloat16)


def draw_text_states(key, part):
    key = jax.random.fold_in(key, 15)
    first = jax.random.fold_in(key, 0)
    values = jnp.clip(jax.random.normal(first, (QUERIES, TEXT, D), jnp.float32), -6.0, 6.0)
    return values.astype(jnp.bfloat16)


def block_levels(stream_key, shape, pieces, low, largest):
    def one(dim, blocks):
        draws = jax.random.uniform(jax.random.fold_in(jax.random.fold_in(stream_key, 6), dim), (blocks,), jnp.float32, low / len(pieces), largest / len(pieces))
        return jnp.repeat(jnp.exp(draws), shape[dim] // blocks).reshape((-1,) + (1,) * (len(shape) - dim - 1))

    factor_of = one(*pieces[0])
    for cut in pieces[1:]:
        factor_of = factor_of * one(*cut)
    return factor_of


def bell_draw(key, shape, deviation, limit, cuts=(), held_as=jnp.bfloat16):
    gain = block_levels(key, shape, cuts, -0.22, 0.18) if cuts else 1.0
    result = jax.random.normal(key, shape, jnp.float32) * deviation * gain
    return jnp.minimum(jnp.maximum(result, -limit), limit).astype(held_as)


def setup_inputs(seed: int = 0) -> dict:
    key_list = jax.random.split(jax.random.key(seed), 11)
    return {
        "queries": draw_queries(jax.random.fold_in(key_list[10], 71), 0),
        "slab": draw_slab(jax.random.fold_in(key_list[10], 71), 0),
        "cand_ids": draw_cand_ids(jax.random.fold_in(key_list[10], 71), 0),
        "patches": draw_patches(jax.random.fold_in(key_list[10], 71), 0),
        "text_states": draw_text_states(jax.random.fold_in(key_list[10], 71), 0),
        "w_query": bell_draw(key_list[5], (D, D), D ** -0.5, 0.21875, ((1, 2),)),
        "w_key": bell_draw(key_list[6], (DP, D), DP ** -0.5, 0.1875, ((1, 2),)),
        "w_value": bell_draw(key_list[7], (DP, D), DP ** -0.5, 0.1875, ((1, 2),)),
        "w_out": bell_draw(key_list[8], (D, D), D ** -0.5, 0.21875, ((1, 2),)),
        "norm_gain": jnp.clip(1.0 + 0.18 * jax.random.normal(key_list[9], (D,), jnp.float32), 0.1, 1.9),
    }


SCALE = 100.0
EPSILON = 1e-06

def attend(projected, key_rows, value_rows):
    batch, text_count, width = projected.shape
    patch_count = key_rows.shape[1]
    head_size = width // HEADS
    query_heads = projected.astype(jnp.float32).reshape(batch, text_count, HEADS, head_size)
    key_heads = key_rows.astype(jnp.float32).reshape(batch, patch_count, HEADS, head_size)
    value_heads = value_rows.astype(jnp.float32).reshape(batch, patch_count, HEADS, head_size)
    scores = jnp.einsum('bthd,bphd->bhtp', query_heads, key_heads) * head_size ** (-0.5)
    highest = lax.optimization_barrier(jnp.max(scores, axis=-1, keepdims=True))
    weights = jnp.exp(scores - highest)
    weights = (weights / lax.optimization_barrier(jnp.sum(weights, axis=-1, keepdims=True))).astype(jnp.bfloat16)
    context = jnp.einsum('bhtp,bphd->bthd', weights.astype(jnp.float32), value_heads)
    return context.reshape(batch, text_count, width).astype(jnp.bfloat16)

def layer_norm(summed, norm_gain):
    mean = lax.optimization_barrier(jnp.mean(summed, axis=-1, keepdims=True))
    centred = summed - mean
    variance = lax.optimization_barrier(jnp.mean(centred * centred, axis=-1, keepdims=True))
    return (centred * lax.rsqrt(variance + EPSILON) * norm_gain).astype(jnp.bfloat16)

def reference(queries, slab, cand_ids, patches, text_states, w_query, w_key, w_value, w_out, norm_gain):
    blocks = slab.reshape(N_SHARD, SLAB_DEV, E)

    def block_stats(block):
        logits = SCALE * jnp.dot(queries, block.T, preferred_element_type=jnp.float32)
        block_peak = lax.optimization_barrier(jnp.max(logits, axis=1))
        return (block_peak, lax.optimization_barrier(jnp.sum(jnp.exp(logits - block_peak[:, None]), axis=1)))
    peaks, totals = lax.map(block_stats, blocks)
    highest = lax.optimization_barrier(jnp.max(peaks, axis=0))
    combined = lax.optimization_barrier(jnp.sum(totals * jnp.exp(peaks - highest[None, :]), axis=0))
    normalizer = highest + jnp.log(combined)
    cand_rows = slab[cand_ids]
    cand_logits = SCALE * jnp.einsum('qe,qke->qk', queries.astype(jnp.float32), cand_rows.astype(jnp.float32))
    retrieval = cand_logits - normalizer[:, None] + math.log(SLAB_ROWS)
    stored = patches.reshape(N_SHARD, STORE, PATCHES, DP)
    key_weight = w_key.astype(jnp.float32)
    value_weight = w_value.astype(jnp.float32)

    def project_block(block):
        block_wide = block.astype(jnp.float32)
        key_block = jnp.einsum('spc,cd->spd', block_wide, key_weight).astype(jnp.bfloat16)
        value_block = jnp.einsum('spc,cd->spd', block_wide, value_weight).astype(jnp.bfloat16)
        return (key_block, value_block)
    key_store, value_store = lax.map(project_block, stored)
    key_store = key_store.reshape(STORED, PATCHES, D)
    value_store = value_store.reshape(STORED, PATCHES, D)
    projected_text = jnp.dot(text_states.reshape(QUERIES * TEXT, D), w_query, preferred_element_type=jnp.float32)
    projected_text = projected_text.astype(jnp.bfloat16).reshape(QUERIES, TEXT, D)
    slot_index = (cand_ids // SLAB_DEV * STORE + cand_ids % SLAB_DEV).astype(jnp.int32)

    def one_query(item):
        projected, states, slots = item
        spread_text = jnp.broadcast_to(projected[None], (TOPK, TEXT, D))
        context = attend(spread_text, key_store[slots], value_store[slots])
        mixed = jnp.dot(context.reshape(TOPK * TEXT, D), w_out, preferred_element_type=jnp.float32)
        summed = states.astype(jnp.float32)[None] + mixed.reshape(TOPK, TEXT, D)
        return layer_norm(summed, norm_gain)
    attended = lax.map(one_query, (projected_text, text_states, slot_index))
    return (retrieval, attended)
```

```python
import functools
import math

import jax
import jax.numpy as jnp
from jax import lax
from jax.experimental import pallas as pl
from jax.experimental.pallas import tpu as pltpu
from jax.sharding import PartitionSpec as P

HEADS = 12
SCALE = 100.0
EPSILON = 1e-06
LANES = 128
EXTRA = 8
UNROLL = 4
VMEM_LIMIT = 48 * 1024 * 1024


def row_of(shape, dim):
    return lax.broadcasted_iota(jnp.int32, shape, dim)


def request_kernel(row_ids, list_ids, text, w_own, w_other, out, projected, *, top_count, query_count):
    step = pl.program_id(0)
    block = out.shape[0]
    rows = text.shape[0] // query_count

    @pl.when(step == 0)
    def _():
        at = 0
        for weight in (w_own, w_other):
            half = jnp.dot(text[...], weight[...], preferred_element_type=jnp.float32).astype(jnp.bfloat16)
            for c in range(half.shape[1] // LANES):
                for q in range(query_count):
                    projected[q, at : at + rows, :] = half[q * rows : (q + 1) * rows, c * LANES : (c + 1) * LANES]
                at += rows

    body = projected.shape[1]
    tile_row = row_of((EXTRA, LANES), 0)
    for i in range(block):
        slot = step * block + i
        listed = list_ids[slot]
        out[i, :body, :] = projected[lax.div(jnp.maximum(listed, 0), top_count)]
        code = jnp.where(tile_row == 0, row_ids[slot].astype(jnp.float32), listed.astype(jnp.float32))
        out[i, body:, :] = code.astype(jnp.bfloat16)


def make_request(row_ids, list_ids, text, w_own, w_other, top_count, query_count):
    slots = row_ids.shape[0]
    rows = text.shape[0] // query_count
    width = w_own.shape[1] + w_other.shape[1]
    body = width // LANES * rows
    block = min(16, slots)
    whole = lambda shape: pl.BlockSpec(shape, lambda i, *_: (0, 0))
    return pl.pallas_call(
        functools.partial(request_kernel, top_count=top_count, query_count=query_count),
        grid_spec=pltpu.PrefetchScalarGridSpec(
            num_scalar_prefetch=2,
            grid=(slots // block,),
            in_specs=[whole(text.shape), whole(w_own.shape), whole(w_other.shape)],
            out_specs=pl.BlockSpec((block, body + EXTRA, LANES), lambda i, *_: (i, 0, 0)),
            scratch_shapes=[pltpu.VMEM((query_count, body, LANES), jnp.bfloat16)],
        ),
        out_shape=jax.ShapeDtypeStruct((slots, body + EXTRA, LANES), jnp.bfloat16),
        compiler_params=pltpu.CompilerParams(vmem_limit_bytes=VMEM_LIMIT),
        cost_estimate=pl.CostEstimate(flops=2 * text.shape[0] * text.shape[1] * width, bytes_accessed=6 << 20, transcendentals=0),
        name="request",
    )(row_ids, list_ids, text, w_own, w_other)


def attend_group(query, keys, values, masks, head_size):
    rows = query.shape[0]
    heads = query.shape[1] // head_size
    spread = jnp.concatenate([query * masks[h].astype(query.dtype) for h in range(heads)], axis=0)
    scores = lax.dot_general(
        spread, keys, (((1,), (1,)), ((), ())), preferred_element_type=jnp.float32
    ) * head_size ** (-0.5)
    highest = jnp.max(scores, axis=-1, keepdims=True)
    weights = jnp.exp(scores - highest)
    weights = (weights / jnp.sum(weights, axis=-1, keepdims=True)).astype(jnp.bfloat16)
    mixed = jnp.dot(weights, values, preferred_element_type=jnp.float32)
    context = mixed[:rows] * masks[0]
    for h in range(1, heads):
        context = context + mixed[h * rows : (h + 1) * rows] * masks[h]
    return context.astype(jnp.bfloat16)


def attend_kernel(row_ids, got, keys, values, *rest, head_size, rows):
    stats = rest[0] if len(rest) == 3 else None
    out, listed = rest[-2:]
    slots = got.shape[0]
    body = got.shape[1]
    columns = keys.shape[2]

    def build(slot, count):
        listed[count] = slot
        return count + jnp.where(row_ids[slot] >= 0, 1, 0)

    count = lax.fori_loop(0, slots, build, 0)
    last = listed[jnp.maximum(count - 1, 0)]
    for g in range(UNROLL):
        listed[count + g] = last

    spans = []
    at = 0
    while at < columns:
        width = min(2 * LANES, columns - at)
        lane_head = row_of((rows, width), 1) // head_size
        spans.append((at, width, [jnp.where(lane_head == h, 1.0, 0.0) for h in range(width // head_size)]))
        at += width

    def group(index, carry):
        for g in range(UNROLL):
            slot = listed[index * UNROLL + g]
            image = row_ids[slot]
            for at, width, masks in spans:
                pieces = [
                    got[slot, (at // LANES + c) * rows : (at // LANES + c + 1) * rows, :] for c in range(width // LANES)
                ]
                query = pieces[0] if len(pieces) == 1 else jnp.concatenate(pieces, axis=1)
                context = attend_group(
                    query, keys[image, :, at : at + width], values[image, :, at : at + width], masks, head_size
                )
                for c in range(width // LANES):
                    out[slot, (at // LANES + c) * rows : (at // LANES + c + 1) * rows, :] = context[
                        :, c * LANES : (c + 1) * LANES
                    ]
        return carry

    lax.fori_loop(0, lax.div(count + UNROLL - 1, UNROLL), group, 0)

    if stats is not None:
        tile_row = row_of((EXTRA, LANES), 0)

        def put(slot, carry):
            exact = jnp.broadcast_to(stats[pl.ds(slot, 1), :], (EXTRA, LANES))
            high = exact.astype(jnp.bfloat16).astype(jnp.float32)
            rest_1 = exact - high
            middle = rest_1.astype(jnp.bfloat16).astype(jnp.float32)
            low = rest_1 - middle
            out[slot, body:, :] = jnp.where(
                tile_row == 0, high, jnp.where(tile_row == 1, middle, jnp.where(tile_row == 2, low, 0.0))
            ).astype(jnp.bfloat16)
            return carry

        lax.fori_loop(0, slots, put, 0)


def attend(row_ids, got, part, keys, values, stats, rows, head_size):
    slots = got.shape[0]
    body = keys.shape[2] // LANES * rows
    height = body + (0 if stats is None else EXTRA)
    operands = [got, keys, values] + ([] if stats is None else [stats])
    in_specs = [
        pl.BlockSpec((slots, body, LANES), lambda i, *_: (0, part, 0)),
        pl.BlockSpec(keys.shape, lambda i, *_: (0, 0, 0)),
        pl.BlockSpec(values.shape, lambda i, *_: (0, 0, 0)),
    ] + ([] if stats is None else [pl.BlockSpec(stats.shape, lambda i, *_: (0, 0))])
    return pl.pallas_call(
        functools.partial(attend_kernel, head_size=head_size, rows=rows),
        grid_spec=pltpu.PrefetchScalarGridSpec(
            num_scalar_prefetch=1,
            grid=(1,),
            in_specs=in_specs,
            out_specs=pl.BlockSpec((slots, height, LANES), lambda i, *_: (0, 0, 0)),
            scratch_shapes=[pltpu.SMEM((slots + UNROLL,), jnp.int32)],
        ),
        out_shape=jax.ShapeDtypeStruct((slots, height, LANES), jnp.bfloat16),
        compiler_params=pltpu.CompilerParams(vmem_limit_bytes=VMEM_LIMIT),
        cost_estimate=pl.CostEstimate(flops=4 << 30, bytes_accessed=6 << 20, transcendentals=1 << 20),
        name="attend",
    )(row_ids, *operands)


def logits_kernel(queries, slab, picked, out, logits):
    query = queries[...].astype(jnp.bfloat16)
    tile = min(256, slab.shape[0])
    peak = None
    for t in range(slab.shape[0] // tile):
        part = SCALE * lax.dot_general(
            slab[t * tile : (t + 1) * tile, :], query, (((1,), (1,)), ((), ())), preferred_element_type=jnp.float32
        )
        logits[t * tile : (t + 1) * tile, :] = part
        top = jnp.max(part, axis=0, keepdims=True)
        peak = top if peak is None else jnp.maximum(peak, top)
    total = jnp.zeros_like(peak)
    for t in range(slab.shape[0] // tile):
        total = total + jnp.sum(jnp.exp(logits[t * tile : (t + 1) * tile, :] - peak), axis=0, keepdims=True)
    store = min(tile, slab.shape[0])
    chosen = row_of((store, queries.shape[0]), 0) == picked[...]
    candidate = jnp.sum(jnp.where(chosen, logits[:store, :], 0.0), axis=0, keepdims=True)
    tile_row = row_of(out.shape, 0)
    out[...] = jnp.where(tile_row == 0, peak, jnp.where(tile_row == 1, total, candidate))


def index_stats(queries, slab, picked):
    count = queries.shape[0]
    return pl.pallas_call(
        logits_kernel,
        out_shape=jax.ShapeDtypeStruct((8, count), jnp.float32),
        scratch_shapes=[pltpu.VMEM((slab.shape[0], count), jnp.float32)],
        compiler_params=pltpu.CompilerParams(vmem_limit_bytes=VMEM_LIMIT),
        cost_estimate=pl.CostEstimate(
            flops=2 * count * slab.shape[0] * slab.shape[1], bytes_accessed=5 << 20, transcendentals=count * slab.shape[0]
        ),
        name="index_stats",
    )(queries, slab, picked)


def finish_kernel(shards, first, second, text, w_out, gain, out, merged, gathered, *, top_count, query_count):
    step = pl.program_id(0)
    rows = text.shape[1]
    half = first.shape[1]

    @pl.when(step == 0)
    def _():
        sent = second[:, half:, :].astype(jnp.float32)
        exact = jnp.sum(jnp.where(row_of(sent.shape, 1) < 3, sent, 0.0), axis=1)
        peak = jnp.max(exact, axis=0, keepdims=True)
        scaled = jnp.exp(exact - peak) * pltpu.roll(exact, LANES - query_count, 1)
        lane = row_of(peak.shape, 1)
        total = jnp.sum(scaled, axis=0, keepdims=True)
        normalizer = peak + jnp.log(jnp.where(lane < query_count, total, 1.0))
        candidate = jnp.sum(exact, axis=0, keepdims=True)
        tile_row = row_of(merged.shape, 0)
        merged[...] = jnp.where(tile_row == 0, normalizer, candidate)

    for k in range(top_count):
        shard = shards[step * top_count + k]
        for j in range(half // rows):
            gathered[k * rows : (k + 1) * rows, j * LANES : (j + 1) * LANES] = first[shard, j * rows : (j + 1) * rows, :]
            column = half // rows + j
            gathered[k * rows : (k + 1) * rows, column * LANES : (column + 1) * LANES] = second[
                shard, j * rows : (j + 1) * rows, :
            ]
    mixed = jnp.dot(gathered[...], w_out[...], preferred_element_type=jnp.float32)
    width = mixed.shape[1]
    summed = mixed.reshape(top_count, rows, width) + text[...].astype(jnp.float32)
    mean = jnp.mean(summed, axis=-1, keepdims=True)
    centred = summed - mean
    variance = jnp.mean(centred * centred, axis=-1, keepdims=True)
    normed = centred * lax.rsqrt(variance + EPSILON) * gain[...].reshape(1, 1, width)
    out[...] = normed.astype(jnp.bfloat16).reshape(out.shape)


def finish(shards, first, second, text, w_out, gain, top_count):
    query_count, rows, width = text.shape
    full = lambda a: pl.BlockSpec(a.shape, lambda i, *_: (0,) * a.ndim)
    return pl.pallas_call(
        functools.partial(finish_kernel, top_count=top_count, query_count=query_count),
        grid_spec=pltpu.PrefetchScalarGridSpec(
            num_scalar_prefetch=1,
            grid=(query_count,),
            in_specs=[
                full(first),
                full(second),
                pl.BlockSpec((1, rows, width), lambda i, *_: (i, 0, 0)),
                full(w_out),
                full(gain),
            ],
            out_specs=[
                pl.BlockSpec((1, top_count, rows, width), lambda i, *_: (i, 0, 0, 0)),
                pl.BlockSpec((8, LANES), lambda i, *_: (0, 0)),
            ],
            scratch_shapes=[pltpu.VMEM((top_count * rows, width), jnp.bfloat16)],
        ),
        out_shape=[
            jax.ShapeDtypeStruct((query_count, top_count, rows, width), jnp.bfloat16),
            jax.ShapeDtypeStruct((8, LANES), jnp.float32),
        ],
        compiler_params=pltpu.CompilerParams(vmem_limit_bytes=VMEM_LIMIT),
        cost_estimate=pl.CostEstimate(
            flops=2 * query_count * top_count * rows * width * width, bytes_accessed=7 << 20, transcendentals=0
        ),
        name="finish",
    )(shards, first, second, text, w_out, gain)


def project_rows(rows_in, weight):
    return jnp.einsum("spc,cd->spd", rows_in, weight, preferred_element_type=jnp.float32).astype(jnp.bfloat16)


def on_device(queries, slab, cand_ids, patches, text_states, w_query, w_key, w_value, w_out, norm_gain):
    shard_count = lax.axis_size("shard")
    core = lax.axis_index("rep")
    query_count, embed_width = queries.shape
    slab_count = slab.shape[0]
    top_count = cand_ids.shape[1]
    list_length = query_count * top_count
    text_count, model_width = text_states.shape[1:]
    head_size = model_width // HEADS
    swap = [(0, 1), (1, 0)]
    w_query_other = lax.ppermute(w_query, "rep", swap)

    own_list = cand_ids.reshape(list_length)
    own_anchor = own_list // slab_count
    here = own_anchor[None, :] == row_of((shard_count, 1), 0)
    row_ids = jnp.sum(jnp.where(here, own_list[None, :] % slab_count + 1, 0), axis=1) - 1
    list_ids = jnp.sum(jnp.where(here, row_of((1, list_length), 1) + 1, 0), axis=1) - 1

    request = make_request(
        row_ids,
        list_ids,
        text_states.reshape(query_count * text_count, model_width),
        w_query,
        w_query_other,
        top_count,
        query_count,
    )
    got = lax.all_to_all(request, "shard", split_axis=0, concat_axis=0, tiled=True)
    all_queries = lax.all_gather(queries.astype(jnp.float32), "shard", axis=0, tiled=True)

    w_key_other = lax.ppermute(w_key, "rep", swap)
    w_value_other = lax.ppermute(w_value, "rep", swap)
    w_out_other = lax.ppermute(w_out, "rep", swap)
    keys = (project_rows(patches, w_key), project_rows(patches, w_key_other))
    values = (project_rows(patches, w_value), project_rows(patches, w_value_other))
    half = model_width // 2
    w_out_whole = jnp.where(
        core == 0,
        jnp.concatenate([w_out, w_out_other], axis=1),
        jnp.concatenate(
            [
                jnp.concatenate([w_out_other[half:], w_out[half:]], axis=1),
                jnp.concatenate([w_out_other[:half], w_out[:half]], axis=1),
            ],
            axis=0,
        ),
    )

    body = got.shape[1] - EXTRA
    got_row = got[:, body, 0].astype(jnp.int32)
    got_list = got[:, body + 1, 0].astype(jnp.int32)
    context_first = attend(got_row, got, 0, keys[0], values[0], None, text_count, head_size)
    back_first = lax.all_to_all(context_first, "shard", split_axis=0, concat_axis=0, tiled=True)

    got_query = jnp.where(got_list >= 0, got_list // top_count, -1)
    picked = jnp.where(got_query[:, None] == row_of((1, query_count), 1), got_row[:, None], -1)
    found = index_stats(all_queries, slab, picked.reshape(1, shard_count * query_count))
    by_owner = found[:3].reshape(3, shard_count, query_count)
    candidate = jnp.sum(by_owner[2], axis=1)
    placed = jnp.where(got_list[:, None] == row_of((1, list_length), 1), candidate[:, None], 0.0)
    stats = jnp.concatenate(
        [
            by_owner[0],
            by_owner[1],
            placed,
            jnp.zeros((shard_count, LANES - 2 * query_count - list_length), jnp.float32),
        ],
        axis=1,
    )
    context_second = attend(got_row, got, 1, keys[1], values[1], stats, text_count, head_size)
    back_second = lax.all_to_all(context_second, "shard", split_axis=0, concat_axis=0, tiled=True)

    attended, merged = finish(
        own_anchor, back_first, back_second, text_states, w_out_whole, norm_gain.reshape(1, model_width), top_count
    )
    cand_logits = merged[1, 2 * query_count : 2 * query_count + list_length].reshape(query_count, top_count)
    retrieval = cand_logits - merged[0, :query_count, None] + math.log(slab_count * shard_count)
    return (retrieval, attended)


def solution(mesh):
    in_specs = (
        P(("shard", "rep"), None),
        P("shard", None),
        P(("shard", "rep"), None),
        P("shard", None, None),
        P(("shard", "rep"), None, None),
        P(None, "rep"),
        P(None, "rep"),
        P(None, "rep"),
        P(None, "rep"),
        P(),
    )
    out_specs = (P(("shard", "rep"), None), P(("shard", "rep"), None, None, None))
    return jax.shard_map(
        on_device, mesh=mesh, in_specs=in_specs, out_specs=out_specs, check_vma=False
    )
```

```python
import functools
import math

import jax
import jax.numpy as jnp
from jax import lax
from jax.experimental import pallas as pl
from jax.experimental.pallas import tpu as pltpu
from jax.sharding import PartitionSpec as P

HEADS = 12
SCALE = 100.0
EPSILON = 1e-06
LANES = 128
EXTRA = 8
UNROLL = 8
VMEM_LIMIT = 48 * 1024 * 1024


def row_of(shape, dim):
    return lax.broadcasted_iota(jnp.int32, shape, dim)


def request_kernel(row_ids, list_ids, text, w_own, w_other, out, projected, *, top_count, query_count):
    step = pl.program_id(0)
    block = out.shape[0]
    rows = text.shape[0] // query_count

    @pl.when(step == 0)
    def _():
        at = 0
        for weight in (w_own, w_other):
            half = jnp.dot(text[...], weight[...], preferred_element_type=jnp.float32).astype(jnp.bfloat16)
            for c in range(half.shape[1] // LANES):
                for q in range(query_count):
                    projected[q, at : at + rows, :] = half[q * rows : (q + 1) * rows, c * LANES : (c + 1) * LANES]
                at += rows

    body = projected.shape[1]
    tile_row = row_of((EXTRA, LANES), 0)
    for i in range(block):
        slot = step * block + i
        listed = list_ids[slot]
        out[i, :body, :] = projected[lax.div(jnp.maximum(listed, 0), top_count)]
        code = jnp.where(tile_row == 0, row_ids[slot].astype(jnp.float32), listed.astype(jnp.float32))
        out[i, body:, :] = code.astype(jnp.bfloat16)


def make_request(row_ids, list_ids, text, w_own, w_other, top_count, query_count):
    slots = row_ids.shape[0]
    rows = text.shape[0] // query_count
    width = w_own.shape[1] + w_other.shape[1]
    body = width // LANES * rows
    block = min(16, slots)
    whole = lambda shape: pl.BlockSpec(shape, lambda i, *_: (0, 0))
    return pl.pallas_call(
        functools.partial(request_kernel, top_count=top_count, query_count=query_count),
        grid_spec=pltpu.PrefetchScalarGridSpec(
            num_scalar_prefetch=2,
            grid=(slots // block,),
            in_specs=[whole(text.shape), whole(w_own.shape), whole(w_other.shape)],
            out_specs=pl.BlockSpec((block, body + EXTRA, LANES), lambda i, *_: (i, 0, 0)),
            scratch_shapes=[pltpu.VMEM((query_count, body, LANES), jnp.bfloat16)],
        ),
        out_shape=pltpu.HBM((slots, body + EXTRA, LANES), jnp.bfloat16),
        compiler_params=pltpu.CompilerParams(vmem_limit_bytes=VMEM_LIMIT),
        cost_estimate=pl.CostEstimate(flops=2 * text.shape[0] * text.shape[1] * width, bytes_accessed=6 << 20, transcendentals=0),
        name="request",
    )(row_ids, list_ids, in_hbm(text), in_hbm(w_own), in_hbm(w_other))


def attend_kernel(got, codes, keys, values, *rest, head_size, rows):
    stats = rest[0] if len(rest) == 6 else None
    out, decoded, table, listed, sem = rest[-5:]
    slots, body = got.shape[:2]
    columns = keys.shape[2]

    lane = row_of((EXTRA, LANES), 1)
    code = jnp.zeros((EXTRA, LANES), jnp.float32)
    for slot in range(slots):
        code = jnp.where(lane == slot, codes[slot].astype(jnp.float32), code)
    decoded[...] = code.astype(jnp.int32)
    copy = pltpu.make_async_copy(decoded, table, sem)
    copy.start()
    copy.wait()

    def build(slot, count):
        listed[count] = slot
        return count + jnp.where(table[0, slot] >= 0, 1, 0)

    count = lax.fori_loop(0, slots, build, 0)
    last = listed[jnp.maximum(count - 1, 0)]
    for g in range(UNROLL):
        listed[count + g] = last

    spans = []
    at = 0
    while at < columns:
        width = min(2 * LANES, columns - at)
        lane_head = row_of((rows, width), 1) // head_size
        spans.append((at, width, [jnp.where(lane_head == h, 1.0, 0.0) for h in range(width // head_size)]))
        at += width

    def group(index, carry):
        chosen = [listed[index * UNROLL + g] for g in range(UNROLL)]
        images = [table[0, slot] for slot in chosen]
        work = [(g, span) for g in range(UNROLL) for span in spans]
        scores = []
        for g, (at, width, masks) in work:
            pieces = [
                got[chosen[g], (at // LANES + c) * rows : (at // LANES + c + 1) * rows, :] for c in range(width // LANES)
            ]
            query = pieces[0] if len(pieces) == 1 else jnp.concatenate(pieces, axis=1)
            spread = jnp.concatenate([query * mask.astype(query.dtype) for mask in masks], axis=0)
            scores.append(
                lax.dot_general(
                    spread,
                    keys[images[g], :, at : at + width],
                    (((1,), (1,)), ((), ())),
                    preferred_element_type=jnp.float32,
                )
            )
        scores = [score * head_size ** (-0.5) for score in scores]
        highest = [jnp.max(score, axis=-1, keepdims=True) for score in scores]
        powers = [jnp.exp(score - top) for score, top in zip(scores, highest)]
        totals = [jnp.sum(power, axis=-1, keepdims=True) for power in powers]
        weights = [(power / total).astype(jnp.bfloat16) for power, total in zip(powers, totals)]
        mixed = [
            jnp.dot(weight, values[images[g], :, at : at + width], preferred_element_type=jnp.float32)
            for weight, (g, (at, width, _)) in zip(weights, work)
        ]
        for mix, (g, (at, width, masks)) in zip(mixed, work):
            context = mix[:rows] * masks[0]
            for h in range(1, len(masks)):
                context = context + mix[h * rows : (h + 1) * rows] * masks[h]
            context = context.astype(jnp.bfloat16)
            for c in range(width // LANES):
                out[chosen[g], (at // LANES + c) * rows : (at // LANES + c + 1) * rows, :] = context[
                    :, c * LANES : (c + 1) * LANES
                ]
        return carry

    lax.fori_loop(0, lax.div(count + UNROLL - 1, UNROLL), group, 0)

    if stats is not None:
        tile_row = row_of((EXTRA, LANES), 0)
        for slot in range(slots):
            exact = jnp.broadcast_to(stats[slot : slot + 1, :], (EXTRA, LANES))
            high = exact.astype(jnp.bfloat16).astype(jnp.float32)
            left = exact - high
            middle = left.astype(jnp.bfloat16).astype(jnp.float32)
            low = left - middle
            out[slot, body:, :] = jnp.where(
                tile_row == 0, high, jnp.where(tile_row == 1, middle, jnp.where(tile_row == 2, low, 0.0))
            ).astype(jnp.bfloat16)


def in_hbm(array):
    return pltpu.with_memory_space_constraint(array, pltpu.HBM)


def attend(got, part, keys, values, stats, rows, head_size):
    slots, sent = got.shape[:2]
    body = keys.shape[2] // LANES * rows
    height = body + (0 if stats is None else EXTRA)
    last = (sent - EXTRA) // EXTRA
    operands = [in_hbm(got), in_hbm(got), in_hbm(keys), in_hbm(values)] + ([] if stats is None else [stats])
    in_specs = [
        pl.BlockSpec((slots, body, LANES), lambda i: (0, part, 0)),
        pl.BlockSpec((slots, EXTRA, LANES), lambda i: (0, last, 0)),
        pl.BlockSpec(keys.shape, lambda i: (0, 0, 0)),
        pl.BlockSpec(values.shape, lambda i: (0, 0, 0)),
    ] + ([] if stats is None else [pl.BlockSpec(stats.shape, lambda i: (0, 0))])
    return pl.pallas_call(
        functools.partial(attend_kernel, head_size=head_size, rows=rows),
        grid=(1,),
        in_specs=in_specs,
        out_specs=[
            pl.BlockSpec((slots, height, LANES), lambda i: (0, 0, 0)),
            pl.BlockSpec((EXTRA, LANES), lambda i: (0, 0)),
        ],
        scratch_shapes=[
            pltpu.SMEM((EXTRA, LANES), jnp.int32),
            pltpu.SMEM((slots + UNROLL,), jnp.int32),
            pltpu.SemaphoreType.DMA,
        ],
        out_shape=[
            pltpu.HBM((slots, height, LANES), jnp.bfloat16),
            jax.ShapeDtypeStruct((EXTRA, LANES), jnp.int32),
        ],
        compiler_params=pltpu.CompilerParams(vmem_limit_bytes=VMEM_LIMIT),
        cost_estimate=pl.CostEstimate(flops=4 << 30, bytes_accessed=6 << 20, transcendentals=1 << 20),
        name="attend",
    )(*operands)


def logits_kernel(queries, slab, picked, out, logits):
    query = queries[...].astype(jnp.bfloat16)
    tile = min(256, slab.shape[0])
    peak = None
    for t in range(slab.shape[0] // tile):
        part = SCALE * lax.dot_general(
            slab[t * tile : (t + 1) * tile, :], query, (((1,), (1,)), ((), ())), preferred_element_type=jnp.float32
        )
        logits[t * tile : (t + 1) * tile, :] = part
        top = jnp.max(part, axis=0, keepdims=True)
        peak = top if peak is None else jnp.maximum(peak, top)
    total = jnp.zeros_like(peak)
    for t in range(slab.shape[0] // tile):
        total = total + jnp.sum(jnp.exp(logits[t * tile : (t + 1) * tile, :] - peak), axis=0, keepdims=True)
    store = min(tile, slab.shape[0])
    chosen = row_of((store, queries.shape[0]), 0) == picked[...]
    candidate = jnp.sum(jnp.where(chosen, logits[:store, :], 0.0), axis=0, keepdims=True)
    tile_row = row_of(out.shape, 0)
    out[...] = jnp.where(tile_row == 0, peak, jnp.where(tile_row == 1, total, candidate))


def index_stats(queries, slab, picked):
    count = queries.shape[0]
    return pl.pallas_call(
        logits_kernel,
        out_shape=jax.ShapeDtypeStruct((8, count), jnp.float32),
        scratch_shapes=[pltpu.VMEM((slab.shape[0], count), jnp.float32)],
        compiler_params=pltpu.CompilerParams(vmem_limit_bytes=VMEM_LIMIT),
        cost_estimate=pl.CostEstimate(
            flops=2 * count * slab.shape[0] * slab.shape[1], bytes_accessed=5 << 20, transcendentals=count * slab.shape[0]
        ),
        name="index_stats",
    )(queries, slab, picked)


def finish_kernel(shards, first, second, text, w_out, gain, out, merged, gathered, *, top_count, query_count):
    step = pl.program_id(0)
    rows = text.shape[1]
    half = first.shape[1]

    @pl.when(step == 0)
    def _():
        sent = second[:, half:, :].astype(jnp.float32)
        exact = jnp.sum(jnp.where(row_of(sent.shape, 1) < 3, sent, 0.0), axis=1)
        peak = jnp.max(exact, axis=0, keepdims=True)
        scaled = jnp.exp(exact - peak) * pltpu.roll(exact, LANES - query_count, 1)
        lane = row_of(peak.shape, 1)
        total = jnp.sum(scaled, axis=0, keepdims=True)
        normalizer = peak + jnp.log(jnp.where(lane < query_count, total, 1.0))
        candidate = jnp.sum(exact, axis=0, keepdims=True)
        tile_row = row_of(merged.shape, 0)
        merged[...] = jnp.where(tile_row == 0, normalizer, candidate)

    for k in range(top_count):
        shard = shards[step * top_count + k]
        for j in range(half // rows):
            gathered[k * rows : (k + 1) * rows, j * LANES : (j + 1) * LANES] = first[shard, j * rows : (j + 1) * rows, :]
            column = half // rows + j
            gathered[k * rows : (k + 1) * rows, column * LANES : (column + 1) * LANES] = second[
                shard, j * rows : (j + 1) * rows, :
            ]
    mixed = jnp.dot(gathered[...], w_out[...], preferred_element_type=jnp.float32)
    width = mixed.shape[1]
    summed = mixed.reshape(top_count, rows, width) + text[...].astype(jnp.float32)
    mean = jnp.mean(summed, axis=-1, keepdims=True)
    centred = summed - mean
    variance = jnp.mean(centred * centred, axis=-1, keepdims=True)
    normed = centred * lax.rsqrt(variance + EPSILON) * gain[...].reshape(1, 1, width)
    out[...] = normed.astype(jnp.bfloat16).reshape(out.shape)


def finish(shards, first, second, text, w_out, gain, top_count):
    query_count, rows, width = text.shape
    full = lambda a: pl.BlockSpec(a.shape, lambda i, *_: (0,) * a.ndim)
    return pl.pallas_call(
        functools.partial(finish_kernel, top_count=top_count, query_count=query_count),
        grid_spec=pltpu.PrefetchScalarGridSpec(
            num_scalar_prefetch=1,
            grid=(query_count,),
            in_specs=[
                full(first),
                full(second),
                pl.BlockSpec((1, rows, width), lambda i, *_: (i, 0, 0)),
                full(w_out),
                full(gain),
            ],
            out_specs=[
                pl.BlockSpec((1, top_count, rows, width), lambda i, *_: (i, 0, 0, 0)),
                pl.BlockSpec((8, LANES), lambda i, *_: (0, 0)),
            ],
            scratch_shapes=[pltpu.VMEM((top_count * rows, width), jnp.bfloat16)],
        ),
        out_shape=[
            jax.ShapeDtypeStruct((query_count, top_count, rows, width), jnp.bfloat16),
            jax.ShapeDtypeStruct((8, LANES), jnp.float32),
        ],
        compiler_params=pltpu.CompilerParams(vmem_limit_bytes=VMEM_LIMIT),
        cost_estimate=pl.CostEstimate(
            flops=2 * query_count * top_count * rows * width * width, bytes_accessed=7 << 20, transcendentals=0
        ),
        name="finish",
    )(shards, in_hbm(first), in_hbm(second), text, in_hbm(w_out), gain)


def project_rows(rows_in, weight):
    return jnp.einsum("spc,cd->spd", rows_in, weight, preferred_element_type=jnp.float32).astype(jnp.bfloat16)


def on_device(queries, slab, cand_ids, patches, text_states, w_query, w_key, w_value, w_out, norm_gain):
    shard_count = lax.axis_size("shard")
    core = lax.axis_index("rep")
    query_count, embed_width = queries.shape
    slab_count = slab.shape[0]
    top_count = cand_ids.shape[1]
    list_length = query_count * top_count
    text_count, model_width = text_states.shape[1:]
    head_size = model_width // HEADS
    swap = [(0, 1), (1, 0)]
    w_query_other = lax.ppermute(w_query, "rep", swap)

    own_list = cand_ids.reshape(list_length)
    own_anchor = own_list // slab_count
    here = own_anchor[None, :] == row_of((shard_count, 1), 0)
    row_ids = jnp.sum(jnp.where(here, own_list[None, :] % slab_count + 1, 0), axis=1) - 1
    list_ids = jnp.sum(jnp.where(here, row_of((1, list_length), 1) + 1, 0), axis=1) - 1

    request = make_request(
        row_ids,
        list_ids,
        text_states.reshape(query_count * text_count, model_width),
        w_query,
        w_query_other,
        top_count,
        query_count,
    )
    got = lax.all_to_all(request, "shard", split_axis=0, concat_axis=0, tiled=True)
    all_queries = lax.all_gather(queries.astype(jnp.float32), "shard", axis=0, tiled=True)

    w_key_other = lax.ppermute(w_key, "rep", swap)
    w_value_other = lax.ppermute(w_value, "rep", swap)
    w_out_other = lax.ppermute(w_out, "rep", swap)
    keys = (project_rows(patches, w_key), project_rows(patches, w_key_other))
    values = (project_rows(patches, w_value), project_rows(patches, w_value_other))
    half = model_width // 2
    w_out_whole = jnp.where(
        core == 0,
        jnp.concatenate([w_out, w_out_other], axis=1),
        jnp.concatenate(
            [
                jnp.concatenate([w_out_other[half:], w_out[half:]], axis=1),
                jnp.concatenate([w_out_other[:half], w_out[:half]], axis=1),
            ],
            axis=0,
        ),
    )

    context_first, decoded = attend(got, 0, keys[0], values[0], None, text_count, head_size)
    got_row, got_list = decoded[0, :shard_count], decoded[1, :shard_count]
    back_first = lax.all_to_all(context_first, "shard", split_axis=0, concat_axis=0, tiled=True)

    got_query = jnp.where(got_list >= 0, got_list // top_count, -1)
    picked = jnp.where(got_query[:, None] == row_of((1, query_count), 1), got_row[:, None], -1)
    found = index_stats(all_queries, slab, picked.reshape(1, shard_count * query_count))
    by_owner = found[:3].reshape(3, shard_count, query_count)
    candidate = jnp.sum(by_owner[2], axis=1)
    placed = jnp.where(got_list[:, None] == row_of((1, list_length), 1), candidate[:, None], 0.0)
    stats = jnp.concatenate(
        [
            by_owner[0],
            by_owner[1],
            placed,
            jnp.zeros((shard_count, LANES - 2 * query_count - list_length), jnp.float32),
        ],
        axis=1,
    )
    context_second, _ = attend(got, 1, keys[1], values[1], stats, text_count, head_size)
    back_second = lax.all_to_all(context_second, "shard", split_axis=0, concat_axis=0, tiled=True)

    attended, merged = finish(
        own_anchor, back_first, back_second, text_states, w_out_whole, norm_gain.reshape(1, model_width), top_count
    )
    cand_logits = merged[1, 2 * query_count : 2 * query_count + list_length].reshape(query_count, top_count)
    retrieval = cand_logits - merged[0, :query_count, None] + math.log(slab_count * shard_count)
    return (retrieval, attended)


def solution(mesh):
    in_specs = (
        P(("shard", "rep"), None),
        P("shard", None),
        P(("shard", "rep"), None),
        P("shard", None, None),
        P(("shard", "rep"), None, None),
        P(None, "rep"),
        P(None, "rep"),
        P(None, "rep"),
        P(None, "rep"),
        P(),
    )
    out_specs = (P(("shard", "rep"), None), P(("shard", "rep"), None, None, None))
    return jax.shard_map(
        on_device, mesh=mesh, in_specs=in_specs, out_specs=out_specs, check_vma=False
    )
```

```python
import functools
import math

import jax
import jax.numpy as jnp
from jax import lax
from jax.experimental import pallas as pl
from jax.experimental.pallas import tpu as pltpu
from jax.sharding import PartitionSpec as P

HEADS = 12
SCALE = 100.0
EPSILON = 1e-06
LANES = 128
EXTRA = 8
UNROLL = 8
GRIDS = {128: (4, 8, 4), 8: (2, 2, 2)}
VMEM_LIMIT = 48 * 1024 * 1024


def row_of(shape, dim):
    return lax.broadcasted_iota(jnp.int32, shape, dim)


def in_hbm(array):
    return pltpu.with_memory_space_constraint(array, pltpu.HBM)


def project_kernel(text, queries, codes, w_own, w_other, out):
    rows = text.shape[0]
    half = w_own.shape[1]
    out[:rows, :half] = jnp.dot(text[...], w_own[...], preferred_element_type=jnp.float32).astype(jnp.bfloat16)
    out[:rows, half:] = jnp.dot(text[...], w_other[...], preferred_element_type=jnp.float32).astype(jnp.bfloat16)
    count, width = queries.shape
    pieces = [queries[...].astype(jnp.float32)]
    if count < EXTRA:
        pieces.append(jnp.zeros((EXTRA - count, width), jnp.float32))
    code = [jnp.broadcast_to(codes[i : i + 1, :].astype(jnp.float32), (EXTRA, LANES)) for i in range(2)]
    code.append(jnp.zeros((EXTRA, width - 2 * LANES), jnp.float32))
    pieces.append(jnp.concatenate(code, axis=1))
    out[rows:, :] = jnp.concatenate(pieces, axis=0).astype(jnp.bfloat16)


def project(text, queries, codes, w_own, w_other):
    width = w_own.shape[1] + w_other.shape[1]
    return pl.pallas_call(
        project_kernel,
        out_shape=jax.ShapeDtypeStruct((text.shape[0] + 2 * EXTRA, width), jnp.bfloat16),
        compiler_params=pltpu.CompilerParams(vmem_limit_bytes=VMEM_LIMIT),
        cost_estimate=pl.CostEstimate(
            flops=2 * text.shape[0] * text.shape[1] * width, bytes_accessed=2 << 20, transcendentals=0
        ),
        name="project",
    )(text, queries, codes, w_own, w_other)


def to_scalars(vectors, decoded, table, sem):
    decoded[...] = vectors
    copy = pltpu.make_async_copy(decoded, table, sem)
    copy.start()
    copy.wait()


def request_kernel(place, owners, out, decoded, table, shared, sem, *, grid_x, rows, query_count, top_count):
    step = pl.program_id(0)
    depth, height = owners.shape[:2]
    texts = height - 2 * EXTRA
    slot_rows = depth * rows
    shared_rows = shared.shape[0]
    tile_row = row_of((EXTRA, LANES), 0)

    @pl.when(step == 0)
    def _():
        found = [jnp.zeros((EXTRA, LANES), jnp.float32) for _ in range(2)]
        for z in range(depth):
            code = owners[z, texts + EXTRA :, :].astype(jnp.float32)
            found = [jnp.where(tile_row == z, code[:, i * LANES : (i + 1) * LANES], found[i]) for i in range(2)]
        to_scalars(jnp.concatenate(found, axis=0).astype(jnp.int32), decoded, table, sem)
        picked = [owners[z, texts : texts + EXTRA, :].astype(jnp.float32)[:query_count] for z in range(depth)]
        shared[...] = jnp.concatenate(picked, axis=0).astype(jnp.bfloat16)

    shard = (lax.div(step, grid_x) * depth + place[0]) * grid_x + lax.rem(step, grid_x)
    lane = row_of((EXTRA, LANES), 1)
    code = jnp.full((EXTRA, LANES), -1.0, jnp.float32)
    for z in range(depth):
        image, listed = table[z, shard], table[EXTRA + z, shard]
        first = lax.div(jnp.maximum(listed, 0), top_count) * rows
        out[0, z * rows : (z + 1) * rows, :] = owners[z, pl.ds(pl.multiple_of(first, rows), rows), :]
        code = jnp.where(lane == z, image.astype(jnp.float32), code)
        code = jnp.where(lane == EXTRA + z, listed.astype(jnp.float32), code)
    out[0, slot_rows : slot_rows + shared_rows, :] = shared[...]
    out[0, slot_rows + shared_rows :, :LANES] = code.astype(jnp.bfloat16)


def make_request(place, owners, grid_y, grid_x, rows, query_count, top_count):
    depth, height, width = owners.shape
    shared_rows = depth * query_count
    total = depth * rows + shared_rows + EXTRA
    return pl.pallas_call(
        functools.partial(
            request_kernel, grid_x=grid_x, rows=rows, query_count=query_count, top_count=top_count
        ),
        grid_spec=pltpu.PrefetchScalarGridSpec(
            num_scalar_prefetch=1,
            grid=(grid_y * grid_x,),
            in_specs=[pl.BlockSpec(owners.shape, lambda i, *_: (0, 0, 0))],
            out_specs=pl.BlockSpec((1, total, width), lambda i, *_: (i, 0, 0)),
            scratch_shapes=[
                pltpu.VMEM((2 * EXTRA, LANES), jnp.int32),
                pltpu.SMEM((2 * EXTRA, LANES), jnp.int32),
                pltpu.VMEM((shared_rows, width), jnp.bfloat16),
                pltpu.SemaphoreType.DMA,
            ],
        ),
        out_shape=pltpu.HBM((grid_y * grid_x, total, width), jnp.bfloat16),
        compiler_params=pltpu.CompilerParams(vmem_limit_bytes=VMEM_LIMIT),
        cost_estimate=pl.CostEstimate(flops=1 << 20, bytes_accessed=6 << 20, transcendentals=0),
        name="request",
    )(place, in_hbm(owners))


def index_stats(query, slab, picked, logits):
    count = query.shape[0]
    tile = min(256, slab.shape[0])
    peak = None
    for t in range(slab.shape[0] // tile):
        part = SCALE * lax.dot_general(
            slab[t * tile : (t + 1) * tile, :], query, (((1,), (1,)), ((), ())), preferred_element_type=jnp.float32
        )
        logits[t * tile : (t + 1) * tile, :] = part
        top = jnp.max(part, axis=0, keepdims=True)
        peak = top if peak is None else jnp.maximum(peak, top)
    total = jnp.zeros_like(peak)
    for t in range(slab.shape[0] // tile):
        total = total + jnp.sum(jnp.exp(logits[t * tile : (t + 1) * tile, :] - peak), axis=0, keepdims=True)
    chosen = row_of((tile, count), 0) == picked
    candidate = jnp.sum(jnp.where(chosen, logits[:tile, :], 0.0), axis=0, keepdims=True)
    return peak, total, candidate


def split_rows(exact):
    tile_row = row_of((EXTRA, LANES), 0)
    exact = jnp.broadcast_to(exact, (EXTRA, LANES))
    high = exact.astype(jnp.bfloat16).astype(jnp.float32)
    left = exact - high
    middle = left.astype(jnp.bfloat16).astype(jnp.float32)
    parts = jnp.where(tile_row == 0, high, jnp.where(tile_row == 1, middle, left - middle))
    return jnp.where(tile_row < 3, parts, 0.0)


def serve_kernel(
    got_hbm, slab_hbm, keys_hbm, values_hbm, out,
    got, slab, keys, values, logits, decoded, table, listed, sems, *, grid_x, depth, rows, query_count, top_count, head_size
):
    copies = [
        pltpu.make_async_copy(source, target, sems.at[i])
        for i, (source, target) in enumerate(
            [(got_hbm, got), (slab_hbm, slab), (keys_hbm, keys), (values_hbm, values)]
        )
    ]
    for copy in copies:
        copy.start()
    sources, height = got.shape[:2]
    slots = sources * depth
    columns = keys.shape[2]
    slot_rows = depth * rows
    shared_rows = depth * query_count
    body = columns // LANES * rows
    per_chunk = LANES // query_count
    lane = row_of((EXTRA, LANES), 1)
    tile_row = row_of((EXTRA, LANES), 0)

    copies[0].wait()
    found = [jnp.zeros((EXTRA, LANES), jnp.float32) for _ in range(-(-sources // EXTRA))]
    for source in range(sources):
        code = got[source, slot_rows + shared_rows :, :LANES].astype(jnp.float32)
        found[source // EXTRA] = jnp.where(tile_row == source % EXTRA, code, found[source // EXTRA])
    found = found[0] if len(found) == 1 else jnp.concatenate(found, axis=0)
    to_scalars(found.astype(jnp.int32), decoded, table, sems.at[4])

    count = 0
    chunks = [jnp.full((EXTRA, LANES), -1, jnp.int32) for _ in range(-(-slots // per_chunk))]
    for slot in range(slots):
        image, entry = table[slot // depth, slot % depth], table[slot // depth, EXTRA + slot % depth]
        query = lax.div(jnp.maximum(entry, 0), top_count)
        at = slot % per_chunk * query_count + query
        chunks[slot // per_chunk] = jnp.where(lane == at, image, chunks[slot // per_chunk])
        listed[count] = slot
        count = count + jnp.where(image >= 0, 1, 0)
    last = listed[jnp.maximum(count - 1, 0)]
    for g in range(UNROLL):
        listed[count + g] = last

    queries = jnp.concatenate([got[source, slot_rows : slot_rows + shared_rows, :] for source in range(sources)], axis=0)
    missing = len(chunks) * LANES - queries.shape[0]
    if missing:
        queries = jnp.concatenate([queries, jnp.zeros((missing, queries.shape[1]), queries.dtype)], axis=0)
    copies[1].wait()
    stats = index_stats(queries, slab, jnp.concatenate([chunk[:1] for chunk in chunks], axis=1), logits)
    for c in range(len(chunks)):
        tiles = [split_rows(stat[:, c * LANES : (c + 1) * LANES]) for stat in stats]
        tiles = [tiles[0], pltpu.roll(tiles[1], query_count, 1), pltpu.roll(tiles[2], 2 * query_count, 1)]
        for slot in range(c * per_chunk, min((c + 1) * per_chunk, slots)):
            source, z = slot // depth, slot % depth
            at = slot % per_chunk
            owner = (source // grid_x * depth + z) * grid_x + source % grid_x
            place = lane // query_count
            tile = jnp.where(place == at, tiles[0], jnp.where(place == (at + 1) % per_chunk, tiles[1], tiles[2]))
            out[owner, body:, :] = tile.astype(jnp.bfloat16)

    copies[2].wait()
    copies[3].wait()
    spans = []
    at = 0
    while at < columns:
        width = min(2 * LANES, columns - at)
        lane_head = row_of((rows, width), 1) // head_size
        spans.append((at, width, [jnp.where(lane_head == h, 1.0, 0.0) for h in range(width // head_size)]))
        at += width

    def group(index, carry):
        chosen = [listed[index * UNROLL + g] for g in range(UNROLL)]
        places = [(lax.div(slot, depth), lax.rem(slot, depth)) for slot in chosen]
        images = [table[source, z] for source, z in places]
        owners = [
            (lax.div(source, grid_x) * depth + z) * grid_x + lax.rem(source, grid_x) for source, z in places
        ]
        work = [(g, span) for g in range(UNROLL) for span in spans]
        scores = []
        for g, (at, width, masks) in work:
            source, z = places[g]
            query = got[source, pl.ds(pl.multiple_of(z * rows, rows), rows), at : at + width]
            spread = jnp.concatenate([query * mask.astype(query.dtype) for mask in masks], axis=0)
            scores.append(
                lax.dot_general(
                    spread,
                    keys[images[g], :, at : at + width],
                    (((1,), (1,)), ((), ())),
                    preferred_element_type=jnp.float32,
                )
            )
        scores = [score * head_size ** (-0.5) for score in scores]
        highest = [jnp.max(score, axis=-1, keepdims=True) for score in scores]
        powers = [jnp.exp(score - top) for score, top in zip(scores, highest)]
        totals = [jnp.sum(power, axis=-1, keepdims=True) for power in powers]
        weights = [(power / total).astype(jnp.bfloat16) for power, total in zip(powers, totals)]
        mixed = [
            jnp.dot(weight, values[images[g], :, at : at + width], preferred_element_type=jnp.float32)
            for weight, (g, (at, width, _)) in zip(weights, work)
        ]
        for mix, (g, (at, width, masks)) in zip(mixed, work):
            context = mix[:rows] * masks[0]
            for h in range(1, len(masks)):
                context = context + mix[h * rows : (h + 1) * rows] * masks[h]
            context = context.astype(jnp.bfloat16)
            for c in range(width // LANES):
                out[owners[g], (at // LANES + c) * rows : (at // LANES + c + 1) * rows, :] = context[
                    :, c * LANES : (c + 1) * LANES
                ]
        return carry

    lax.fori_loop(0, lax.div(count + UNROLL - 1, UNROLL), group, 0)


def serve(got, slab, keys, values, grid_x, depth, rows, query_count, top_count, head_size):
    sources = got.shape[0]
    slots = sources * depth
    body = keys.shape[2] // LANES * rows
    lanes = -(-slots * query_count // LANES) * LANES
    operands = [got, slab, keys, values]
    codes = (-(-sources // EXTRA) * EXTRA, LANES)
    return pl.pallas_call(
        functools.partial(
            serve_kernel,
            grid_x=grid_x,
            depth=depth,
            rows=rows,
            query_count=query_count,
            top_count=top_count,
            head_size=head_size,
        ),
        grid=(1,),
        in_specs=[pl.BlockSpec(memory_space=pltpu.HBM)] * 4,
        out_specs=pl.BlockSpec((slots, body + EXTRA, LANES), lambda i: (0, 0, 0)),
        scratch_shapes=[pltpu.VMEM(a.shape, a.dtype) for a in operands]
        + [
            pltpu.VMEM((slab.shape[0], lanes), jnp.float32),
            pltpu.VMEM(codes, jnp.int32),
            pltpu.SMEM(codes, jnp.int32),
            pltpu.SMEM((slots + UNROLL,), jnp.int32),
            pltpu.SemaphoreType.DMA((5,)),
        ],
        out_shape=pltpu.HBM((slots, body + EXTRA, LANES), jnp.bfloat16),
        compiler_params=pltpu.CompilerParams(vmem_limit_bytes=VMEM_LIMIT),
        cost_estimate=pl.CostEstimate(flops=8 << 30, bytes_accessed=14 << 20, transcendentals=2 << 20),
        name="serve",
    )(*[in_hbm(a) for a in operands])


def finish_kernel(
    shards, place, back, text, w_out, gain, found, out, exact, normalizers, gathered, *, top_count, query_count, shift
):
    step = pl.program_id(0)
    rows = text.shape[1]
    body = back.shape[1] - EXTRA

    @pl.when(step == 0)
    def _():
        sent = back[:, body:, :].astype(jnp.float32)
        joined = jnp.sum(jnp.where(row_of(sent.shape, 1) < 3, sent, 0.0), axis=1)
        joined = pltpu.roll(joined, lax.rem(LANES - place[0] * query_count, LANES), 1)
        exact[...] = joined
        peak = jnp.max(joined, axis=0, keepdims=True)
        scaled = jnp.exp(joined - peak) * pltpu.roll(joined, LANES - query_count, 1)
        total = jnp.sum(scaled, axis=0, keepdims=True)
        total = jnp.where(row_of(total.shape, 1) < query_count, total, 1.0)
        normalizers[...] = jnp.broadcast_to(peak + jnp.log(total), normalizers.shape)

    picked = jnp.concatenate([exact[pl.ds(shards[step * top_count + k], 1), :] for k in range(top_count)], axis=0)
    lane = row_of(picked.shape, 1)
    candidate = jnp.sum(jnp.where(lane == 2 * query_count + step, picked, 0.0), axis=1, keepdims=True)
    normalizer = jnp.sum(jnp.where(lane[:1] == step, normalizers[:1, :], 0.0), axis=1, keepdims=True)
    result = candidate - normalizer + shift
    result = jnp.sum(jnp.where(lane == row_of(picked.shape, 0), result, 0.0), axis=0, keepdims=True)
    found[pl.ds(step, 1), :] = result[:, :top_count]

    for k in range(top_count):
        shard = shards[step * top_count + k]
        for j in range(body // rows):
            gathered[k * rows : (k + 1) * rows, j * LANES : (j + 1) * LANES] = back[shard, j * rows : (j + 1) * rows, :]
    mixed = jnp.dot(gathered[...], w_out[...], preferred_element_type=jnp.float32)
    width = mixed.shape[1]
    summed = mixed.reshape(top_count, rows, width) + text[...].astype(jnp.float32)
    mean = jnp.mean(summed, axis=-1, keepdims=True)
    centred = summed - mean
    variance = jnp.mean(centred * centred, axis=-1, keepdims=True)
    normed = centred * lax.rsqrt(variance + EPSILON) * gain[...].reshape(1, 1, width)
    out[...] = normed.astype(jnp.bfloat16).reshape(out.shape)


def finish(shards, place, back, text, w_out, gain, top_count, shift):
    query_count, rows, width = text.shape
    full = lambda a: pl.BlockSpec(a.shape, lambda i, *_: (0,) * a.ndim)
    return pl.pallas_call(
        functools.partial(finish_kernel, top_count=top_count, query_count=query_count, shift=shift),
        grid_spec=pltpu.PrefetchScalarGridSpec(
            num_scalar_prefetch=2,
            grid=(query_count,),
            in_specs=[
                full(back),
                pl.BlockSpec((1, rows, width), lambda i, *_: (i, 0, 0)),
                full(w_out),
                full(gain),
            ],
            out_specs=[
                pl.BlockSpec((query_count, top_count), lambda i, *_: (0, 0)),
                pl.BlockSpec((1, top_count, rows, width), lambda i, *_: (i, 0, 0, 0)),
            ],
            scratch_shapes=[
                pltpu.VMEM((back.shape[0], LANES), jnp.float32),
                pltpu.VMEM((EXTRA, LANES), jnp.float32),
                pltpu.VMEM((top_count * rows, width), jnp.bfloat16),
            ],
        ),
        out_shape=[
            jax.ShapeDtypeStruct((query_count, top_count), jnp.float32),
            jax.ShapeDtypeStruct((query_count, top_count, rows, width), jnp.bfloat16),
        ],
        compiler_params=pltpu.CompilerParams(vmem_limit_bytes=VMEM_LIMIT),
        cost_estimate=pl.CostEstimate(
            flops=2 * query_count * top_count * rows * width * width, bytes_accessed=7 << 20, transcendentals=0
        ),
        name="finish",
    )(shards, place, in_hbm(back), text, in_hbm(w_out), gain)


def project_rows(rows_in, weight):
    return jnp.einsum("spc,cd->spd", rows_in, weight, preferred_element_type=jnp.float32).astype(jnp.bfloat16)


def on_device(queries, slab, cand_ids, patches, text_states, w_query, w_key, w_value, w_out, norm_gain):
    shard_count = lax.axis_size("shard")
    shard_here = lax.axis_index("shard")
    core = lax.axis_index("rep")
    grid_y, depth, grid_x = GRIDS[shard_count]
    query_count = queries.shape[0]
    slab_count = slab.shape[0]
    top_count = cand_ids.shape[1]
    list_length = query_count * top_count
    text_count, model_width = text_states.shape[1:]
    head_size = model_width // HEADS
    here_x, here_z, here_y = shard_here % grid_x, shard_here // grid_x % depth, shard_here // (grid_x * depth)
    columns = [
        [(y * depth + z) * grid_x + x for z in range(depth)] for y in range(grid_y) for x in range(grid_x)
    ]
    planes = [
        [(y * depth + z) * grid_x + x for y in range(grid_y) for x in range(grid_x)] for z in range(depth)
    ]
    swap = [(0, 1), (1, 0)]
    w_query_other = lax.ppermute(w_query, "rep", swap)

    own_list = cand_ids.reshape(list_length)
    own_anchor = own_list // slab_count
    here = own_anchor[None, :] == row_of((LANES, 1), 0)
    row_ids = jnp.sum(jnp.where(here, own_list[None, :] % slab_count + 1, 0), axis=1) - 1
    list_ids = jnp.sum(jnp.where(here, row_of((1, list_length), 1) + 1, 0), axis=1) - 1

    sent = project(
        text_states.reshape(query_count * text_count, model_width),
        queries,
        jnp.stack([row_ids, list_ids]),
        w_query,
        w_query_other,
    )
    owners = lax.all_gather(sent, "shard", axis=0, tiled=True, axis_index_groups=columns)
    request = make_request(
        here_z.reshape(1),
        owners.reshape(depth, sent.shape[0], model_width),
        grid_y,
        grid_x,
        text_count,
        query_count,
        top_count,
    )
    got = lax.all_to_all(request, "shard", split_axis=0, concat_axis=0, tiled=True, axis_index_groups=planes)

    keys = project_rows(patches, jnp.concatenate([w_key, lax.ppermute(w_key, "rep", swap)], axis=1))
    values = project_rows(patches, jnp.concatenate([w_value, lax.ppermute(w_value, "rep", swap)], axis=1))
    w_out_other = lax.ppermute(w_out, "rep", swap)
    half = model_width // 2
    w_out_whole = jnp.where(
        core == 0,
        jnp.concatenate([w_out, w_out_other], axis=1),
        jnp.concatenate(
            [
                jnp.concatenate([w_out_other[half:], w_out[half:]], axis=1),
                jnp.concatenate([w_out_other[:half], w_out[:half]], axis=1),
            ],
            axis=0,
        ),
    )

    context = serve(got, slab, keys, values, grid_x, depth, text_count, query_count, top_count, head_size)
    back = lax.all_to_all(context, "shard", split_axis=0, concat_axis=0, tiled=True)

    place = ((here_y * grid_x + here_x) * depth + here_z) % (LANES // query_count)
    retrieval, attended = finish(
        own_anchor,
        place.reshape(1),
        back,
        text_states,
        w_out_whole,
        norm_gain.reshape(1, model_width),
        top_count,
        math.log(slab_count * shard_count),
    )
    return (retrieval, attended)


def solution(mesh):
    in_specs = (
        P(("shard", "rep"), None),
        P("shard", None),
        P(("shard", "rep"), None),
        P("shard", None, None),
        P(("shard", "rep"), None, None),
        P(None, "rep"),
        P(None, "rep"),
        P(None, "rep"),
        P(None, "rep"),
        P(),
    )
    out_specs = (P(("shard", "rep"), None), P(("shard", "rep"), None, None, None))
    return jax.shard_map(
        on_device, mesh=mesh, in_specs=in_specs, out_specs=out_specs, check_vma=False
    )
```

```python
import functools
import math

import jax
import jax.numpy as jnp
from jax import lax
from jax.experimental import pallas as pl
from jax.experimental.pallas import tpu as pltpu
from jax.sharding import PartitionSpec as P

HEADS = 12
SCALE = 100.0
EPSILON = 1e-06
LANES = 128
EXTRA = 8
UNROLL = 16
GRIDS = {128: (4, 8, 4), 8: (2, 2, 2)}
VMEM_LIMIT = 48 * 1024 * 1024


def row_of(shape, dim):
    return lax.broadcasted_iota(jnp.int32, shape, dim)


def in_hbm(array):
    return pltpu.with_memory_space_constraint(array, pltpu.HBM)


def project_kernel(ids, text, queries, w_own, w_other, out, *, slab_count):
    rows = text.shape[0]
    half = w_own.shape[1]
    count, width = queries.shape
    lane = row_of((EXTRA, LANES), 1)
    image = jnp.full((EXTRA, LANES), -1, jnp.int32)
    listed = image
    for entry in range(ids.shape[0] * ids.shape[1]):
        row = ids[entry // ids.shape[1], entry % ids.shape[1]]
        here = lane == lax.div(row, slab_count)
        image = jnp.where(here, lax.rem(row, slab_count), image)
        listed = jnp.where(here, entry, listed)
    pieces = [queries[...].astype(jnp.float32)]
    if count < EXTRA:
        pieces.append(jnp.zeros((EXTRA - count, width), jnp.float32))
    code = [image.astype(jnp.float32), listed.astype(jnp.float32)]
    code.append(jnp.zeros((EXTRA, width - 2 * LANES), jnp.float32))
    pieces.append(jnp.concatenate(code, axis=1))
    out[rows:, :] = jnp.concatenate(pieces, axis=0).astype(jnp.bfloat16)
    out[:rows, :half] = jnp.dot(text[...], w_own[...], preferred_element_type=jnp.float32).astype(jnp.bfloat16)
    out[:rows, half:] = jnp.dot(text[...], w_other[...], preferred_element_type=jnp.float32).astype(jnp.bfloat16)


def project(ids, text, queries, w_own, w_other, slab_count):
    width = w_own.shape[1] + w_other.shape[1]
    operands = [text, queries, w_own, w_other]
    return pl.pallas_call(
        functools.partial(project_kernel, slab_count=slab_count),
        grid_spec=pltpu.PrefetchScalarGridSpec(
            num_scalar_prefetch=1,
            grid=(1,),
            in_specs=[pl.BlockSpec(a.shape, lambda i, *_: (0, 0)) for a in operands],
            out_specs=pl.BlockSpec((text.shape[0] + 2 * EXTRA, width), lambda i, *_: (0, 0)),
        ),
        out_shape=jax.ShapeDtypeStruct((text.shape[0] + 2 * EXTRA, width), jnp.bfloat16),
        compiler_params=pltpu.CompilerParams(vmem_limit_bytes=VMEM_LIMIT),
        cost_estimate=pl.CostEstimate(
            flops=2 * text.shape[0] * text.shape[1] * width, bytes_accessed=2 << 20, transcendentals=0
        ),
        name="project",
    )(ids, *[in_hbm(a) for a in operands])


def to_scalars(vectors, decoded, table, sem):
    decoded[...] = vectors
    copy = pltpu.make_async_copy(decoded, table, sem)
    copy.start()
    copy.wait()


def request_kernel(place, owners, out, decoded, table, shared, sem, *, grid_x, rows, query_count, top_count):
    step = pl.program_id(0)
    depth, height = owners.shape[:2]
    texts = height - 2 * EXTRA
    slot_rows = depth * rows
    shared_rows = shared.shape[0]
    tile_row = row_of((EXTRA, LANES), 0)

    @pl.when(step == 0)
    def _():
        found = [jnp.zeros((EXTRA, LANES), jnp.float32) for _ in range(2)]
        for z in range(depth):
            code = owners[z, texts + EXTRA :, :].astype(jnp.float32)
            found = [jnp.where(tile_row == z, code[:, i * LANES : (i + 1) * LANES], found[i]) for i in range(2)]
        to_scalars(jnp.concatenate(found, axis=0).astype(jnp.int32), decoded, table, sem)
        picked = [owners[z, texts : texts + EXTRA, :].astype(jnp.float32)[:query_count] for z in range(depth)]
        shared[...] = jnp.concatenate(picked, axis=0).astype(jnp.bfloat16)

    lane = row_of((EXTRA, LANES), 1)
    for i in range(out.shape[0]):
        target = step * out.shape[0] + i
        shard = (lax.div(target, grid_x) * depth + place[0]) * grid_x + lax.rem(target, grid_x)
        code = jnp.full((EXTRA, LANES), -1.0, jnp.float32)
        for z in range(depth):
            image, listed = table[z, shard], table[EXTRA + z, shard]
            first = lax.div(jnp.maximum(listed, 0), top_count) * rows
            out[i, z * rows : (z + 1) * rows, :] = owners[z, pl.ds(pl.multiple_of(first, rows), rows), :]
            code = jnp.where(lane == z, image.astype(jnp.float32), code)
            code = jnp.where(lane == EXTRA + z, listed.astype(jnp.float32), code)
        out[i, slot_rows : slot_rows + shared_rows, :] = shared[...]
        out[i, slot_rows + shared_rows :, :LANES] = code.astype(jnp.bfloat16)


def make_request(place, owners, grid_y, grid_x, rows, query_count, top_count):
    depth, height, width = owners.shape
    shared_rows = depth * query_count
    total = depth * rows + shared_rows + EXTRA
    return pl.pallas_call(
        functools.partial(
            request_kernel, grid_x=grid_x, rows=rows, query_count=query_count, top_count=top_count
        ),
        grid_spec=pltpu.PrefetchScalarGridSpec(
            num_scalar_prefetch=1,
            grid=(grid_y * grid_x // 4,),
            in_specs=[pl.BlockSpec(owners.shape, lambda i, *_: (0, 0, 0))],
            out_specs=pl.BlockSpec((4, total, width), lambda i, *_: (i, 0, 0)),
            scratch_shapes=[
                pltpu.VMEM((2 * EXTRA, LANES), jnp.int32),
                pltpu.SMEM((2 * EXTRA, LANES), jnp.int32),
                pltpu.VMEM((shared_rows, width), jnp.bfloat16),
                pltpu.SemaphoreType.DMA,
            ],
        ),
        out_shape=pltpu.HBM((grid_y * grid_x, total, width), jnp.bfloat16),
        compiler_params=pltpu.CompilerParams(vmem_limit_bytes=VMEM_LIMIT),
        cost_estimate=pl.CostEstimate(flops=1 << 20, bytes_accessed=6 << 20, transcendentals=0),
        name="request",
    )(place, in_hbm(owners))


def index_stats(query, slab, picked, logits):
    count = query.shape[0]
    tile = min(256, slab.shape[0])
    peak = None
    for t in range(slab.shape[0] // tile):
        part = SCALE * lax.dot_general(
            slab[t * tile : (t + 1) * tile, :], query, (((1,), (1,)), ((), ())), preferred_element_type=jnp.float32
        )
        logits[t * tile : (t + 1) * tile, :] = part
        top = jnp.max(part, axis=0, keepdims=True)
        peak = top if peak is None else jnp.maximum(peak, top)
    total = jnp.zeros_like(peak)
    for t in range(slab.shape[0] // tile):
        total = total + jnp.sum(jnp.exp(logits[t * tile : (t + 1) * tile, :] - peak), axis=0, keepdims=True)
    chosen = row_of((tile, count), 0) == picked
    candidate = jnp.sum(jnp.where(chosen, logits[:tile, :], 0.0), axis=0, keepdims=True)
    return peak, total, candidate


def split_rows(exact):
    tile_row = row_of((EXTRA, LANES), 0)
    exact = jnp.broadcast_to(exact, (EXTRA, LANES))
    high = exact.astype(jnp.bfloat16).astype(jnp.float32)
    left = exact - high
    middle = left.astype(jnp.bfloat16).astype(jnp.float32)
    parts = jnp.where(tile_row == 0, high, jnp.where(tile_row == 1, middle, left - middle))
    return jnp.where(tile_row < 3, parts, 0.0)


def serve_kernel(
    got_hbm, slab_hbm, keys_hbm, values_hbm, out_hbm,
    out, got, slab, keys, values, logits, decoded, table, listed, sems, *, grid_x, depth, rows, query_count, top_count, head_size
):
    sources = got.shape[0]
    slots = sources * depth
    columns = keys.shape[2]
    slot_rows = depth * rows
    late = got.shape[1] - slot_rows
    copies = [
        pltpu.make_async_copy(source, target, sems.at[i])
        for i, (source, target) in enumerate(
            [
                (got_hbm.at[:, pl.ds(slot_rows, late), :], got.at[:, pl.ds(slot_rows, late), :]),
                (slab_hbm, slab),
                (got_hbm.at[:, pl.ds(0, slot_rows), :], got.at[:, pl.ds(0, slot_rows), :]),
                (keys_hbm, keys),
                (values_hbm, values),
            ]
        )
    ]
    for copy in copies:
        copy.start()
    shared_rows = depth * query_count
    body = columns // LANES * rows
    per_chunk = LANES // query_count
    lane = row_of((EXTRA, LANES), 1)
    tile_row = row_of((EXTRA, LANES), 0)

    copies[0].wait()
    found = [jnp.zeros((EXTRA, LANES), jnp.float32) for _ in range(-(-sources // EXTRA))]
    for source in range(sources):
        code = got[source, slot_rows + shared_rows :, :LANES].astype(jnp.float32)
        found[source // EXTRA] = jnp.where(tile_row == source % EXTRA, code, found[source // EXTRA])
    found = found[0] if len(found) == 1 else jnp.concatenate(found, axis=0)
    to_scalars(found.astype(jnp.int32), decoded, table, sems.at[5])

    count = 0
    chunks = [jnp.full((EXTRA, LANES), -1, jnp.int32) for _ in range(-(-slots // per_chunk))]
    for slot in range(slots):
        image, entry = table[slot // depth, slot % depth], table[slot // depth, EXTRA + slot % depth]
        query = lax.div(jnp.maximum(entry, 0), top_count)
        at = slot % per_chunk * query_count + query
        chunks[slot // per_chunk] = jnp.where(lane == at, image, chunks[slot // per_chunk])
        listed[count] = slot
        count = count + jnp.where(image >= 0, 1, 0)
    last = listed[jnp.maximum(count - 1, 0)]
    for g in range(UNROLL):
        listed[count + g] = last

    queries = jnp.concatenate([got[source, slot_rows : slot_rows + shared_rows, :] for source in range(sources)], axis=0)
    missing = len(chunks) * LANES - queries.shape[0]
    if missing:
        queries = jnp.concatenate([queries, jnp.zeros((missing, queries.shape[1]), queries.dtype)], axis=0)
    copies[1].wait()
    stats = index_stats(queries, slab, jnp.concatenate([chunk[:1] for chunk in chunks], axis=1), logits)
    for c in range(len(chunks)):
        tiles = [split_rows(stat[:, c * LANES : (c + 1) * LANES]) for stat in stats]
        tiles = [tiles[0], pltpu.roll(tiles[1], query_count, 1), pltpu.roll(tiles[2], 2 * query_count, 1)]
        for slot in range(c * per_chunk, min((c + 1) * per_chunk, slots)):
            source, z = slot // depth, slot % depth
            at = slot % per_chunk
            owner = (source // grid_x * depth + z) * grid_x + source % grid_x
            place = lane // query_count
            tile = jnp.where(place == at, tiles[0], jnp.where(place == (at + 1) % per_chunk, tiles[1], tiles[2]))
            out[owner, body:, :] = tile.astype(jnp.bfloat16)

    stats_out = pltpu.make_async_copy(
        out.at[:, pl.ds(body, EXTRA), :], out_hbm.at[:, pl.ds(body, EXTRA), :], sems.at[6]
    )
    stats_out.start()

    def send(owner):
        return pltpu.make_async_copy(out.at[owner, pl.ds(0, body), :], out_hbm.at[owner, pl.ds(0, body), :], sems.at[7])

    copies[2].wait()
    copies[3].wait()
    copies[4].wait()
    spans = []
    at = 0
    while at < columns:
        width = min(2 * LANES, columns - at)
        lane_head = row_of((rows, width), 1) // head_size
        spans.append((at, width, [jnp.where(lane_head == h, 1.0, 0.0) for h in range(width // head_size)]))
        at += width

    def group(index, carry):
        chosen = [listed[index * UNROLL + g] for g in range(UNROLL)]
        places = [(lax.div(slot, depth), lax.rem(slot, depth)) for slot in chosen]
        images = [table[source, z] for source, z in places]
        owners = [
            (lax.div(source, grid_x) * depth + z) * grid_x + lax.rem(source, grid_x) for source, z in places
        ]
        work = [(g, span) for g in range(UNROLL) for span in spans]
        scores = []
        for g, (at, width, masks) in work:
            source, z = places[g]
            query = got[source, pl.ds(pl.multiple_of(z * rows, rows), rows), at : at + width]
            spread = jnp.concatenate([query * mask.astype(query.dtype) for mask in masks], axis=0)
            scores.append(
                lax.dot_general(
                    spread,
                    keys[images[g], :, at : at + width],
                    (((1,), (1,)), ((), ())),
                    preferred_element_type=jnp.float32,
                )
            )
        scores = [score * head_size ** (-0.5) for score in scores]
        highest = [jnp.max(score, axis=-1, keepdims=True) for score in scores]
        powers = [jnp.exp(score - top) for score, top in zip(scores, highest)]
        totals = [jnp.sum(power, axis=-1, keepdims=True) for power in powers]
        weights = [(power / total).astype(jnp.bfloat16) for power, total in zip(powers, totals)]
        mixed = [
            jnp.dot(weight, values[images[g], :, at : at + width], preferred_element_type=jnp.float32)
            for weight, (g, (at, width, _)) in zip(weights, work)
        ]
        for mix, (g, (at, width, masks)) in zip(mixed, work):
            context = mix[:rows] * masks[0]
            for h in range(1, len(masks)):
                context = context + mix[h * rows : (h + 1) * rows] * masks[h]
            context = context.astype(jnp.bfloat16)
            for c in range(width // LANES):
                out[owners[g], (at // LANES + c) * rows : (at // LANES + c + 1) * rows, :] = context[
                    :, c * LANES : (c + 1) * LANES
                ]
        for owner in owners:
            send(owner).start()
        return carry

    def drain(index, carry):
        for _ in range(UNROLL):
            send(0).wait()
        return carry

    groups = lax.div(count + UNROLL - 1, UNROLL)
    lax.fori_loop(0, groups, group, 0)
    lax.fori_loop(0, groups, drain, 0)
    stats_out.wait()


def serve(got, slab, keys, values, grid_x, depth, rows, query_count, top_count, head_size):
    sources = got.shape[0]
    slots = sources * depth
    body = keys.shape[2] // LANES * rows
    lanes = -(-slots * query_count // LANES) * LANES
    operands = [got, slab, keys, values]
    codes = (-(-sources // EXTRA) * EXTRA, LANES)
    return pl.pallas_call(
        functools.partial(
            serve_kernel,
            grid_x=grid_x,
            depth=depth,
            rows=rows,
            query_count=query_count,
            top_count=top_count,
            head_size=head_size,
        ),
        grid=(1,),
        in_specs=[pl.BlockSpec(memory_space=pltpu.HBM)] * 4,
        out_specs=pl.BlockSpec(memory_space=pltpu.HBM),
        scratch_shapes=[pltpu.VMEM((slots, body + EXTRA, LANES), jnp.bfloat16)]
        + [pltpu.VMEM(a.shape, a.dtype) for a in operands]
        + [
            pltpu.VMEM((slab.shape[0], lanes), jnp.float32),
            pltpu.VMEM(codes, jnp.int32),
            pltpu.SMEM(codes, jnp.int32),
            pltpu.SMEM((slots + UNROLL,), jnp.int32),
            pltpu.SemaphoreType.DMA((8,)),
        ],
        out_shape=pltpu.HBM((slots, body + EXTRA, LANES), jnp.bfloat16),
        compiler_params=pltpu.CompilerParams(vmem_limit_bytes=VMEM_LIMIT),
        cost_estimate=pl.CostEstimate(flops=8 << 30, bytes_accessed=14 << 20, transcendentals=2 << 20),
        name="serve",
    )(*[in_hbm(a) for a in operands])


def finish_kernel(
    shards, place, back_hbm, text, w_out, gain, found, out,
    exact, normalizers, gathered, back, sent, sems, *, top_count, query_count, shift
):
    step = pl.program_id(0)
    rows = text.shape[1]
    body = back.shape[1]

    def fetch(entry, query):
        return pltpu.make_async_copy(back_hbm.at[shards[entry], pl.ds(0, body), :], back.at[entry], sems.at[query])

    @pl.when(step == 0)
    def _():
        stats = pltpu.make_async_copy(back_hbm.at[:, pl.ds(body, EXTRA), :], sent, sems.at[query_count])
        stats.start()
        for query in range(query_count):
            for k in range(top_count):
                fetch(query * top_count + k, query // text.shape[0]).start()
        stats.wait()
        parts = sent[...].astype(jnp.float32)
        joined = jnp.sum(jnp.where(row_of(parts.shape, 1) < 3, parts, 0.0), axis=1)
        joined = pltpu.roll(joined, lax.rem(LANES - place[0] * query_count, LANES), 1)
        exact[...] = joined
        peak = jnp.max(joined, axis=0, keepdims=True)
        scaled = jnp.exp(joined - peak) * pltpu.roll(joined, LANES - query_count, 1)
        total = jnp.sum(scaled, axis=0, keepdims=True)
        total = jnp.where(row_of(total.shape, 1) < query_count, total, 1.0)
        normalizers[...] = jnp.broadcast_to(peak + jnp.log(total), normalizers.shape)

    per_step = text.shape[0]
    for i in range(per_step):
        query = step * per_step + i
        picked = jnp.concatenate(
            [exact[pl.ds(shards[query * top_count + k], 1), :] for k in range(top_count)], axis=0
        )
        lane = row_of(picked.shape, 1)
        candidate = jnp.sum(jnp.where(lane == 2 * query_count + query, picked, 0.0), axis=1, keepdims=True)
        normalizer = jnp.sum(jnp.where(lane[:1] == query, normalizers[:1, :], 0.0), axis=1, keepdims=True)
        result = candidate - normalizer + shift
        result = jnp.sum(jnp.where(lane == row_of(picked.shape, 0), result, 0.0), axis=0, keepdims=True)
        found[pl.ds(query, 1), :] = result[:, :top_count]

    entries = per_step * top_count
    for k in range(entries):
        fetch(step * entries + k, step).wait()
    for k in range(entries):
        for j in range(body // rows):
            gathered[k * rows : (k + 1) * rows, j * LANES : (j + 1) * LANES] = back[
                step * entries + k, j * rows : (j + 1) * rows, :
            ]
    mixed = jnp.dot(gathered[...], w_out[...], preferred_element_type=jnp.float32)
    width = mixed.shape[1]
    summed = mixed.reshape(per_step, top_count, rows, width) + text[...].astype(jnp.float32).reshape(per_step, 1, rows, width)
    mean = jnp.mean(summed, axis=-1, keepdims=True)
    centred = summed - mean
    variance = jnp.mean(centred * centred, axis=-1, keepdims=True)
    normed = centred * lax.rsqrt(variance + EPSILON) * gain[...].reshape(1, 1, 1, width)
    out[...] = normed.astype(jnp.bfloat16)


def finish(shards, place, back, text, w_out, gain, top_count, shift):
    query_count, rows, width = text.shape
    per_step = 2
    full = lambda a: pl.BlockSpec(a.shape, lambda i, *_: (0,) * a.ndim)
    return pl.pallas_call(
        functools.partial(finish_kernel, top_count=top_count, query_count=query_count, shift=shift),
        grid_spec=pltpu.PrefetchScalarGridSpec(
            num_scalar_prefetch=2,
            grid=(query_count // per_step,),
            in_specs=[
                pl.BlockSpec(memory_space=pltpu.HBM),
                pl.BlockSpec((per_step, rows, width), lambda i, *_: (i, 0, 0)),
                full(w_out),
                full(gain),
            ],
            out_specs=[
                pl.BlockSpec((query_count, top_count), lambda i, *_: (0, 0)),
                pl.BlockSpec((per_step, top_count, rows, width), lambda i, *_: (i, 0, 0, 0)),
            ],
            scratch_shapes=[
                pltpu.VMEM((back.shape[0], LANES), jnp.float32),
                pltpu.VMEM((EXTRA, LANES), jnp.float32),
                pltpu.VMEM((per_step * top_count * rows, width), jnp.bfloat16),
                pltpu.VMEM((query_count * top_count, back.shape[1] - EXTRA, LANES), jnp.bfloat16),
                pltpu.VMEM((back.shape[0], EXTRA, LANES), jnp.bfloat16),
                pltpu.SemaphoreType.DMA((query_count + 1,)),
            ],
        ),
        out_shape=[
            jax.ShapeDtypeStruct((query_count, top_count), jnp.float32),
            jax.ShapeDtypeStruct((query_count, top_count, rows, width), jnp.bfloat16),
        ],
        compiler_params=pltpu.CompilerParams(vmem_limit_bytes=VMEM_LIMIT),
        cost_estimate=pl.CostEstimate(
            flops=2 * query_count * top_count * rows * width * width, bytes_accessed=7 << 20, transcendentals=0
        ),
        name="finish",
    )(shards, place, in_hbm(back), text, in_hbm(w_out), gain)


def project_rows(rows_in, weight):
    return jnp.einsum("spc,cd->spd", rows_in, weight, preferred_element_type=jnp.float32).astype(jnp.bfloat16)


def on_device(queries, slab, cand_ids, patches, text_states, w_query, w_key, w_value, w_out, norm_gain):
    shard_count = lax.axis_size("shard")
    shard_here = lax.axis_index("shard")
    core = lax.axis_index("rep")
    grid_y, depth, grid_x = GRIDS[shard_count]
    query_count = queries.shape[0]
    slab_count = slab.shape[0]
    top_count = cand_ids.shape[1]
    list_length = query_count * top_count
    text_count, model_width = text_states.shape[1:]
    head_size = model_width // HEADS
    here_x, here_z, here_y = shard_here % grid_x, shard_here // grid_x % depth, shard_here // (grid_x * depth)
    columns = [
        [(y * depth + z) * grid_x + x for z in range(depth)] for y in range(grid_y) for x in range(grid_x)
    ]
    planes = [
        [(y * depth + z) * grid_x + x for y in range(grid_y) for x in range(grid_x)] for z in range(depth)
    ]
    swap = [(0, 1), (1, 0)]
    w_query_other = lax.ppermute(w_query, "rep", swap)

    own_list = cand_ids.reshape(list_length)
    own_anchor = own_list // slab_count
    sent = project(
        cand_ids,
        text_states.reshape(query_count * text_count, model_width),
        queries,
        w_query,
        w_query_other,
        slab_count,
    )
    owners = lax.all_gather(sent, "shard", axis=0, tiled=True, axis_index_groups=columns)
    request = make_request(
        here_z.reshape(1),
        owners.reshape(depth, sent.shape[0], model_width),
        grid_y,
        grid_x,
        text_count,
        query_count,
        top_count,
    )
    got = lax.all_to_all(request, "shard", split_axis=0, concat_axis=0, tiled=True, axis_index_groups=planes)

    keys = project_rows(patches, jnp.concatenate([w_key, lax.ppermute(w_key, "rep", swap)], axis=1))
    values = project_rows(patches, jnp.concatenate([w_value, lax.ppermute(w_value, "rep", swap)], axis=1))
    w_out_other = lax.ppermute(w_out, "rep", swap)
    half = model_width // 2
    w_out_whole = jnp.where(
        core == 0,
        jnp.concatenate([w_out, w_out_other], axis=1),
        jnp.concatenate(
            [
                jnp.concatenate([w_out_other[half:], w_out[half:]], axis=1),
                jnp.concatenate([w_out_other[:half], w_out[:half]], axis=1),
            ],
            axis=0,
        ),
    )

    context = serve(got, slab, keys, values, grid_x, depth, text_count, query_count, top_count, head_size)
    back = lax.all_to_all(context, "shard", split_axis=0, concat_axis=0, tiled=True)

    place = ((here_y * grid_x + here_x) * depth + here_z) % (LANES // query_count)
    retrieval, attended = finish(
        own_anchor,
        place.reshape(1),
        back,
        text_states,
        w_out_whole,
        norm_gain.reshape(1, model_width),
        top_count,
        math.log(slab_count * shard_count),
    )
    return (retrieval, attended)


def solution(mesh):
    in_specs = (
        P(("shard", "rep"), None),
        P("shard", None),
        P(("shard", "rep"), None),
        P("shard", None, None),
        P(("shard", "rep"), None, None),
        P(None, "rep"),
        P(None, "rep"),
        P(None, "rep"),
        P(None, "rep"),
        P(),
    )
    out_specs = (P(("shard", "rep"), None), P(("shard", "rep"), None, None, None))
    return jax.shard_map(
        on_device, mesh=mesh, in_specs=in_specs, out_specs=out_specs, check_vma=False
    )
```

```python
import functools
import math

import jax
import jax.numpy as jnp
from jax import lax
from jax.experimental import pallas as pl
from jax.experimental.pallas import tpu as pltpu
from jax.sharding import PartitionSpec as P

HEADS = 12
SCALE = 100.0
EPSILON = 1e-06
LANES = 128
EXTRA = 8
UNROLL = 16
GRIDS = {128: (4, 8, 4), 8: (2, 2, 2)}
VMEM_LIMIT = 48 * 1024 * 1024


def row_of(shape, dim):
    return lax.broadcasted_iota(jnp.int32, shape, dim)


def in_hbm(array):
    return pltpu.with_memory_space_constraint(array, pltpu.HBM)


def project_kernel(ids, text, queries, w_own, w_other, out, *, slab_count):
    rows = text.shape[0]
    half = w_own.shape[1]
    count, width = queries.shape
    lane = row_of((EXTRA, LANES), 1)
    image = jnp.full((EXTRA, LANES), -1, jnp.int32)
    listed = image
    for entry in range(ids.shape[0] * ids.shape[1]):
        row = ids[entry // ids.shape[1], entry % ids.shape[1]]
        here = lane == lax.div(row, slab_count)
        image = jnp.where(here, lax.rem(row, slab_count), image)
        listed = jnp.where(here, entry, listed)
    pieces = [queries[...].astype(jnp.float32)]
    if count < EXTRA:
        pieces.append(jnp.zeros((EXTRA - count, width), jnp.float32))
    code = [image.astype(jnp.float32), listed.astype(jnp.float32)]
    code.append(jnp.zeros((EXTRA, width - 2 * LANES), jnp.float32))
    pieces.append(jnp.concatenate(code, axis=1))
    out[rows:, :] = jnp.concatenate(pieces, axis=0).astype(jnp.bfloat16)
    out[:rows, :half] = jnp.dot(text[...], w_own[...], preferred_element_type=jnp.float32).astype(jnp.bfloat16)
    out[:rows, half:] = jnp.dot(text[...], w_other[...], preferred_element_type=jnp.float32).astype(jnp.bfloat16)


def project(ids, text, queries, w_own, w_other, slab_count):
    width = w_own.shape[1] + w_other.shape[1]
    operands = [text, queries, w_own, w_other]
    return pl.pallas_call(
        functools.partial(project_kernel, slab_count=slab_count),
        grid_spec=pltpu.PrefetchScalarGridSpec(
            num_scalar_prefetch=1,
            grid=(1,),
            in_specs=[pl.BlockSpec(a.shape, lambda i, *_: (0, 0)) for a in operands],
            out_specs=pl.BlockSpec((text.shape[0] + 2 * EXTRA, width), lambda i, *_: (0, 0)),
        ),
        out_shape=jax.ShapeDtypeStruct((text.shape[0] + 2 * EXTRA, width), jnp.bfloat16),
        compiler_params=pltpu.CompilerParams(vmem_limit_bytes=VMEM_LIMIT),
        cost_estimate=pl.CostEstimate(
            flops=2 * text.shape[0] * text.shape[1] * width, bytes_accessed=2 << 20, transcendentals=0
        ),
        name="project",
    )(ids, in_hbm(text), in_hbm(queries), in_hbm(w_own), w_other)


def to_scalars(vectors, decoded, table, sem):
    decoded[...] = vectors
    copy = pltpu.make_async_copy(decoded, table, sem)
    copy.start()
    copy.wait()


def read_codes(owners, decoded, table, sem):
    depth, height = owners.shape[:2]
    tile_row = row_of((EXTRA, LANES), 0)
    found = [jnp.zeros((EXTRA, LANES), jnp.float32) for _ in range(2)]
    for z in range(depth):
        code = owners[z, height - EXTRA :, : 2 * LANES].astype(jnp.float32)
        found = [jnp.where(tile_row == z, code[:, i * LANES : (i + 1) * LANES], found[i]) for i in range(2)]
    to_scalars(jnp.concatenate(found, axis=0).astype(jnp.int32), decoded, table, sem)


def first_request_kernel(place, owners, out, decoded, table, sem, *, grid_x, rows, top_count):
    step = pl.program_id(0)
    depth = owners.shape[0]
    columns = out.shape[2]

    @pl.when(step == 0)
    def _():
        read_codes(owners, decoded, table, sem)

    lane = row_of((EXTRA, LANES), 1)
    for i in range(out.shape[0]):
        target = step * out.shape[0] + i
        shard = (lax.div(target, grid_x) * depth + place[0]) * grid_x + lax.rem(target, grid_x)
        code = jnp.full((EXTRA, LANES), -1.0, jnp.float32)
        for z in range(depth):
            image, entry = table[z, shard], table[EXTRA + z, shard]
            first = lax.div(jnp.maximum(entry, 0), top_count) * rows
            out[i, z * rows : (z + 1) * rows, :] = owners[z, pl.ds(pl.multiple_of(first, rows), rows), :columns]
            code = jnp.where(lane == z, image.astype(jnp.float32), code)
            code = jnp.where(lane == EXTRA + z, entry.astype(jnp.float32), code)
        out[i, depth * rows :, :LANES] = code.astype(jnp.bfloat16)


def first_request(place, owners, grid_y, grid_x, rows, top_count):
    depth, height, width = owners.shape
    columns = width // 2
    total = depth * rows + EXTRA
    block = 4
    return pl.pallas_call(
        functools.partial(first_request_kernel, grid_x=grid_x, rows=rows, top_count=top_count),
        grid_spec=pltpu.PrefetchScalarGridSpec(
            num_scalar_prefetch=1,
            grid=(grid_y * grid_x // block,),
            in_specs=[pl.BlockSpec(owners.shape, lambda i, *_: (0, 0, 0))],
            out_specs=pl.BlockSpec((block, total, columns), lambda i, *_: (i, 0, 0)),
            scratch_shapes=[
                pltpu.VMEM((2 * EXTRA, LANES), jnp.int32),
                pltpu.SMEM((2 * EXTRA, LANES), jnp.int32),
                pltpu.SemaphoreType.DMA,
            ],
        ),
        out_shape=pltpu.HBM((grid_y * grid_x, total, columns), jnp.bfloat16),
        compiler_params=pltpu.CompilerParams(vmem_limit_bytes=VMEM_LIMIT),
        cost_estimate=pl.CostEstimate(flops=1 << 20, bytes_accessed=4 << 20, transcendentals=0),
        name="first_request",
    )(place, in_hbm(owners))


def second_request_kernel(place, after, owners, *rest, grid_y, grid_x, rows, query_count, top_count):
    outs = rest[: grid_y * grid_x]
    decoded, table, sem = rest[grid_y * grid_x :]
    depth, height, width = owners.shape
    columns = width // 2
    texts = height - 2 * EXTRA
    read_codes(owners, decoded, table, sem)
    picked = [owners[z, texts : texts + EXTRA, :].astype(jnp.float32)[:query_count] for z in range(depth)]
    shared = jnp.concatenate(picked, axis=0).astype(jnp.bfloat16)
    for k, out in enumerate(outs):
        y = lax.rem(place[1] + k // grid_x, grid_y)
        x = lax.rem(place[2] + k % grid_x, grid_x)
        shard = (y * depth + place[0]) * grid_x + x
        for z in range(depth):
            first = lax.div(jnp.maximum(table[EXTRA + z, shard], 0), top_count) * rows
            out[z * rows : (z + 1) * rows, :] = owners[z, pl.ds(pl.multiple_of(first, rows), rows), columns:]
        at = depth * rows
        out[at : at + shared.shape[0], :] = shared[:, :columns]
        out[at + shared.shape[0] :, :] = shared[:, columns:]


def second_request(place, after, owners, grid_y, grid_x, rows, query_count, top_count):
    depth, height, width = owners.shape
    total = depth * rows + 2 * depth * query_count
    count = grid_y * grid_x
    return pl.pallas_call(
        functools.partial(
            second_request_kernel,
            grid_y=grid_y,
            grid_x=grid_x,
            rows=rows,
            query_count=query_count,
            top_count=top_count,
        ),
        grid_spec=pltpu.PrefetchScalarGridSpec(
            num_scalar_prefetch=2,
            grid=(1,),
            in_specs=[pl.BlockSpec(owners.shape, lambda i, *_: (0, 0, 0))],
            out_specs=[pl.BlockSpec((total, width // 2), lambda i, *_: (0, 0))] * count,
            scratch_shapes=[
                pltpu.VMEM((2 * EXTRA, LANES), jnp.int32),
                pltpu.SMEM((2 * EXTRA, LANES), jnp.int32),
                pltpu.SemaphoreType.DMA,
            ],
        ),
        out_shape=[pltpu.HBM((total, width // 2), jnp.bfloat16)] * count,
        compiler_params=pltpu.CompilerParams(vmem_limit_bytes=VMEM_LIMIT),
        cost_estimate=pl.CostEstimate(flops=1 << 20, bytes_accessed=4 << 20, transcendentals=0),
        name="second_request",
    )(place, after, in_hbm(owners))


def index_stats(query, slab, picked, logits):
    count = query.shape[0]
    tile = min(256, slab.shape[0])
    peak = None
    for t in range(slab.shape[0] // tile):
        part = SCALE * lax.dot_general(
            slab[t * tile : (t + 1) * tile, :], query, (((1,), (1,)), ((), ())), preferred_element_type=jnp.float32
        )
        logits[t * tile : (t + 1) * tile, :] = part
        top = jnp.max(part, axis=0, keepdims=True)
        peak = top if peak is None else jnp.maximum(peak, top)
    total = jnp.zeros_like(peak)
    for t in range(slab.shape[0] // tile):
        total = total + jnp.sum(jnp.exp(logits[t * tile : (t + 1) * tile, :] - peak), axis=0, keepdims=True)
    chosen = row_of((tile, count), 0) == picked
    candidate = jnp.sum(jnp.where(chosen, logits[:tile, :], 0.0), axis=0, keepdims=True)
    return peak, total, candidate


def split_rows(exact):
    tile_row = row_of((EXTRA, LANES), 0)
    exact = jnp.broadcast_to(exact, (EXTRA, LANES))
    high = exact.astype(jnp.bfloat16).astype(jnp.float32)
    left = exact - high
    middle = left.astype(jnp.bfloat16).astype(jnp.float32)
    parts = jnp.where(tile_row == 0, high, jnp.where(tile_row == 1, middle, left - middle))
    return jnp.where(tile_row < 3, parts, 0.0)


def list_slots(slots, depth, table, listed):
    count = 0
    for slot in range(slots):
        listed[count] = slot
        count = count + jnp.where(table[slot // depth, slot % depth] >= 0, 1, 0)
    last = listed[jnp.maximum(count - 1, 0)]
    for g in range(UNROLL):
        listed[count + g] = last
    return count


def attend_slots(count, listed, table, got, keys, values, out, send, *, grid_x, depth, rows, head_size):
    columns = keys.shape[2]
    spans = []
    at = 0
    while at < columns:
        width = min(2 * LANES, columns - at)
        lane_head = row_of((rows, width), 1) // head_size
        spans.append((at, width, [jnp.where(lane_head == h, 1.0, 0.0) for h in range(width // head_size)]))
        at += width

    def group(index, carry):
        chosen = [listed[index * UNROLL + g] for g in range(UNROLL)]
        places = [(lax.div(slot, depth), lax.rem(slot, depth)) for slot in chosen]
        images = [table[source, z] for source, z in places]
        owners = [
            (lax.div(source, grid_x) * depth + z) * grid_x + lax.rem(source, grid_x) for source, z in places
        ]
        work = [(g, span) for g in range(UNROLL) for span in spans]
        scores = []
        for g, (at, width, masks) in work:
            source, z = places[g]
            query = got[source, pl.ds(pl.multiple_of(z * rows, rows), rows), at : at + width]
            spread = jnp.concatenate([query * mask.astype(query.dtype) for mask in masks], axis=0)
            scores.append(
                lax.dot_general(
                    spread,
                    keys[images[g], :, at : at + width],
                    (((1,), (1,)), ((), ())),
                    preferred_element_type=jnp.float32,
                )
            )
        scores = [score * head_size ** (-0.5) for score in scores]
        highest = [jnp.max(score, axis=-1, keepdims=True) for score in scores]
        powers = [jnp.exp(score - top) for score, top in zip(scores, highest)]
        totals = [jnp.sum(power, axis=-1, keepdims=True) for power in powers]
        weights = [(power / total).astype(jnp.bfloat16) for power, total in zip(powers, totals)]
        mixed = [
            jnp.dot(weight, values[images[g], :, at : at + width], preferred_element_type=jnp.float32)
            for weight, (g, (at, width, _)) in zip(weights, work)
        ]
        for mix, (g, (at, width, masks)) in zip(mixed, work):
            context = mix[:rows] * masks[0]
            for h in range(1, len(masks)):
                context = context + mix[h * rows : (h + 1) * rows] * masks[h]
            context = context.astype(jnp.bfloat16)
            for c in range(width // LANES):
                out[owners[g], (at // LANES + c) * rows : (at // LANES + c + 1) * rows, :] = context[
                    :, c * LANES : (c + 1) * LANES
                ]
        for owner in owners:
            send(owner).start()
        return carry

    def drain(index, carry):
        for _ in range(UNROLL):
            send(0).wait()
        return carry

    groups = lax.div(count + UNROLL - 1, UNROLL)
    lax.fori_loop(0, groups, group, 0)
    lax.fori_loop(0, groups, drain, 0)


def first_serve_kernel(
    got_hbm, keys_hbm, values_hbm, out_hbm, decoded, out, got, keys, values, table, listed, sems,
    *, grid_x, depth, rows, head_size
):
    copies = [
        pltpu.make_async_copy(source, target, sems.at[i])
        for i, (source, target) in enumerate([(got_hbm, got), (keys_hbm, keys), (values_hbm, values)])
    ]
    for copy in copies:
        copy.start()
    sources = got.shape[0]
    tile_row = row_of((EXTRA, LANES), 0)
    copies[0].wait()
    found = [jnp.zeros((EXTRA, LANES), jnp.float32) for _ in range(-(-sources // EXTRA))]
    for source in range(sources):
        code = got[source, depth * rows :, :LANES].astype(jnp.float32)
        found[source // EXTRA] = jnp.where(tile_row == source % EXTRA, code, found[source // EXTRA])
    found = found[0] if len(found) == 1 else jnp.concatenate(found, axis=0)
    to_scalars(found.astype(jnp.int32), decoded, table, sems.at[3])
    count = list_slots(sources * depth, depth, table, listed)

    def send(owner):
        return pltpu.make_async_copy(out.at[owner], out_hbm.at[owner], sems.at[4])

    copies[1].wait()
    copies[2].wait()
    attend_slots(
        count, listed, table, got, keys, values, out, send, grid_x=grid_x, depth=depth, rows=rows, head_size=head_size
    )


def first_serve(got, keys, values, grid_x, depth, rows, head_size):
    sources = got.shape[0]
    slots = sources * depth
    body = keys.shape[2] // LANES * rows
    operands = [got, keys, values]
    codes = (-(-sources // EXTRA) * EXTRA, LANES)
    return pl.pallas_call(
        functools.partial(first_serve_kernel, grid_x=grid_x, depth=depth, rows=rows, head_size=head_size),
        grid=(1,),
        in_specs=[pl.BlockSpec(memory_space=pltpu.HBM)] * 3,
        out_specs=[pl.BlockSpec(memory_space=pltpu.HBM), pl.BlockSpec(codes, lambda i: (0, 0))],
        scratch_shapes=[pltpu.VMEM((slots, body, LANES), jnp.bfloat16)]
        + [pltpu.VMEM(a.shape, a.dtype) for a in operands]
        + [
            pltpu.SMEM(codes, jnp.int32),
            pltpu.SMEM((slots + UNROLL,), jnp.int32),
            pltpu.SemaphoreType.DMA((5,)),
        ],
        out_shape=[pltpu.HBM((slots, body, LANES), jnp.bfloat16), jax.ShapeDtypeStruct(codes, jnp.int32)],
        compiler_params=pltpu.CompilerParams(vmem_limit_bytes=VMEM_LIMIT),
        cost_estimate=pl.CostEstimate(flops=4 << 30, bytes_accessed=6 << 20, transcendentals=1 << 20),
        name="first_serve",
    )(*[in_hbm(a) for a in operands])


def second_serve_kernel(
    place, table, *rest, grid_y, grid_x, depth, rows, query_count, top_count, head_size
):
    sources = grid_y * grid_x
    arrived = rest[:sources]
    slab_hbm, keys_hbm, values_hbm, out_hbm, out, got, slab, keys, values, logits, listed, sems = rest[sources:]
    slots = sources * depth
    columns = keys.shape[2]
    slot_rows = depth * rows
    shared_rows = depth * query_count
    body = columns // LANES * rows
    per_chunk = LANES // query_count
    late = got.shape[1] - slot_rows
    lane = row_of((EXTRA, LANES), 1)

    def fetch(k, start, size, sem):
        y = lax.rem(place[1] + grid_y - k // grid_x, grid_y)
        x = lax.rem(place[2] + grid_x - k % grid_x, grid_x)
        return pltpu.make_async_copy(
            arrived[k].at[pl.ds(start, size), :], got.at[y * grid_x + x, pl.ds(start, size), :], sems.at[sem]
        )

    early = [fetch(k, slot_rows, late, 0) for k in range(sources)]
    main = [fetch(k, 0, slot_rows, 1) for k in range(sources)]
    copies = [
        pltpu.make_async_copy(source, target, sems.at[2 + i])
        for i, (source, target) in enumerate([(slab_hbm, slab), (keys_hbm, keys), (values_hbm, values)])
    ]
    for copy in early + copies[:1] + main + copies[1:]:
        copy.start()

    count = list_slots(slots, depth, table, listed)
    chunks = [jnp.full((EXTRA, LANES), -1, jnp.int32) for _ in range(-(-slots // per_chunk))]
    for slot in range(slots):
        image, entry = table[slot // depth, slot % depth], table[slot // depth, EXTRA + slot % depth]
        query = lax.div(jnp.maximum(entry, 0), top_count)
        at = slot % per_chunk * query_count + query
        chunks[slot // per_chunk] = jnp.where(lane == at, image, chunks[slot // per_chunk])

    for copy in early:
        copy.wait()
    queries = jnp.concatenate(
        [
            jnp.concatenate(
                [
                    got[source, slot_rows + i * shared_rows : slot_rows + (i + 1) * shared_rows, :]
                    for i in range(late // shared_rows)
                ],
                axis=1,
            )
            for source in range(sources)
        ],
        axis=0,
    )
    missing = len(chunks) * LANES - queries.shape[0]
    if missing:
        queries = jnp.concatenate([queries, jnp.zeros((missing, queries.shape[1]), queries.dtype)], axis=0)
    copies[0].wait()
    stats = index_stats(queries, slab, jnp.concatenate([chunk[:1] for chunk in chunks], axis=1), logits)
    for c in range(len(chunks)):
        tiles = [split_rows(stat[:, c * LANES : (c + 1) * LANES]) for stat in stats]
        tiles = [tiles[0], pltpu.roll(tiles[1], query_count, 1), pltpu.roll(tiles[2], 2 * query_count, 1)]
        for slot in range(c * per_chunk, min((c + 1) * per_chunk, slots)):
            source, z = slot // depth, slot % depth
            at = slot % per_chunk
            owner = (source // grid_x * depth + z) * grid_x + source % grid_x
            part = lane // query_count
            tile = jnp.where(part == at, tiles[0], jnp.where(part == (at + 1) % per_chunk, tiles[1], tiles[2]))
            out[owner, body:, :] = tile.astype(jnp.bfloat16)
    stats_out = pltpu.make_async_copy(
        out.at[:, pl.ds(body, EXTRA), :], out_hbm.at[:, pl.ds(body, EXTRA), :], sems.at[5]
    )
    stats_out.start()

    def send(owner):
        return pltpu.make_async_copy(out.at[owner, pl.ds(0, body), :], out_hbm.at[owner, pl.ds(0, body), :], sems.at[6])

    for copy in main + copies[1:]:
        copy.wait()
    attend_slots(
        count, listed, table, got, keys, values, out, send, grid_x=grid_x, depth=depth, rows=rows, head_size=head_size
    )
    stats_out.wait()


def second_serve(place, table, arrived, slab, keys, values, grid_y, grid_x, depth, rows, query_count, top_count, head_size):
    sources = grid_y * grid_x
    slots = sources * depth
    body = keys.shape[2] // LANES * rows
    lanes = -(-slots * query_count // LANES) * LANES
    operands = [*arrived, slab, keys, values]
    return pl.pallas_call(
        functools.partial(
            second_serve_kernel,
            grid_y=grid_y,
            grid_x=grid_x,
            depth=depth,
            rows=rows,
            query_count=query_count,
            top_count=top_count,
            head_size=head_size,
        ),
        grid_spec=pltpu.PrefetchScalarGridSpec(
            num_scalar_prefetch=2,
            grid=(1,),
            in_specs=[pl.BlockSpec(memory_space=pltpu.HBM)] * len(operands),
            out_specs=pl.BlockSpec(memory_space=pltpu.HBM),
            scratch_shapes=[
                pltpu.VMEM((slots, body + EXTRA, LANES), jnp.bfloat16),
                pltpu.VMEM((sources, *arrived[0].shape), jnp.bfloat16),
            ]
            + [pltpu.VMEM(a.shape, a.dtype) for a in (slab, keys, values)]
            + [
                pltpu.VMEM((slab.shape[0], lanes), jnp.float32),
                pltpu.SMEM((slots + UNROLL,), jnp.int32),
                pltpu.SemaphoreType.DMA((7,)),
            ],
        ),
        out_shape=pltpu.HBM((slots, body + EXTRA, LANES), jnp.bfloat16),
        compiler_params=pltpu.CompilerParams(vmem_limit_bytes=VMEM_LIMIT),
        cost_estimate=pl.CostEstimate(flops=6 << 30, bytes_accessed=10 << 20, transcendentals=2 << 20),
        name="second_serve",
    )(place, table, *[in_hbm(a) for a in operands])


def finish_kernel(
    shards, place, first_hbm, second_hbm, text, w_out, gain, found, out,
    exact, normalizers, gathered, back, sent, sems, *, top_count, query_count, shift
):
    step = pl.program_id(0)
    rows = text.shape[1]
    body = back.shape[1]
    half = body // 2

    def fetch(entry, query):
        return [
            pltpu.make_async_copy(
                source.at[shards[entry], pl.ds(0, half), :], back.at[entry, pl.ds(i * half, half), :], sems.at[query]
            )
            for i, source in enumerate((first_hbm, second_hbm))
        ]

    @pl.when(step == 0)
    def _():
        stats = pltpu.make_async_copy(second_hbm.at[:, pl.ds(half, EXTRA), :], sent, sems.at[query_count])
        stats.start()
        for query in range(query_count):
            for k in range(top_count):
                for copy in fetch(query * top_count + k, query // text.shape[0]):
                    copy.start()
        stats.wait()
        parts = sent[...].astype(jnp.float32)
        joined = jnp.sum(jnp.where(row_of(parts.shape, 1) < 3, parts, 0.0), axis=1)
        joined = pltpu.roll(joined, lax.rem(LANES - place[0] * query_count, LANES), 1)
        exact[...] = joined
        peak = jnp.max(joined, axis=0, keepdims=True)
        scaled = jnp.exp(joined - peak) * pltpu.roll(joined, LANES - query_count, 1)
        total = jnp.sum(scaled, axis=0, keepdims=True)
        total = jnp.where(row_of(total.shape, 1) < query_count, total, 1.0)
        normalizers[...] = jnp.broadcast_to(peak + jnp.log(total), normalizers.shape)

    per_step = text.shape[0]
    for i in range(per_step):
        query = step * per_step + i
        picked = jnp.concatenate(
            [exact[pl.ds(shards[query * top_count + k], 1), :] for k in range(top_count)], axis=0
        )
        lane = row_of(picked.shape, 1)
        candidate = jnp.sum(jnp.where(lane == 2 * query_count + query, picked, 0.0), axis=1, keepdims=True)
        normalizer = jnp.sum(jnp.where(lane[:1] == query, normalizers[:1, :], 0.0), axis=1, keepdims=True)
        result = candidate - normalizer + shift
        result = jnp.sum(jnp.where(lane == row_of(picked.shape, 0), result, 0.0), axis=0, keepdims=True)
        found[pl.ds(query, 1), :] = result[:, :top_count]

    entries = per_step * top_count
    for k in range(entries):
        for copy in fetch(step * entries + k, step):
            copy.wait()
    for k in range(entries):
        for j in range(body // rows):
            gathered[k * rows : (k + 1) * rows, j * LANES : (j + 1) * LANES] = back[
                step * entries + k, j * rows : (j + 1) * rows, :
            ]
    mixed = jnp.dot(gathered[...], w_out[...], preferred_element_type=jnp.float32)
    width = mixed.shape[1]
    summed = mixed.reshape(per_step, top_count, rows, width) + text[...].astype(jnp.float32).reshape(per_step, 1, rows, width)
    mean = jnp.mean(summed, axis=-1, keepdims=True)
    centred = summed - mean
    variance = jnp.mean(centred * centred, axis=-1, keepdims=True)
    normed = centred * lax.rsqrt(variance + EPSILON) * gain[...].reshape(1, 1, 1, width)
    out[...] = normed.astype(jnp.bfloat16)


def finish(shards, place, first, second, text, w_out, gain, top_count, shift):
    query_count, rows, width = text.shape
    per_step = 2
    full = lambda a: pl.BlockSpec(a.shape, lambda i, *_: (0,) * a.ndim)
    return pl.pallas_call(
        functools.partial(finish_kernel, top_count=top_count, query_count=query_count, shift=shift),
        grid_spec=pltpu.PrefetchScalarGridSpec(
            num_scalar_prefetch=2,
            grid=(query_count // per_step,),
            in_specs=[
                pl.BlockSpec(memory_space=pltpu.HBM),
                pl.BlockSpec(memory_space=pltpu.HBM),
                pl.BlockSpec((per_step, rows, width), lambda i, *_: (i, 0, 0)),
                full(w_out),
                full(gain),
            ],
            out_specs=[
                pl.BlockSpec((query_count, top_count), lambda i, *_: (0, 0)),
                pl.BlockSpec((per_step, top_count, rows, width), lambda i, *_: (i, 0, 0, 0)),
            ],
            scratch_shapes=[
                pltpu.VMEM((first.shape[0], LANES), jnp.float32),
                pltpu.VMEM((EXTRA, LANES), jnp.float32),
                pltpu.VMEM((per_step * top_count * rows, width), jnp.bfloat16),
                pltpu.VMEM((query_count * top_count, 2 * first.shape[1], LANES), jnp.bfloat16),
                pltpu.VMEM((first.shape[0], EXTRA, LANES), jnp.bfloat16),
                pltpu.SemaphoreType.DMA((query_count + 1,)),
            ],
        ),
        out_shape=[
            jax.ShapeDtypeStruct((query_count, top_count), jnp.float32),
            jax.ShapeDtypeStruct((query_count, top_count, rows, width), jnp.bfloat16),
        ],
        compiler_params=pltpu.CompilerParams(vmem_limit_bytes=VMEM_LIMIT),
        cost_estimate=pl.CostEstimate(
            flops=2 * query_count * top_count * rows * width * width, bytes_accessed=7 << 20, transcendentals=0
        ),
        name="finish",
    )(shards, place, in_hbm(first), in_hbm(second), text, in_hbm(w_out), gain)


def project_rows(rows_in, weight):
    return jnp.einsum("spc,cd->spd", rows_in, weight, preferred_element_type=jnp.float32).astype(jnp.bfloat16)


def on_device(queries, slab, cand_ids, patches, text_states, w_query, w_key, w_value, w_out, norm_gain):
    shard_count = lax.axis_size("shard")
    shard_here = lax.axis_index("shard")
    core = lax.axis_index("rep")
    grid_y, depth, grid_x = GRIDS[shard_count]
    query_count = queries.shape[0]
    slab_count = slab.shape[0]
    top_count = cand_ids.shape[1]
    list_length = query_count * top_count
    text_count, model_width = text_states.shape[1:]
    head_size = model_width // HEADS
    here_x, here_z, here_y = shard_here % grid_x, shard_here // grid_x % depth, shard_here // (grid_x * depth)
    columns = [
        [(y * depth + z) * grid_x + x for z in range(depth)] for y in range(grid_y) for x in range(grid_x)
    ]
    planes = [
        [(y * depth + z) * grid_x + x for y in range(grid_y) for x in range(grid_x)] for z in range(depth)
    ]
    swap = [(0, 1), (1, 0)]
    w_query_other = lax.ppermute(w_query, "rep", swap)

    own_list = cand_ids.reshape(list_length)
    own_anchor = own_list // slab_count
    sent = project(
        cand_ids,
        text_states.reshape(query_count * text_count, model_width),
        queries,
        w_query,
        w_query_other,
        slab_count,
    )
    owners = lax.all_gather(sent, "shard", axis=0, tiled=True, axis_index_groups=columns)
    owners = owners.reshape(depth, sent.shape[0], model_width)
    at = jnp.stack([here_z, here_y, here_x])
    request = first_request(at, owners, grid_y, grid_x, text_count, top_count)
    got = lax.all_to_all(request, "shard", split_axis=0, concat_axis=0, tiled=True, axis_index_groups=planes)
    context_first, codes = first_serve(
        got, project_rows(patches, w_key), project_rows(patches, w_value), grid_x, depth, text_count, head_size
    )
    back_first = lax.all_to_all(context_first, "shard", split_axis=0, concat_axis=0, tiled=True)

    request = second_request(at, codes, owners, grid_y, grid_x, text_count, query_count, top_count)
    arrived = [request[0]]
    for k in range(1, grid_y * grid_x):
        moves = [
            (
                (y * depth + z) * grid_x + x,
                ((y + k // grid_x) % grid_y * depth + z) * grid_x + (x + k % grid_x) % grid_x,
            )
            for y in range(grid_y)
            for z in range(depth)
            for x in range(grid_x)
        ]
        arrived.append(lax.ppermute(request[k], "shard", moves))
    keys = project_rows(patches, lax.ppermute(w_key, "rep", swap))
    values = project_rows(patches, lax.ppermute(w_value, "rep", swap))
    w_out_other = lax.ppermute(w_out, "rep", swap)
    half = model_width // 2
    w_out_whole = jnp.where(
        core == 0,
        jnp.concatenate([w_out, w_out_other], axis=1),
        jnp.concatenate(
            [
                jnp.concatenate([w_out_other[half:], w_out[half:]], axis=1),
                jnp.concatenate([w_out_other[:half], w_out[:half]], axis=1),
            ],
            axis=0,
        ),
    )

    context_second = second_serve(
        at, codes, arrived, slab, keys, values, grid_y, grid_x, depth, text_count, query_count, top_count, head_size
    )
    back_second = lax.all_to_all(context_second, "shard", split_axis=0, concat_axis=0, tiled=True)

    place = ((here_y * grid_x + here_x) * depth + here_z) % (LANES // query_count)
    retrieval, attended = finish(
        own_anchor,
        place.reshape(1),
        back_first,
        back_second,
        text_states,
        w_out_whole,
        norm_gain.reshape(1, model_width),
        top_count,
        math.log(slab_count * shard_count),
    )
    return (retrieval, attended)


def solution(mesh):
    in_specs = (
        P(("shard", "rep"), None),
        P("shard", None),
        P(("shard", "rep"), None),
        P("shard", None, None),
        P(("shard", "rep"), None, None),
        P(None, "rep"),
        P(None, "rep"),
        P(None, "rep"),
        P(None, "rep"),
        P(),
    )
    out_specs = (P(("shard", "rep"), None), P(("shard", "rep"), None, None, None))
    return jax.shard_map(
        on_device, mesh=mesh, in_specs=in_specs, out_specs=out_specs, check_vma=False
    )
```

```python
import functools
import math

import jax
import jax.numpy as jnp
from jax import lax
from jax.experimental import pallas as pl
from jax.experimental.pallas import tpu as pltpu
from jax.sharding import PartitionSpec as P

HEADS = 12
SCALE = 100.0
EPSILON = 1e-06
LANES = 128
EXTRA = 8
UNROLL = 16
PAIR = 2
GRIDS = {128: (4, 8, 4), 8: (2, 2, 2)}
VMEM_LIMIT = 48 * 1024 * 1024


def row_of(shape, dim):
    return lax.broadcasted_iota(jnp.int32, shape, dim)


def split_source(source, grid_y, grid_x):
    if isinstance(source, int):
        return source // (grid_y * grid_x), source // grid_x % grid_y, source % grid_x
    return lax.div(source, grid_y * grid_x), lax.rem(lax.div(source, grid_x), grid_y), lax.rem(source, grid_x)


def owner_of(source, k, grid_y, grid_x, owned):
    in_pair, y, x = split_source(source, grid_y, grid_x)
    return (y * owned * PAIR + k * PAIR + in_pair) * grid_x + x


def in_hbm(array):
    return pltpu.with_memory_space_constraint(array, pltpu.HBM)


def project_kernel(ids, text, queries, w_own, w_other, out, *, slab_count):
    rows = text.shape[0]
    half = w_own.shape[1]
    count, width = queries.shape
    lane = row_of((EXTRA, LANES), 1)
    image = jnp.full((EXTRA, LANES), -1, jnp.int32)
    listed = image
    for entry in range(ids.shape[0] * ids.shape[1]):
        row = ids[entry // ids.shape[1], entry % ids.shape[1]]
        here = lane == lax.div(row, slab_count)
        image = jnp.where(here, lax.rem(row, slab_count), image)
        listed = jnp.where(here, entry, listed)
    pieces = [queries[...].astype(jnp.float32)]
    if count < EXTRA:
        pieces.append(jnp.zeros((EXTRA - count, width), jnp.float32))
    code = [image.astype(jnp.float32), listed.astype(jnp.float32)]
    code.append(jnp.zeros((EXTRA, width - 2 * LANES), jnp.float32))
    pieces.append(jnp.concatenate(code, axis=1))
    out[rows:, :] = jnp.concatenate(pieces, axis=0).astype(jnp.bfloat16)
    out[:rows, :half] = jnp.dot(text[...], w_own[...], preferred_element_type=jnp.float32).astype(jnp.bfloat16)
    out[:rows, half:] = jnp.dot(text[...], w_other[...], preferred_element_type=jnp.float32).astype(jnp.bfloat16)


def project(ids, text, queries, w_own, w_other, slab_count):
    width = w_own.shape[1] + w_other.shape[1]
    operands = [text, queries, w_own, w_other]
    return pl.pallas_call(
        functools.partial(project_kernel, slab_count=slab_count),
        grid_spec=pltpu.PrefetchScalarGridSpec(
            num_scalar_prefetch=1,
            grid=(1,),
            in_specs=[pl.BlockSpec(a.shape, lambda i, *_: (0, 0)) for a in operands],
            out_specs=pl.BlockSpec((text.shape[0] + 2 * EXTRA, width), lambda i, *_: (0, 0)),
        ),
        out_shape=jax.ShapeDtypeStruct((text.shape[0] + 2 * EXTRA, width), jnp.bfloat16),
        compiler_params=pltpu.CompilerParams(vmem_limit_bytes=VMEM_LIMIT),
        cost_estimate=pl.CostEstimate(
            flops=2 * text.shape[0] * text.shape[1] * width, bytes_accessed=2 << 20, transcendentals=0
        ),
        name="project",
    )(ids, in_hbm(text), in_hbm(queries), in_hbm(w_own), w_other)


def to_scalars(vectors, decoded, table, sem):
    decoded[...] = vectors
    copy = pltpu.make_async_copy(decoded, table, sem)
    copy.start()
    copy.wait()


def request_kernel(
    place, owners, out, decoded, table, shared, sem, *, grid_y, grid_x, rows, query_count, top_count
):
    step = pl.program_id(0)
    depth, height = owners.shape[:2]
    texts = height - 2 * EXTRA
    slot_rows = depth * rows
    shared_rows = shared.shape[0]
    tile_row = row_of((EXTRA, LANES), 0)

    @pl.when(step == 0)
    def _():
        found = [jnp.zeros((EXTRA, LANES), jnp.float32) for _ in range(2)]
        for z in range(depth):
            code = owners[z, texts + EXTRA :, :].astype(jnp.float32)
            found = [jnp.where(tile_row == z, code[:, i * LANES : (i + 1) * LANES], found[i]) for i in range(2)]
        to_scalars(jnp.concatenate(found, axis=0).astype(jnp.int32), decoded, table, sem)
        picked = [owners[z, texts : texts + EXTRA, :].astype(jnp.float32)[:query_count] for z in range(depth)]
        shared[...] = jnp.concatenate(picked, axis=0).astype(jnp.bfloat16)

    lane = row_of((EXTRA, LANES), 1)
    for i in range(out.shape[0]):
        target = step * out.shape[0] + i
        in_pair, y, x = split_source(target, grid_y, grid_x)
        shard = (y * depth * PAIR + place[0] + in_pair) * grid_x + x
        code = jnp.full((EXTRA, LANES), -1.0, jnp.float32)
        for z in range(depth):
            image, listed = table[z, shard], table[EXTRA + z, shard]
            first = lax.div(jnp.maximum(listed, 0), top_count) * rows
            out[i, z * rows : (z + 1) * rows, :] = owners[z, pl.ds(pl.multiple_of(first, rows), rows), :]
            code = jnp.where(lane == z, image.astype(jnp.float32), code)
            code = jnp.where(lane == EXTRA + z, listed.astype(jnp.float32), code)
        out[i, slot_rows : slot_rows + shared_rows, :] = shared[...]
        out[i, slot_rows + shared_rows :, :LANES] = code.astype(jnp.bfloat16)


def make_request(place, owners, grid_y, grid_x, rows, query_count, top_count):
    depth, height, width = owners.shape
    shared_rows = depth * query_count
    total = depth * rows + shared_rows + EXTRA
    targets = PAIR * grid_y * grid_x
    block = min(8, targets)
    return pl.pallas_call(
        functools.partial(
            request_kernel,
            grid_y=grid_y,
            grid_x=grid_x,
            rows=rows,
            query_count=query_count,
            top_count=top_count,
        ),
        grid_spec=pltpu.PrefetchScalarGridSpec(
            num_scalar_prefetch=1,
            grid=(targets // block,),
            in_specs=[pl.BlockSpec(owners.shape, lambda i, *_: (0, 0, 0))],
            out_specs=pl.BlockSpec((block, total, width), lambda i, *_: (i, 0, 0)),
            scratch_shapes=[
                pltpu.VMEM((2 * EXTRA, LANES), jnp.int32),
                pltpu.SMEM((2 * EXTRA, LANES), jnp.int32),
                pltpu.VMEM((shared_rows, width), jnp.bfloat16),
                pltpu.SemaphoreType.DMA,
            ],
        ),
        out_shape=pltpu.HBM((targets, total, width), jnp.bfloat16),
        compiler_params=pltpu.CompilerParams(vmem_limit_bytes=VMEM_LIMIT),
        cost_estimate=pl.CostEstimate(flops=1 << 20, bytes_accessed=6 << 20, transcendentals=0),
        name="request",
    )(place, in_hbm(owners))


def index_stats(query, slab, picked, logits):
    count = query.shape[0]
    tile = min(256, slab.shape[0])
    peak = None
    for t in range(slab.shape[0] // tile):
        part = SCALE * lax.dot_general(
            slab[t * tile : (t + 1) * tile, :], query, (((1,), (1,)), ((), ())), preferred_element_type=jnp.float32
        )
        logits[t * tile : (t + 1) * tile, :] = part
        top = jnp.max(part, axis=0, keepdims=True)
        peak = top if peak is None else jnp.maximum(peak, top)
    total = jnp.zeros_like(peak)
    for t in range(slab.shape[0] // tile):
        total = total + jnp.sum(jnp.exp(logits[t * tile : (t + 1) * tile, :] - peak), axis=0, keepdims=True)
    chosen = row_of((tile, count), 0) == picked
    candidate = jnp.sum(jnp.where(chosen, logits[:tile, :], 0.0), axis=0, keepdims=True)
    return peak, total, candidate


def split_rows(exact):
    tile_row = row_of((EXTRA, LANES), 0)
    exact = jnp.broadcast_to(exact, (EXTRA, LANES))
    high = exact.astype(jnp.bfloat16).astype(jnp.float32)
    left = exact - high
    middle = left.astype(jnp.bfloat16).astype(jnp.float32)
    parts = jnp.where(tile_row == 0, high, jnp.where(tile_row == 1, middle, left - middle))
    return jnp.where(tile_row < 3, parts, 0.0)


def serve_kernel(
    got_hbm, slab_hbm, keys_hbm, values_hbm, out_hbm,
    out, got, slab, keys, values, logits, decoded, table, listed, sems, *, grid_y, grid_x, depth, rows, query_count, top_count, head_size
):
    sources = got.shape[0]
    slots = sources * depth
    columns = keys.shape[2]
    slot_rows = depth * rows
    late = got.shape[1] - slot_rows
    copies = [
        pltpu.make_async_copy(source, target, sems.at[i])
        for i, (source, target) in enumerate(
            [
                (got_hbm.at[:, pl.ds(slot_rows, late), :], got.at[:, pl.ds(slot_rows, late), :]),
                (slab_hbm, slab),
                (got_hbm.at[:, pl.ds(0, slot_rows), :], got.at[:, pl.ds(0, slot_rows), :]),
                (keys_hbm, keys),
                (values_hbm, values),
            ]
        )
    ]
    for copy in copies:
        copy.start()
    shared_rows = depth * query_count
    body = columns // LANES * rows
    per_chunk = LANES // query_count
    lane = row_of((EXTRA, LANES), 1)
    tile_row = row_of((EXTRA, LANES), 0)

    copies[0].wait()
    found = [jnp.zeros((EXTRA, LANES), jnp.float32) for _ in range(-(-sources // EXTRA))]
    for source in range(sources):
        code = got[source, slot_rows + shared_rows :, :LANES].astype(jnp.float32)
        found[source // EXTRA] = jnp.where(tile_row == source % EXTRA, code, found[source // EXTRA])
    found = found[0] if len(found) == 1 else jnp.concatenate(found, axis=0)
    to_scalars(found.astype(jnp.int32), decoded, table, sems.at[5])

    count = 0
    chunks = [jnp.full((EXTRA, LANES), -1, jnp.int32) for _ in range(-(-slots // per_chunk))]
    for slot in range(slots):
        image, entry = table[slot // depth, slot % depth], table[slot // depth, EXTRA + slot % depth]
        query = lax.div(jnp.maximum(entry, 0), top_count)
        at = slot % per_chunk * query_count + query
        chunks[slot // per_chunk] = jnp.where(lane == at, image, chunks[slot // per_chunk])
        listed[count] = slot
        count = count + jnp.where(image >= 0, 1, 0)
    last = listed[jnp.maximum(count - 1, 0)]
    for g in range(UNROLL):
        listed[count + g] = last

    queries = jnp.concatenate([got[source, slot_rows : slot_rows + shared_rows, :] for source in range(sources)], axis=0)
    missing = len(chunks) * LANES - queries.shape[0]
    if missing:
        queries = jnp.concatenate([queries, jnp.zeros((missing, queries.shape[1]), queries.dtype)], axis=0)
    copies[1].wait()
    stats = index_stats(queries, slab, jnp.concatenate([chunk[:1] for chunk in chunks], axis=1), logits)
    for c in range(len(chunks)):
        tiles = [split_rows(stat[:, c * LANES : (c + 1) * LANES]) for stat in stats]
        tiles = [tiles[0], pltpu.roll(tiles[1], query_count, 1), pltpu.roll(tiles[2], 2 * query_count, 1)]
        for slot in range(c * per_chunk, min((c + 1) * per_chunk, slots)):
            source, z = slot // depth, slot % depth
            at = slot % per_chunk
            owner = owner_of(source, z, grid_y, grid_x, depth)
            place = lane // query_count
            tile = jnp.where(place == at, tiles[0], jnp.where(place == (at + 1) % per_chunk, tiles[1], tiles[2]))
            out[owner, body:, :] = tile.astype(jnp.bfloat16)

    stats_out = pltpu.make_async_copy(
        out.at[:, pl.ds(body, EXTRA), :], out_hbm.at[:, pl.ds(body, EXTRA), :], sems.at[6]
    )
    stats_out.start()

    def send(owner):
        return pltpu.make_async_copy(out.at[owner, pl.ds(0, body), :], out_hbm.at[owner, pl.ds(0, body), :], sems.at[7])

    copies[2].wait()
    copies[3].wait()
    copies[4].wait()
    spans = []
    at = 0
    while at < columns:
        width = min(2 * LANES, columns - at)
        lane_head = row_of((rows, width), 1) // head_size
        spans.append((at, width, [jnp.where(lane_head == h, 1.0, 0.0) for h in range(width // head_size)]))
        at += width

    def group(index, carry):
        chosen = [listed[index * UNROLL + g] for g in range(UNROLL)]
        places = [(lax.div(slot, depth), lax.rem(slot, depth)) for slot in chosen]
        images = [table[source, z] for source, z in places]
        owners = [owner_of(source, z, grid_y, grid_x, depth) for source, z in places]
        work = [(g, span) for g in range(UNROLL) for span in spans]
        scores = []
        for g, (at, width, masks) in work:
            source, z = places[g]
            query = got[source, pl.ds(pl.multiple_of(z * rows, rows), rows), at : at + width]
            spread = jnp.concatenate([query * mask.astype(query.dtype) for mask in masks], axis=0)
            scores.append(
                lax.dot_general(
                    spread,
                    keys[images[g], :, at : at + width],
                    (((1,), (1,)), ((), ())),
                    preferred_element_type=jnp.float32,
                )
            )
        scores = [score * head_size ** (-0.5) for score in scores]
        highest = [jnp.max(score, axis=-1, keepdims=True) for score in scores]
        powers = [jnp.exp(score - top) for score, top in zip(scores, highest)]
        totals = [jnp.sum(power, axis=-1, keepdims=True) for power in powers]
        weights = [(power / total).astype(jnp.bfloat16) for power, total in zip(powers, totals)]
        mixed = [
            jnp.dot(weight, values[images[g], :, at : at + width], preferred_element_type=jnp.float32)
            for weight, (g, (at, width, _)) in zip(weights, work)
        ]
        for mix, (g, (at, width, masks)) in zip(mixed, work):
            context = mix[:rows] * masks[0]
            for h in range(1, len(masks)):
                context = context + mix[h * rows : (h + 1) * rows] * masks[h]
            context = context.astype(jnp.bfloat16)
            for c in range(width // LANES):
                out[owners[g], (at // LANES + c) * rows : (at // LANES + c + 1) * rows, :] = context[
                    :, c * LANES : (c + 1) * LANES
                ]
        for owner in owners:
            send(owner).start()
        return carry

    def drain(index, carry):
        for _ in range(UNROLL):
            send(0).wait()
        return carry

    groups = lax.div(count + UNROLL - 1, UNROLL)
    lax.fori_loop(0, groups, group, 0)
    lax.fori_loop(0, groups, drain, 0)
    stats_out.wait()


def serve(got, slab, keys, values, grid_y, grid_x, depth, rows, query_count, top_count, head_size):
    sources = got.shape[0]
    slots = sources * depth
    body = keys.shape[2] // LANES * rows
    lanes = -(-slots * query_count // LANES) * LANES
    operands = [got, slab, keys, values]
    codes = (-(-sources // EXTRA) * EXTRA, LANES)
    return pl.pallas_call(
        functools.partial(
            serve_kernel,
            grid_y=grid_y,
            grid_x=grid_x,
            depth=depth,
            rows=rows,
            query_count=query_count,
            top_count=top_count,
            head_size=head_size,
        ),
        grid=(1,),
        in_specs=[pl.BlockSpec(memory_space=pltpu.HBM)] * 4,
        out_specs=pl.BlockSpec(memory_space=pltpu.HBM),
        scratch_shapes=[pltpu.VMEM((slots, body + EXTRA, LANES), jnp.bfloat16)]
        + [pltpu.VMEM(a.shape, a.dtype) for a in operands]
        + [
            pltpu.VMEM((slab.shape[0], lanes), jnp.float32),
            pltpu.VMEM(codes, jnp.int32),
            pltpu.SMEM(codes, jnp.int32),
            pltpu.SMEM((slots + UNROLL,), jnp.int32),
            pltpu.SemaphoreType.DMA((8,)),
        ],
        out_shape=pltpu.HBM((slots, body + EXTRA, LANES), jnp.bfloat16),
        compiler_params=pltpu.CompilerParams(vmem_limit_bytes=VMEM_LIMIT),
        cost_estimate=pl.CostEstimate(flops=8 << 30, bytes_accessed=14 << 20, transcendentals=2 << 20),
        name="serve",
    )(*[in_hbm(a) for a in operands])


def finish_kernel(
    shards, place, back_hbm, text, w_out, gain, found, out,
    exact, normalizers, gathered, back, sent, sems, *, top_count, query_count, shift
):
    step = pl.program_id(0)
    rows = text.shape[1]
    body = back.shape[1]

    def fetch(entry, query):
        return pltpu.make_async_copy(back_hbm.at[shards[entry], pl.ds(0, body), :], back.at[entry], sems.at[query])

    @pl.when(step == 0)
    def _():
        stats = pltpu.make_async_copy(back_hbm.at[:, pl.ds(body, EXTRA), :], sent, sems.at[query_count])
        stats.start()
        for query in range(query_count):
            for k in range(top_count):
                fetch(query * top_count + k, query // text.shape[0]).start()
        stats.wait()
        parts = sent[...].astype(jnp.float32)
        joined = jnp.sum(jnp.where(row_of(parts.shape, 1) < 3, parts, 0.0), axis=1)
        joined = pltpu.roll(joined, lax.rem(LANES - place[0] * query_count, LANES), 1)
        exact[...] = joined
        peak = jnp.max(joined, axis=0, keepdims=True)
        scaled = jnp.exp(joined - peak) * pltpu.roll(joined, LANES - query_count, 1)
        total = jnp.sum(scaled, axis=0, keepdims=True)
        total = jnp.where(row_of(total.shape, 1) < query_count, total, 1.0)
        normalizers[...] = jnp.broadcast_to(peak + jnp.log(total), normalizers.shape)

    per_step = text.shape[0]
    for i in range(per_step):
        query = step * per_step + i
        picked = jnp.concatenate(
            [exact[pl.ds(shards[query * top_count + k], 1), :] for k in range(top_count)], axis=0
        )
        lane = row_of(picked.shape, 1)
        candidate = jnp.sum(jnp.where(lane == 2 * query_count + query, picked, 0.0), axis=1, keepdims=True)
        normalizer = jnp.sum(jnp.where(lane[:1] == query, normalizers[:1, :], 0.0), axis=1, keepdims=True)
        result = candidate - normalizer + shift
        result = jnp.sum(jnp.where(lane == row_of(picked.shape, 0), result, 0.0), axis=0, keepdims=True)
        found[pl.ds(query, 1), :] = result[:, :top_count]

    entries = per_step * top_count
    for k in range(entries):
        fetch(step * entries + k, step).wait()
    for k in range(entries):
        for j in range(body // rows):
            gathered[k * rows : (k + 1) * rows, j * LANES : (j + 1) * LANES] = back[
                step * entries + k, j * rows : (j + 1) * rows, :
            ]
    mixed = jnp.dot(gathered[...], w_out[...], preferred_element_type=jnp.float32)
    width = mixed.shape[1]
    summed = mixed.reshape(per_step, top_count, rows, width) + text[...].astype(jnp.float32).reshape(per_step, 1, rows, width)
    mean = jnp.mean(summed, axis=-1, keepdims=True)
    centred = summed - mean
    variance = jnp.mean(centred * centred, axis=-1, keepdims=True)
    normed = centred * lax.rsqrt(variance + EPSILON) * gain[...].reshape(1, 1, 1, width)
    out[...] = normed.astype(jnp.bfloat16)


def finish(shards, place, back, text, w_out, gain, top_count, shift):
    query_count, rows, width = text.shape
    per_step = 2
    full = lambda a: pl.BlockSpec(a.shape, lambda i, *_: (0,) * a.ndim)
    return pl.pallas_call(
        functools.partial(finish_kernel, top_count=top_count, query_count=query_count, shift=shift),
        grid_spec=pltpu.PrefetchScalarGridSpec(
            num_scalar_prefetch=2,
            grid=(query_count // per_step,),
            in_specs=[
                pl.BlockSpec(memory_space=pltpu.HBM),
                pl.BlockSpec((per_step, rows, width), lambda i, *_: (i, 0, 0)),
                full(w_out),
                full(gain),
            ],
            out_specs=[
                pl.BlockSpec((query_count, top_count), lambda i, *_: (0, 0)),
                pl.BlockSpec((per_step, top_count, rows, width), lambda i, *_: (i, 0, 0, 0)),
            ],
            scratch_shapes=[
                pltpu.VMEM((back.shape[0], LANES), jnp.float32),
                pltpu.VMEM((EXTRA, LANES), jnp.float32),
                pltpu.VMEM((per_step * top_count * rows, width), jnp.bfloat16),
                pltpu.VMEM((query_count * top_count, back.shape[1] - EXTRA, LANES), jnp.bfloat16),
                pltpu.VMEM((back.shape[0], EXTRA, LANES), jnp.bfloat16),
                pltpu.SemaphoreType.DMA((query_count + 1,)),
            ],
        ),
        out_shape=[
            jax.ShapeDtypeStruct((query_count, top_count), jnp.float32),
            jax.ShapeDtypeStruct((query_count, top_count, rows, width), jnp.bfloat16),
        ],
        compiler_params=pltpu.CompilerParams(vmem_limit_bytes=VMEM_LIMIT),
        cost_estimate=pl.CostEstimate(
            flops=2 * query_count * top_count * rows * width * width, bytes_accessed=7 << 20, transcendentals=0
        ),
        name="finish",
    )(shards, place, in_hbm(back), text, in_hbm(w_out), gain)


def project_rows(rows_in, weight):
    return jnp.einsum("spc,cd->spd", rows_in, weight, preferred_element_type=jnp.float32).astype(jnp.bfloat16)


def on_device(queries, slab, cand_ids, patches, text_states, w_query, w_key, w_value, w_out, norm_gain):
    shard_count = lax.axis_size("shard")
    shard_here = lax.axis_index("shard")
    core = lax.axis_index("rep")
    grid_y, depth, grid_x = GRIDS[shard_count]
    query_count = queries.shape[0]
    slab_count = slab.shape[0]
    top_count = cand_ids.shape[1]
    list_length = query_count * top_count
    text_count, model_width = text_states.shape[1:]
    head_size = model_width // HEADS
    here_x, here_z, here_y = shard_here % grid_x, shard_here // grid_x % depth, shard_here // (grid_x * depth)
    owned = depth // PAIR
    columns = [
        [(y * depth + k * PAIR + in_pair) * grid_x + x for k in range(owned)]
        for y in range(grid_y)
        for x in range(grid_x)
        for in_pair in range(PAIR)
    ]
    pairs = [
        [
            (y * depth + k * PAIR + in_pair) * grid_x + x
            for in_pair in range(PAIR)
            for y in range(grid_y)
            for x in range(grid_x)
        ]
        for k in range(owned)
    ]
    swap = [(0, 1), (1, 0)]
    w_query_other = lax.ppermute(w_query, "rep", swap)

    own_list = cand_ids.reshape(list_length)
    own_anchor = own_list // slab_count
    sent = project(
        cand_ids,
        text_states.reshape(query_count * text_count, model_width),
        queries,
        w_query,
        w_query_other,
        slab_count,
    )
    owners = lax.all_gather(sent, "shard", axis=0, tiled=True, axis_index_groups=columns)
    request = make_request(
        (here_z // PAIR * PAIR).reshape(1),
        owners.reshape(owned, sent.shape[0], model_width),
        grid_y,
        grid_x,
        text_count,
        query_count,
        top_count,
    )
    got = lax.all_to_all(request, "shard", split_axis=0, concat_axis=0, tiled=True, axis_index_groups=pairs)

    keys = project_rows(patches, jnp.concatenate([w_key, lax.ppermute(w_key, "rep", swap)], axis=1))
    values = project_rows(patches, jnp.concatenate([w_value, lax.ppermute(w_value, "rep", swap)], axis=1))
    w_out_other = lax.ppermute(w_out, "rep", swap)
    half = model_width // 2
    w_out_whole = jnp.where(
        core == 0,
        jnp.concatenate([w_out, w_out_other], axis=1),
        jnp.concatenate(
            [
                jnp.concatenate([w_out_other[half:], w_out[half:]], axis=1),
                jnp.concatenate([w_out_other[:half], w_out[:half]], axis=1),
            ],
            axis=0,
        ),
    )

    context = serve(
        got, slab, keys, values, grid_y, grid_x, owned, text_count, query_count, top_count, head_size
    )
    back = lax.all_to_all(context, "shard", split_axis=0, concat_axis=0, tiled=True)

    source = (here_z % PAIR * grid_y + here_y) * grid_x + here_x
    place = (source * owned + here_z // PAIR) % (LANES // query_count)
    retrieval, attended = finish(
        own_anchor,
        place.reshape(1),
        back,
        text_states,
        w_out_whole,
        norm_gain.reshape(1, model_width),
        top_count,
        math.log(slab_count * shard_count),
    )
    return (retrieval, attended)


def solution(mesh):
    in_specs = (
        P(("shard", "rep"), None),
        P("shard", None),
        P(("shard", "rep"), None),
        P("shard", None, None),
        P(("shard", "rep"), None, None),
        P(None, "rep"),
        P(None, "rep"),
        P(None, "rep"),
        P(None, "rep"),
        P(),
    )
    out_specs = (P(("shard", "rep"), None), P(("shard", "rep"), None, None, None))
    return jax.shard_map(
        on_device, mesh=mesh, in_specs=in_specs, out_specs=out_specs, check_vma=False
    )
```

```python
import functools
import math

import jax
import jax.numpy as jnp
from jax import lax
from jax.experimental import pallas as pl
from jax.experimental.pallas import tpu as pltpu
from jax.sharding import PartitionSpec as P

HEADS = 12
SCALE = 100.0
EPSILON = 1e-06
LANES = 128
EXTRA = 8
UNROLL = 16
PAIR = 2
GRIDS = {128: (4, 8, 4), 8: (2, 2, 2)}
VMEM_LIMIT = 48 * 1024 * 1024


def row_of(shape, dim):
    return lax.broadcasted_iota(jnp.int32, shape, dim)


def split_source(source, grid_y, grid_x):
    if isinstance(source, int):
        return source // (grid_y * grid_x), source // grid_x % grid_y, source % grid_x
    return lax.div(source, grid_y * grid_x), lax.rem(lax.div(source, grid_x), grid_y), lax.rem(source, grid_x)


def owner_of(source, k, grid_y, grid_x, owned):
    in_pair, y, x = split_source(source, grid_y, grid_x)
    return (y * owned * PAIR + k * PAIR + in_pair) * grid_x + x


def in_hbm(array):
    return pltpu.with_memory_space_constraint(array, pltpu.HBM)


def pack_kernel(ids, text, queries, out, *, slab_count):
    rows = text.shape[0]
    count, width = queries.shape
    lane = row_of((EXTRA, LANES), 1)
    image = jnp.full((EXTRA, LANES), -1, jnp.int32)
    listed = image
    for entry in range(ids.shape[0] * ids.shape[1]):
        row = ids[entry // ids.shape[1], entry % ids.shape[1]]
        here = lane == lax.div(row, slab_count)
        image = jnp.where(here, lax.rem(row, slab_count), image)
        listed = jnp.where(here, entry, listed)
    pieces = [queries[...].astype(jnp.float32)]
    if count < EXTRA:
        pieces.append(jnp.zeros((EXTRA - count, width), jnp.float32))
    code = [image.astype(jnp.float32), listed.astype(jnp.float32)]
    code.append(jnp.zeros((EXTRA, width - 2 * LANES), jnp.float32))
    pieces.append(jnp.concatenate(code, axis=1))
    out[:rows, :] = text[...]
    out[rows:, :] = jnp.concatenate(pieces, axis=0).astype(jnp.bfloat16)


def pack(ids, text, queries, slab_count):
    rows, width = text.shape
    return pl.pallas_call(
        functools.partial(pack_kernel, slab_count=slab_count),
        grid=(1,),
        in_specs=[pl.BlockSpec(memory_space=pltpu.SMEM)]
        + [pl.BlockSpec(a.shape, lambda i: (0, 0)) for a in (text, queries)],
        out_specs=pl.BlockSpec((rows + 2 * EXTRA, width), lambda i: (0, 0)),
        out_shape=jax.ShapeDtypeStruct((rows + 2 * EXTRA, width), jnp.bfloat16),
        compiler_params=pltpu.CompilerParams(vmem_limit_bytes=VMEM_LIMIT),
        cost_estimate=pl.CostEstimate(flops=1 << 20, bytes_accessed=1 << 18, transcendentals=0),
        name="pack",
    )(ids, in_hbm(text), in_hbm(queries))


def to_scalars(vectors, decoded, table, sem):
    decoded[...] = vectors
    copy = pltpu.make_async_copy(decoded, table, sem)
    copy.start()
    copy.wait()


def request_kernel(
    place, owners, w_own, w_other, out, decoded, table, projected, shared, sem,
    *, grid_y, grid_x, rows, query_count, top_count
):
    step = pl.program_id(0)
    depth, height, width = owners.shape
    texts = height - 2 * EXTRA
    body = projected.shape[1]
    tile_row = row_of((EXTRA, LANES), 0)

    @pl.when(step == 0)
    def _():
        found = [jnp.zeros((EXTRA, LANES), jnp.float32) for _ in range(2)]
        for z in range(depth):
            code = owners[z, texts + EXTRA :, : 2 * LANES].astype(jnp.float32)
            found = [jnp.where(tile_row == z, code[:, i * LANES : (i + 1) * LANES], found[i]) for i in range(2)]
        decoded[...] = jnp.concatenate(found, axis=0).astype(jnp.int32)
        copy = pltpu.make_async_copy(decoded, table, sem)
        copy.start()
        states = owners[:, :texts, :].reshape(depth * texts, width)
        at = 0
        for weight in (w_own, w_other):
            half = jnp.dot(states, weight[...], preferred_element_type=jnp.float32).astype(jnp.bfloat16)
            for c in range(half.shape[1] // LANES):
                for t in range(depth * query_count):
                    projected[t, at : at + rows, :] = half[t * rows : (t + 1) * rows, c * LANES : (c + 1) * LANES]
                at += rows
        picked = [owners[z, texts : texts + EXTRA, :].astype(jnp.float32)[:query_count] for z in range(depth)]
        picked = jnp.concatenate(picked, axis=0).astype(jnp.bfloat16)
        for c in range(width // LANES):
            size = depth * query_count
            shared[c * size : (c + 1) * size, :] = picked[:, c * LANES : (c + 1) * LANES]
        copy.wait()

    lane = row_of((EXTRA, LANES), 1)
    for i in range(out.shape[0]):
        target = step * out.shape[0] + i
        in_pair, y, x = split_source(target, grid_y, grid_x)
        shard = (y * depth * PAIR + place[0] + in_pair) * grid_x + x
        code = jnp.full((EXTRA, LANES), -1.0, jnp.float32)
        for z in range(depth):
            image, listed = table[z, shard], table[EXTRA + z, shard]
            query = lax.div(jnp.maximum(listed, 0), top_count)
            out[i, z * body : (z + 1) * body, :] = projected[z * query_count + query]
            code = jnp.where(lane == z, image.astype(jnp.float32), code)
            code = jnp.where(lane == EXTRA + z, listed.astype(jnp.float32), code)
        out[i, depth * body : depth * body + shared.shape[0], :] = shared[...]
        out[i, depth * body + shared.shape[0] :, :] = code.astype(jnp.bfloat16)


def make_request(place, owners, w_own, w_other, grid_y, grid_x, rows, query_count, top_count):
    depth, height, width = owners.shape
    body = width // LANES * rows
    shared_rows = depth * query_count * (width // LANES)
    total = depth * body + shared_rows + EXTRA
    targets = PAIR * grid_y * grid_x
    block = min(8, targets)
    whole = lambda a: pl.BlockSpec(a.shape, lambda i, *_: (0,) * a.ndim)
    return pl.pallas_call(
        functools.partial(
            request_kernel,
            grid_y=grid_y,
            grid_x=grid_x,
            rows=rows,
            query_count=query_count,
            top_count=top_count,
        ),
        grid_spec=pltpu.PrefetchScalarGridSpec(
            num_scalar_prefetch=1,
            grid=(targets // block,),
            in_specs=[whole(owners), whole(w_own), whole(w_other)],
            out_specs=pl.BlockSpec((block, total, LANES), lambda i, *_: (i, 0, 0)),
            scratch_shapes=[
                pltpu.VMEM((2 * EXTRA, LANES), jnp.int32),
                pltpu.SMEM((2 * EXTRA, LANES), jnp.int32),
                pltpu.VMEM((depth * query_count, body, LANES), jnp.bfloat16),
                pltpu.VMEM((shared_rows, LANES), jnp.bfloat16),
                pltpu.SemaphoreType.DMA,
            ],
        ),
        out_shape=pltpu.HBM((targets, total, LANES), jnp.bfloat16),
        compiler_params=pltpu.CompilerParams(vmem_limit_bytes=VMEM_LIMIT),
        cost_estimate=pl.CostEstimate(flops=1 << 29, bytes_accessed=6 << 20, transcendentals=0),
        name="request",
    )(place, in_hbm(owners), in_hbm(w_own), in_hbm(w_other))


def index_stats(query, slab, picked, logits):
    count = query.shape[0]
    tile = min(256, slab.shape[0])
    peak = None
    for t in range(slab.shape[0] // tile):
        part = SCALE * lax.dot_general(
            slab[t * tile : (t + 1) * tile, :], query, (((1,), (1,)), ((), ())), preferred_element_type=jnp.float32
        )
        logits[t * tile : (t + 1) * tile, :] = part
        top = jnp.max(part, axis=0, keepdims=True)
        peak = top if peak is None else jnp.maximum(peak, top)
    total = jnp.zeros_like(peak)
    for t in range(slab.shape[0] // tile):
        total = total + jnp.sum(jnp.exp(logits[t * tile : (t + 1) * tile, :] - peak), axis=0, keepdims=True)
    chosen = row_of((tile, count), 0) == picked
    candidate = jnp.sum(jnp.where(chosen, logits[:tile, :], 0.0), axis=0, keepdims=True)
    return peak, total, candidate


def split_rows(exact):
    tile_row = row_of((EXTRA, LANES), 0)
    exact = jnp.broadcast_to(exact, (EXTRA, LANES))
    high = exact.astype(jnp.bfloat16).astype(jnp.float32)
    left = exact - high
    middle = left.astype(jnp.bfloat16).astype(jnp.float32)
    parts = jnp.where(tile_row == 0, high, jnp.where(tile_row == 1, middle, left - middle))
    return jnp.where(tile_row < 3, parts, 0.0)


def serve_kernel(
    got_hbm, slab_hbm, keys_hbm, values_hbm, out_hbm,
    out, got, slab, keys, values, logits, decoded, table, listed, sems, *, grid_y, grid_x, depth, rows, query_count, top_count, head_size
):
    sources = got.shape[0]
    slots = sources * depth
    columns = keys.shape[2]
    body = columns // LANES * rows
    slot_rows = depth * body
    late = got.shape[1] - slot_rows
    copies = [
        pltpu.make_async_copy(source, target, sems.at[i])
        for i, (source, target) in enumerate(
            [
                (got_hbm.at[:, pl.ds(slot_rows, late), :], got.at[:, pl.ds(slot_rows, late), :]),
                (slab_hbm, slab),
                (got_hbm.at[:, pl.ds(0, slot_rows), :], got.at[:, pl.ds(0, slot_rows), :]),
                (keys_hbm, keys),
                (values_hbm, values),
            ]
        )
    ]
    for copy in copies:
        copy.start()
    size = depth * query_count
    shared_rows = size * (columns // LANES)
    per_chunk = LANES // query_count
    lane = row_of((EXTRA, LANES), 1)
    tile_row = row_of((EXTRA, LANES), 0)

    copies[0].wait()
    found = [jnp.zeros((EXTRA, LANES), jnp.float32) for _ in range(-(-sources // EXTRA))]
    for source in range(sources):
        code = got[source, slot_rows + shared_rows :, :LANES].astype(jnp.float32)
        found[source // EXTRA] = jnp.where(tile_row == source % EXTRA, code, found[source // EXTRA])
    found = found[0] if len(found) == 1 else jnp.concatenate(found, axis=0)
    to_scalars(found.astype(jnp.int32), decoded, table, sems.at[5])

    count = 0
    chunks = [jnp.full((EXTRA, LANES), -1, jnp.int32) for _ in range(-(-slots // per_chunk))]
    for slot in range(slots):
        image, entry = table[slot // depth, slot % depth], table[slot // depth, EXTRA + slot % depth]
        query = lax.div(jnp.maximum(entry, 0), top_count)
        at = slot % per_chunk * query_count + query
        chunks[slot // per_chunk] = jnp.where(lane == at, image, chunks[slot // per_chunk])
        listed[count] = slot
        count = count + jnp.where(image >= 0, 1, 0)
    last = listed[jnp.maximum(count - 1, 0)]
    for g in range(UNROLL):
        listed[count + g] = last

    queries = jnp.concatenate(
        [
            jnp.concatenate(
                [
                    got[source, slot_rows + c * size : slot_rows + (c + 1) * size, :]
                    for c in range(columns // LANES)
                ],
                axis=1,
            )
            for source in range(sources)
        ],
        axis=0,
    )
    missing = len(chunks) * LANES - queries.shape[0]
    if missing:
        queries = jnp.concatenate([queries, jnp.zeros((missing, queries.shape[1]), queries.dtype)], axis=0)
    copies[1].wait()
    stats = index_stats(queries, slab, jnp.concatenate([chunk[:1] for chunk in chunks], axis=1), logits)
    for c in range(len(chunks)):
        tiles = [split_rows(stat[:, c * LANES : (c + 1) * LANES]) for stat in stats]
        tiles = [tiles[0], pltpu.roll(tiles[1], query_count, 1), pltpu.roll(tiles[2], 2 * query_count, 1)]
        for slot in range(c * per_chunk, min((c + 1) * per_chunk, slots)):
            source, z = slot // depth, slot % depth
            at = slot % per_chunk
            owner = owner_of(source, z, grid_y, grid_x, depth)
            place = lane // query_count
            tile = jnp.where(place == at, tiles[0], jnp.where(place == (at + 1) % per_chunk, tiles[1], tiles[2]))
            out[owner, body:, :] = tile.astype(jnp.bfloat16)

    stats_out = pltpu.make_async_copy(
        out.at[:, pl.ds(body, EXTRA), :], out_hbm.at[:, pl.ds(body, EXTRA), :], sems.at[6]
    )
    stats_out.start()

    def send(owner):
        return pltpu.make_async_copy(out.at[owner, pl.ds(0, body), :], out_hbm.at[owner, pl.ds(0, body), :], sems.at[7])

    copies[2].wait()
    copies[3].wait()
    copies[4].wait()
    spans = []
    at = 0
    while at < columns:
        width = min(2 * LANES, columns - at)
        lane_head = row_of((rows, width), 1) // head_size
        spans.append((at, width, [jnp.where(lane_head == h, 1.0, 0.0) for h in range(width // head_size)]))
        at += width

    def group(index, carry):
        chosen = [listed[index * UNROLL + g] for g in range(UNROLL)]
        places = [(lax.div(slot, depth), lax.rem(slot, depth)) for slot in chosen]
        images = [table[source, z] for source, z in places]
        owners = [owner_of(source, z, grid_y, grid_x, depth) for source, z in places]
        work = [(g, span) for g in range(UNROLL) for span in spans]
        scores = []
        for g, (at, width, masks) in work:
            source, z = places[g]
            pieces = [
                got[source, pl.ds(pl.multiple_of(z * body + c * rows, rows), rows), :]
                for c in range(at // LANES, (at + width) // LANES)
            ]
            query = pieces[0] if len(pieces) == 1 else jnp.concatenate(pieces, axis=1)
            spread = jnp.concatenate([query * mask.astype(query.dtype) for mask in masks], axis=0)
            scores.append(
                lax.dot_general(
                    spread,
                    keys[images[g], :, at : at + width],
                    (((1,), (1,)), ((), ())),
                    preferred_element_type=jnp.float32,
                )
            )
        scores = [score * head_size ** (-0.5) for score in scores]
        highest = [jnp.max(score, axis=-1, keepdims=True) for score in scores]
        powers = [jnp.exp(score - top) for score, top in zip(scores, highest)]
        totals = [jnp.sum(power, axis=-1, keepdims=True) for power in powers]
        weights = [(power / total).astype(jnp.bfloat16) for power, total in zip(powers, totals)]
        mixed = [
            jnp.dot(weight, values[images[g], :, at : at + width], preferred_element_type=jnp.float32)
            for weight, (g, (at, width, _)) in zip(weights, work)
        ]
        for mix, (g, (at, width, masks)) in zip(mixed, work):
            context = mix[:rows] * masks[0]
            for h in range(1, len(masks)):
                context = context + mix[h * rows : (h + 1) * rows] * masks[h]
            context = context.astype(jnp.bfloat16)
            for c in range(width // LANES):
                out[owners[g], (at // LANES + c) * rows : (at // LANES + c + 1) * rows, :] = context[
                    :, c * LANES : (c + 1) * LANES
                ]
        for owner in owners:
            send(owner).start()
        return carry

    def drain(index, carry):
        for _ in range(UNROLL):
            send(0).wait()
        return carry

    groups = lax.div(count + UNROLL - 1, UNROLL)
    lax.fori_loop(0, groups, group, 0)
    lax.fori_loop(0, groups, drain, 0)
    stats_out.wait()


def serve(got, slab, keys, values, grid_y, grid_x, depth, rows, query_count, top_count, head_size):
    sources = got.shape[0]
    slots = sources * depth
    body = keys.shape[2] // LANES * rows
    lanes = -(-slots * query_count // LANES) * LANES
    operands = [got, slab, keys, values]
    codes = (-(-sources // EXTRA) * EXTRA, LANES)
    return pl.pallas_call(
        functools.partial(
            serve_kernel,
            grid_y=grid_y,
            grid_x=grid_x,
            depth=depth,
            rows=rows,
            query_count=query_count,
            top_count=top_count,
            head_size=head_size,
        ),
        grid=(1,),
        in_specs=[pl.BlockSpec(memory_space=pltpu.HBM)] * 4,
        out_specs=pl.BlockSpec(memory_space=pltpu.HBM),
        scratch_shapes=[pltpu.VMEM((slots, body + EXTRA, LANES), jnp.bfloat16)]
        + [pltpu.VMEM(a.shape, a.dtype) for a in operands]
        + [
            pltpu.VMEM((slab.shape[0], lanes), jnp.float32),
            pltpu.VMEM(codes, jnp.int32),
            pltpu.SMEM(codes, jnp.int32),
            pltpu.SMEM((slots + UNROLL,), jnp.int32),
            pltpu.SemaphoreType.DMA((8,)),
        ],
        out_shape=pltpu.HBM((slots, body + EXTRA, LANES), jnp.bfloat16),
        compiler_params=pltpu.CompilerParams(vmem_limit_bytes=VMEM_LIMIT),
        cost_estimate=pl.CostEstimate(flops=8 << 30, bytes_accessed=14 << 20, transcendentals=2 << 20),
        name="serve",
    )(*[in_hbm(a) for a in operands])


def finish_kernel(
    shards, place, back_hbm, text_hbm, w_out_hbm, gain_hbm, found, out_hbm,
    exact, gathered, back, sent, text, w_out, gain, out, sems, *, top_count, query_count, chunks, shift
):
    rows, width = text.shape[1:]
    body = back.shape[1]
    entries = query_count * top_count // chunks
    queries = query_count // chunks

    def fetch(entry, chunk):
        return pltpu.make_async_copy(back_hbm.at[shards[entry], pl.ds(0, body), :], back.at[entry], sems.at[chunk])

    loads = [
        pltpu.make_async_copy(source, target, sems.at[chunks + i])
        for i, (source, target) in enumerate(
            [
                (back_hbm.at[:, pl.ds(body, EXTRA), :], sent),
                (w_out_hbm, w_out),
                (text_hbm, text),
                (gain_hbm, gain),
            ]
        )
    ]
    for load in loads:
        load.start()
    for chunk in range(chunks):
        for entry in range(chunk * entries, (chunk + 1) * entries):
            fetch(entry, chunk).start()

    loads[0].wait()
    parts = sent[...].astype(jnp.float32)
    joined = jnp.sum(jnp.where(row_of(parts.shape, 1) < 3, parts, 0.0), axis=1)
    joined = pltpu.roll(joined, lax.rem(LANES - place[0] * query_count, LANES), 1)
    exact[...] = joined
    peak = jnp.max(joined, axis=0, keepdims=True)
    scaled = jnp.exp(joined - peak) * pltpu.roll(joined, LANES - query_count, 1)
    total = jnp.sum(scaled, axis=0, keepdims=True)
    total = jnp.where(row_of(total.shape, 1) < query_count, total, 1.0)
    normalizers = peak + jnp.log(total)
    for query in range(query_count):
        picked = jnp.concatenate([exact[pl.ds(shards[query * top_count + k], 1), :] for k in range(top_count)], axis=0)
        lane = row_of(picked.shape, 1)
        candidate = jnp.sum(jnp.where(lane == 2 * query_count + query, picked, 0.0), axis=1, keepdims=True)
        result = candidate - normalizers[:, query : query + 1] + shift
        result = jnp.sum(jnp.where(lane == row_of(picked.shape, 0), result, 0.0), axis=0, keepdims=True)
        found[query : query + 1, :] = result[:, :top_count]

    for load in loads[1:]:
        load.wait()
    stores = []
    for chunk in range(chunks):
        first = chunk * queries
        for entry in range(chunk * entries, (chunk + 1) * entries):
            fetch(entry, chunk).wait()
        for k in range(entries):
            for j in range(body // rows):
                gathered[chunk, k * rows : (k + 1) * rows, j * LANES : (j + 1) * LANES] = back[
                    chunk * entries + k, j * rows : (j + 1) * rows, :
                ]
        mixed = jnp.dot(gathered[chunk], w_out[...], preferred_element_type=jnp.float32)
        states = text[first : first + queries].astype(jnp.float32).reshape(queries, 1, rows, width)
        summed = mixed.reshape(queries, top_count, rows, width) + states
        mean = jnp.mean(summed, axis=-1, keepdims=True)
        centred = summed - mean
        variance = jnp.mean(centred * centred, axis=-1, keepdims=True)
        normed = centred * lax.rsqrt(variance + EPSILON) * gain[...].reshape(1, 1, 1, width)
        out[first : first + queries] = normed.astype(jnp.bfloat16)
        store = pltpu.make_async_copy(
            out.at[pl.ds(first, queries)], out_hbm.at[pl.ds(first, queries)], sems.at[chunks + 4 + chunk]
        )
        store.start()
        stores.append(store)
    for store in stores:
        store.wait()


def finish(shards, place, back, text, w_out, gain, top_count, shift):
    query_count, rows, width = text.shape
    chunks = 2
    body = back.shape[1] - EXTRA
    entries = query_count * top_count
    return pl.pallas_call(
        functools.partial(finish_kernel, top_count=top_count, query_count=query_count, chunks=chunks, shift=shift),
        grid_spec=pltpu.PrefetchScalarGridSpec(
            num_scalar_prefetch=2,
            grid=(1,),
            in_specs=[pl.BlockSpec(memory_space=pltpu.HBM)] * 4,
            out_specs=[
                pl.BlockSpec((query_count, top_count), lambda i, *_: (0, 0)),
                pl.BlockSpec(memory_space=pltpu.HBM),
            ],
            scratch_shapes=[
                pltpu.VMEM((back.shape[0], LANES), jnp.float32),
                pltpu.VMEM((chunks, entries // chunks * rows, width), jnp.bfloat16),
                pltpu.VMEM((entries, body, LANES), jnp.bfloat16),
                pltpu.VMEM((back.shape[0], EXTRA, LANES), jnp.bfloat16),
                pltpu.VMEM(text.shape, text.dtype),
                pltpu.VMEM(w_out.shape, w_out.dtype),
                pltpu.VMEM(gain.shape, gain.dtype),
                pltpu.VMEM((query_count, top_count, rows, width), jnp.bfloat16),
                pltpu.SemaphoreType.DMA((2 * chunks + 4,)),
            ],
        ),
        out_shape=[
            jax.ShapeDtypeStruct((query_count, top_count), jnp.float32),
            pltpu.HBM((query_count, top_count, rows, width), jnp.bfloat16),
        ],
        compiler_params=pltpu.CompilerParams(vmem_limit_bytes=VMEM_LIMIT),
        cost_estimate=pl.CostEstimate(
            flops=2 * entries * rows * width * width, bytes_accessed=7 << 20, transcendentals=0
        ),
        name="finish",
    )(shards, place, in_hbm(back), in_hbm(text), in_hbm(w_out), in_hbm(gain))


def project_rows(rows_in, weight):
    return jnp.einsum("spc,cd->spd", rows_in, weight, preferred_element_type=jnp.float32).astype(jnp.bfloat16)


def on_device(queries, slab, cand_ids, patches, text_states, w_query, w_key, w_value, w_out, norm_gain):
    shard_count = lax.axis_size("shard")
    shard_here = lax.axis_index("shard")
    core = lax.axis_index("rep")
    grid_y, depth, grid_x = GRIDS[shard_count]
    query_count = queries.shape[0]
    slab_count = slab.shape[0]
    top_count = cand_ids.shape[1]
    list_length = query_count * top_count
    text_count, model_width = text_states.shape[1:]
    head_size = model_width // HEADS
    here_x, here_z, here_y = shard_here % grid_x, shard_here // grid_x % depth, shard_here // (grid_x * depth)
    owned = depth // PAIR
    columns = [
        [(y * depth + k * PAIR + in_pair) * grid_x + x for k in range(owned)]
        for y in range(grid_y)
        for x in range(grid_x)
        for in_pair in range(PAIR)
    ]
    pairs = [
        [
            (y * depth + k * PAIR + in_pair) * grid_x + x
            for in_pair in range(PAIR)
            for y in range(grid_y)
            for x in range(grid_x)
        ]
        for k in range(owned)
    ]
    swap = [(0, 1), (1, 0)]
    w_query_other = lax.ppermute(w_query, "rep", swap)
    own_list = cand_ids.reshape(list_length)
    own_anchor = own_list // slab_count
    sent = pack(cand_ids, text_states.reshape(query_count * text_count, model_width), queries, slab_count)
    owners = lax.all_gather(sent, "shard", axis=0, tiled=True, axis_index_groups=columns)
    request = make_request(
        (here_z // PAIR * PAIR).reshape(1),
        owners.reshape(owned, sent.shape[0], model_width),
        w_query,
        w_query_other,
        grid_y,
        grid_x,
        text_count,
        query_count,
        top_count,
    )
    got = lax.all_to_all(request, "shard", split_axis=0, concat_axis=0, tiled=True, axis_index_groups=pairs)

    keys = project_rows(patches, jnp.concatenate([w_key, lax.ppermute(w_key, "rep", swap)], axis=1))
    values = project_rows(patches, jnp.concatenate([w_value, lax.ppermute(w_value, "rep", swap)], axis=1))
    w_out_other = lax.ppermute(w_out, "rep", swap)
    half = model_width // 2
    w_out_whole = jnp.where(
        core == 0,
        jnp.concatenate([w_out, w_out_other], axis=1),
        jnp.concatenate(
            [
                jnp.concatenate([w_out_other[half:], w_out[half:]], axis=1),
                jnp.concatenate([w_out_other[:half], w_out[:half]], axis=1),
            ],
            axis=0,
        ),
    )

    context = serve(
        got, slab, keys, values, grid_y, grid_x, owned, text_count, query_count, top_count, head_size
    )
    back = lax.all_to_all(context, "shard", split_axis=0, concat_axis=0, tiled=True)

    source = (here_z % PAIR * grid_y + here_y) * grid_x + here_x
    place = (source * owned + here_z // PAIR) % (LANES // query_count)
    retrieval, attended = finish(
        own_anchor,
        place.reshape(1),
        back,
        text_states,
        w_out_whole,
        norm_gain.reshape(1, model_width),
        top_count,
        math.log(slab_count * shard_count),
    )
    return (retrieval, attended)


def solution(mesh):
    in_specs = (
        P(("shard", "rep"), None),
        P("shard", None),
        P(("shard", "rep"), None),
        P("shard", None, None),
        P(("shard", "rep"), None, None),
        P(None, "rep"),
        P(None, "rep"),
        P(None, "rep"),
        P(None, "rep"),
        P(),
    )
    out_specs = (P(("shard", "rep"), None), P(("shard", "rep"), None, None, None))
    return jax.shard_map(
        on_device, mesh=mesh, in_specs=in_specs, out_specs=out_specs, check_vma=False
    )
```

```python
import functools
import math

import jax
import jax.numpy as jnp
from jax import lax
from jax.experimental import pallas as pl
from jax.experimental.pallas import tpu as pltpu
from jax.sharding import PartitionSpec as P

HEADS = 12
SCALE = 100.0
EPSILON = 1e-06
LANES = 128
EXTRA = 8
UNROLL = 16
PAIR = 2
GRIDS = {128: (4, 8, 4), 8: (2, 2, 2)}
VMEM_LIMIT = 48 * 1024 * 1024


def row_of(shape, dim):
    return lax.broadcasted_iota(jnp.int32, shape, dim)


def split_source(source, grid_y, grid_x):
    if isinstance(source, int):
        return source // (grid_y * grid_x), source // grid_x % grid_y, source % grid_x
    return lax.div(source, grid_y * grid_x), lax.rem(lax.div(source, grid_x), grid_y), lax.rem(source, grid_x)


def owner_of(source, k, grid_y, grid_x, owned):
    in_pair, y, x = split_source(source, grid_y, grid_x)
    return (y * owned * PAIR + k * PAIR + in_pair) * grid_x + x


def in_hbm(array):
    return pltpu.with_memory_space_constraint(array, pltpu.HBM)


def pack_kernel(ids_hbm, text_hbm, queries_hbm, out, ids, queries, sems, *, slab_count):
    rows = text_hbm.shape[0]
    copies = [
        pltpu.make_async_copy(ids_hbm, ids, sems.at[0]),
        pltpu.make_async_copy(queries_hbm, queries, sems.at[1]),
        pltpu.make_async_copy(text_hbm, out.at[pl.ds(0, rows), :], sems.at[2]),
    ]
    for copy in copies:
        copy.start()
    count, width = queries.shape
    lane = row_of((EXTRA, LANES), 1)
    image = jnp.full((EXTRA, LANES), -1, jnp.int32)
    listed = image
    copies[0].wait()
    for entry in range(ids.shape[0] * ids.shape[1]):
        row = ids[entry // ids.shape[1], entry % ids.shape[1]]
        here = lane == lax.div(row, slab_count)
        image = jnp.where(here, lax.rem(row, slab_count), image)
        listed = jnp.where(here, entry, listed)
    copies[1].wait()
    pieces = [queries[...].astype(jnp.float32)]
    if count < EXTRA:
        pieces.append(jnp.zeros((EXTRA - count, width), jnp.float32))
    code = [image.astype(jnp.float32), listed.astype(jnp.float32)]
    code.append(jnp.zeros((EXTRA, width - 2 * LANES), jnp.float32))
    pieces.append(jnp.concatenate(code, axis=1))
    out[rows:, :] = jnp.concatenate(pieces, axis=0).astype(jnp.bfloat16)
    copies[2].wait()


def pack(ids, text, queries, slab_count):
    rows, width = text.shape
    return pl.pallas_call(
        functools.partial(pack_kernel, slab_count=slab_count),
        in_specs=[pl.BlockSpec(memory_space=pltpu.HBM)] * 3,
        out_specs=pl.BlockSpec(memory_space=pltpu.VMEM),
        scratch_shapes=[
            pltpu.SMEM(ids.shape, ids.dtype),
            pltpu.VMEM(queries.shape, queries.dtype),
            pltpu.SemaphoreType.DMA((3,)),
        ],
        out_shape=jax.ShapeDtypeStruct((rows + 2 * EXTRA, width), jnp.bfloat16),
        compiler_params=pltpu.CompilerParams(vmem_limit_bytes=VMEM_LIMIT),
        cost_estimate=pl.CostEstimate(flops=1 << 20, bytes_accessed=1 << 18, transcendentals=0),
        name="pack",
    )(in_hbm(ids), in_hbm(text), in_hbm(queries))


def to_scalars(vectors, decoded, table, sem):
    decoded[...] = vectors
    copy = pltpu.make_async_copy(decoded, table, sem)
    copy.start()
    copy.wait()


def request_kernel(
    place, w_own, w_other, *rest, depth, grid_y, grid_x, rows, query_count, top_count
):
    owners = rest[:depth]
    out, decoded, table, projected, shared, sem = rest[depth:]
    step = pl.program_id(0)
    height, width = owners[0].shape
    texts = height - 2 * EXTRA
    body = projected.shape[1]
    tile_row = row_of((EXTRA, LANES), 0)

    @pl.when(step == 0)
    def _():
        places = [lax.rem(place[1] + depth - o, depth) for o in range(depth)]
        found = [jnp.zeros((EXTRA, LANES), jnp.float32) for _ in range(2)]
        for o in range(depth):
            code = owners[o][texts + EXTRA :, : 2 * LANES].astype(jnp.float32)
            found = [jnp.where(tile_row == places[o], code[:, i * LANES : (i + 1) * LANES], found[i]) for i in range(2)]
        decoded[...] = jnp.concatenate(found, axis=0).astype(jnp.int32)
        copy = pltpu.make_async_copy(decoded, table, sem)
        copy.start()
        states = jnp.concatenate([owner[:texts, :] for owner in owners], axis=0)
        at = 0
        for weight in (w_own, w_other):
            half = jnp.dot(states, weight[...], preferred_element_type=jnp.float32).astype(jnp.bfloat16)
            for c in range(half.shape[1] // LANES):
                for o in range(depth):
                    for q in range(query_count):
                        t = o * query_count + q
                        projected[places[o] * query_count + q, at : at + rows, :] = half[
                            t * rows : (t + 1) * rows, c * LANES : (c + 1) * LANES
                        ]
                at += rows
        picked = jnp.zeros((depth * query_count, width), jnp.float32)
        for o in range(depth):
            part = owners[o][texts : texts + EXTRA, :].astype(jnp.float32)[:query_count]
            spread = jnp.concatenate([part] * depth, axis=0)
            picked = jnp.where(row_of(picked.shape, 0) // query_count == places[o], spread, picked)
        picked = picked.astype(jnp.bfloat16)
        for c in range(width // LANES):
            size = depth * query_count
            shared[c * size : (c + 1) * size, :] = picked[:, c * LANES : (c + 1) * LANES]
        copy.wait()

    lane = row_of((EXTRA, LANES), 1)
    for i in range(out.shape[0]):
        target = step * out.shape[0] + i
        in_pair, y, x = split_source(target, grid_y, grid_x)
        shard = (y * depth * PAIR + place[0] + in_pair) * grid_x + x
        code = jnp.full((EXTRA, LANES), -1.0, jnp.float32)
        for z in range(depth):
            image, listed = table[z, shard], table[EXTRA + z, shard]
            query = lax.div(jnp.maximum(listed, 0), top_count)
            out[i, z * body : (z + 1) * body, :] = projected[z * query_count + query]
            code = jnp.where(lane == z, image.astype(jnp.float32), code)
            code = jnp.where(lane == EXTRA + z, listed.astype(jnp.float32), code)
        out[i, depth * body : depth * body + shared.shape[0], :] = shared[...]
        out[i, depth * body + shared.shape[0] :, :] = code.astype(jnp.bfloat16)


def make_request(place, owners, w_own, w_other, grid_y, grid_x, rows, query_count, top_count):
    depth = len(owners)
    width = owners[0].shape[1]
    body = width // LANES * rows
    shared_rows = depth * query_count * (width // LANES)
    total = depth * body + shared_rows + EXTRA
    targets = PAIR * grid_y * grid_x
    block = min(8, targets)
    whole = lambda a: pl.BlockSpec(a.shape, lambda i, *_: (0,) * a.ndim)
    return pl.pallas_call(
        functools.partial(
            request_kernel,
            depth=depth,
            grid_y=grid_y,
            grid_x=grid_x,
            rows=rows,
            query_count=query_count,
            top_count=top_count,
        ),
        grid_spec=pltpu.PrefetchScalarGridSpec(
            num_scalar_prefetch=1,
            grid=(targets // block,),
            in_specs=[whole(w_own), whole(w_other)] + [whole(owner) for owner in owners],
            out_specs=pl.BlockSpec((block, total, LANES), lambda i, *_: (i, 0, 0)),
            scratch_shapes=[
                pltpu.VMEM((2 * EXTRA, LANES), jnp.int32),
                pltpu.SMEM((2 * EXTRA, LANES), jnp.int32),
                pltpu.VMEM((depth * query_count, body, LANES), jnp.bfloat16),
                pltpu.VMEM((shared_rows, LANES), jnp.bfloat16),
                pltpu.SemaphoreType.DMA,
            ],
        ),
        out_shape=pltpu.HBM((targets, total, LANES), jnp.bfloat16),
        compiler_params=pltpu.CompilerParams(vmem_limit_bytes=VMEM_LIMIT),
        cost_estimate=pl.CostEstimate(flops=1 << 29, bytes_accessed=6 << 20, transcendentals=0),
        name="request",
    )(place, in_hbm(w_own), w_other, *owners)


def index_stats(query, slab, picked, logits):
    count = query.shape[0]
    tile = min(256, slab.shape[0])
    peak = None
    for t in range(slab.shape[0] // tile):
        part = SCALE * lax.dot_general(
            slab[t * tile : (t + 1) * tile, :], query, (((1,), (1,)), ((), ())), preferred_element_type=jnp.float32
        )
        logits[t * tile : (t + 1) * tile, :] = part
        top = jnp.max(part, axis=0, keepdims=True)
        peak = top if peak is None else jnp.maximum(peak, top)
    total = jnp.zeros_like(peak)
    for t in range(slab.shape[0] // tile):
        total = total + jnp.sum(jnp.exp(logits[t * tile : (t + 1) * tile, :] - peak), axis=0, keepdims=True)
    chosen = row_of((tile, count), 0) == picked
    candidate = jnp.sum(jnp.where(chosen, logits[:tile, :], 0.0), axis=0, keepdims=True)
    return peak, total, candidate


def split_rows(exact):
    tile_row = row_of((EXTRA, LANES), 0)
    exact = jnp.broadcast_to(exact, (EXTRA, LANES))
    high = exact.astype(jnp.bfloat16).astype(jnp.float32)
    left = exact - high
    middle = left.astype(jnp.bfloat16).astype(jnp.float32)
    parts = jnp.where(tile_row == 0, high, jnp.where(tile_row == 1, middle, left - middle))
    return jnp.where(tile_row < 3, parts, 0.0)


def serve_kernel(
    got_hbm, slab_hbm, keys_hbm, values_hbm, out_hbm,
    out, got, slab, keys, values, logits, decoded, table, listed, sems, *, grid_y, grid_x, depth, rows, query_count, top_count, head_size
):
    sources = got.shape[0]
    slots = sources * depth
    columns = keys.shape[2]
    body = columns // LANES * rows
    slot_rows = depth * body
    late = got.shape[1] - slot_rows
    copies = [
        pltpu.make_async_copy(source, target, sems.at[i])
        for i, (source, target) in enumerate(
            [
                (got_hbm.at[:, pl.ds(slot_rows, late), :], got.at[:, pl.ds(slot_rows, late), :]),
                (slab_hbm, slab),
                (got_hbm.at[:, pl.ds(0, slot_rows), :], got.at[:, pl.ds(0, slot_rows), :]),
                (keys_hbm, keys),
                (values_hbm, values),
            ]
        )
    ]
    for copy in copies:
        copy.start()
    size = depth * query_count
    shared_rows = size * (columns // LANES)
    per_chunk = LANES // query_count
    lane = row_of((EXTRA, LANES), 1)
    tile_row = row_of((EXTRA, LANES), 0)

    copies[0].wait()
    found = [jnp.zeros((EXTRA, LANES), jnp.float32) for _ in range(-(-sources // EXTRA))]
    for source in range(sources):
        code = got[source, slot_rows + shared_rows :, :LANES].astype(jnp.float32)
        found[source // EXTRA] = jnp.where(tile_row == source % EXTRA, code, found[source // EXTRA])
    found = found[0] if len(found) == 1 else jnp.concatenate(found, axis=0)
    to_scalars(found.astype(jnp.int32), decoded, table, sems.at[5])

    count = 0
    chunks = [jnp.full((EXTRA, LANES), -1, jnp.int32) for _ in range(-(-slots // per_chunk))]
    for slot in range(slots):
        image, entry = table[slot // depth, slot % depth], table[slot // depth, EXTRA + slot % depth]
        query = lax.div(jnp.maximum(entry, 0), top_count)
        at = slot % per_chunk * query_count + query
        chunks[slot // per_chunk] = jnp.where(lane == at, image, chunks[slot // per_chunk])
        listed[count] = slot
        count = count + jnp.where(image >= 0, 1, 0)
    last = listed[jnp.maximum(count - 1, 0)]
    for g in range(UNROLL):
        listed[count + g] = last

    queries = jnp.concatenate(
        [
            jnp.concatenate(
                [
                    got[source, slot_rows + c * size : slot_rows + (c + 1) * size, :]
                    for c in range(columns // LANES)
                ],
                axis=1,
            )
            for source in range(sources)
        ],
        axis=0,
    )
    missing = len(chunks) * LANES - queries.shape[0]
    if missing:
        queries = jnp.concatenate([queries, jnp.zeros((missing, queries.shape[1]), queries.dtype)], axis=0)
    copies[1].wait()
    stats = index_stats(queries, slab, jnp.concatenate([chunk[:1] for chunk in chunks], axis=1), logits)
    for c in range(len(chunks)):
        tiles = [split_rows(stat[:, c * LANES : (c + 1) * LANES]) for stat in stats]
        tiles = [tiles[0], pltpu.roll(tiles[1], query_count, 1), pltpu.roll(tiles[2], 2 * query_count, 1)]
        for slot in range(c * per_chunk, min((c + 1) * per_chunk, slots)):
            source, z = slot // depth, slot % depth
            at = slot % per_chunk
            owner = owner_of(source, z, grid_y, grid_x, depth)
            place = lane // query_count
            tile = jnp.where(place == at, tiles[0], jnp.where(place == (at + 1) % per_chunk, tiles[1], tiles[2]))
            out[owner, body:, :] = tile.astype(jnp.bfloat16)

    stats_out = pltpu.make_async_copy(
        out.at[:, pl.ds(body, EXTRA), :], out_hbm.at[:, pl.ds(body, EXTRA), :], sems.at[6]
    )
    stats_out.start()

    def send(owner):
        return pltpu.make_async_copy(out.at[owner, pl.ds(0, body), :], out_hbm.at[owner, pl.ds(0, body), :], sems.at[7])

    copies[2].wait()
    copies[3].wait()
    copies[4].wait()
    spans = []
    at = 0
    while at < columns:
        width = min(2 * LANES, columns - at)
        lane_head = row_of((rows, width), 1) // head_size
        spans.append((at, width, [jnp.where(lane_head == h, 1.0, 0.0) for h in range(width // head_size)]))
        at += width

    def group(index, carry):
        chosen = [listed[index * UNROLL + g] for g in range(UNROLL)]
        places = [(lax.div(slot, depth), lax.rem(slot, depth)) for slot in chosen]
        images = [table[source, z] for source, z in places]
        owners = [owner_of(source, z, grid_y, grid_x, depth) for source, z in places]
        work = [(g, span) for g in range(UNROLL) for span in spans]
        scores = []
        for g, (at, width, masks) in work:
            source, z = places[g]
            pieces = [
                got[source, pl.ds(pl.multiple_of(z * body + c * rows, rows), rows), :]
                for c in range(at // LANES, (at + width) // LANES)
            ]
            query = pieces[0] if len(pieces) == 1 else jnp.concatenate(pieces, axis=1)
            spread = jnp.concatenate([query * mask.astype(query.dtype) for mask in masks], axis=0)
            scores.append(
                lax.dot_general(
                    spread,
                    keys[images[g], :, at : at + width],
                    (((1,), (1,)), ((), ())),
                    preferred_element_type=jnp.float32,
                )
            )
        scores = [score * head_size ** (-0.5) for score in scores]
        highest = [jnp.max(score, axis=-1, keepdims=True) for score in scores]
        powers = [jnp.exp(score - top) for score, top in zip(scores, highest)]
        totals = [jnp.sum(power, axis=-1, keepdims=True) for power in powers]
        weights = [(power / total).astype(jnp.bfloat16) for power, total in zip(powers, totals)]
        mixed = [
            jnp.dot(weight, values[images[g], :, at : at + width], preferred_element_type=jnp.float32)
            for weight, (g, (at, width, _)) in zip(weights, work)
        ]
        for mix, (g, (at, width, masks)) in zip(mixed, work):
            context = mix[:rows] * masks[0]
            for h in range(1, len(masks)):
                context = context + mix[h * rows : (h + 1) * rows] * masks[h]
            context = context.astype(jnp.bfloat16)
            for c in range(width // LANES):
                out[owners[g], (at // LANES + c) * rows : (at // LANES + c + 1) * rows, :] = context[
                    :, c * LANES : (c + 1) * LANES
                ]
        for owner in owners:
            send(owner).start()
        return carry

    def drain(index, carry):
        for _ in range(UNROLL):
            send(0).wait()
        return carry

    groups = lax.div(count + UNROLL - 1, UNROLL)
    lax.fori_loop(0, groups, group, 0)
    lax.fori_loop(0, groups, drain, 0)
    stats_out.wait()


def serve(got, slab, keys, values, grid_y, grid_x, depth, rows, query_count, top_count, head_size):
    sources = got.shape[0]
    slots = sources * depth
    body = keys.shape[2] // LANES * rows
    lanes = -(-slots * query_count // LANES) * LANES
    operands = [got, slab, keys, values]
    codes = (-(-sources // EXTRA) * EXTRA, LANES)
    return pl.pallas_call(
        functools.partial(
            serve_kernel,
            grid_y=grid_y,
            grid_x=grid_x,
            depth=depth,
            rows=rows,
            query_count=query_count,
            top_count=top_count,
            head_size=head_size,
        ),
        grid=(1,),
        in_specs=[pl.BlockSpec(memory_space=pltpu.HBM)] * 4,
        out_specs=pl.BlockSpec(memory_space=pltpu.HBM),
        scratch_shapes=[pltpu.VMEM((slots, body + EXTRA, LANES), jnp.bfloat16)]
        + [pltpu.VMEM(a.shape, a.dtype) for a in operands]
        + [
            pltpu.VMEM((slab.shape[0], lanes), jnp.float32),
            pltpu.VMEM(codes, jnp.int32),
            pltpu.SMEM(codes, jnp.int32),
            pltpu.SMEM((slots + UNROLL,), jnp.int32),
            pltpu.SemaphoreType.DMA((8,)),
        ],
        out_shape=pltpu.HBM((slots, body + EXTRA, LANES), jnp.bfloat16),
        compiler_params=pltpu.CompilerParams(vmem_limit_bytes=VMEM_LIMIT),
        cost_estimate=pl.CostEstimate(flops=8 << 30, bytes_accessed=14 << 20, transcendentals=2 << 20),
        name="serve",
    )(*[in_hbm(a) for a in operands])


def finish_kernel(
    shards, place, back_hbm, text_hbm, w_out_hbm, gain_hbm, found, out_hbm,
    exact, gathered, back, sent, text, w_out, gain, out, sems, *, top_count, query_count, chunks, shift
):
    rows, width = text.shape[1:]
    body = back.shape[1]
    entries = query_count * top_count // chunks
    queries = query_count // chunks

    def fetch(entry, chunk):
        return pltpu.make_async_copy(back_hbm.at[shards[entry], pl.ds(0, body), :], back.at[entry], sems.at[chunk])

    loads = [
        pltpu.make_async_copy(source, target, sems.at[chunks + i])
        for i, (source, target) in enumerate(
            [
                (back_hbm.at[:, pl.ds(body, EXTRA), :], sent),
                (w_out_hbm, w_out),
                (text_hbm, text),
                (gain_hbm, gain),
            ]
        )
    ]
    for load in loads:
        load.start()
    for chunk in range(chunks):
        for entry in range(chunk * entries, (chunk + 1) * entries):
            fetch(entry, chunk).start()

    loads[0].wait()
    parts = sent[...].astype(jnp.float32)
    joined = jnp.sum(jnp.where(row_of(parts.shape, 1) < 3, parts, 0.0), axis=1)
    joined = pltpu.roll(joined, lax.rem(LANES - place[0] * query_count, LANES), 1)
    exact[...] = joined
    peak = jnp.max(joined, axis=0, keepdims=True)
    scaled = jnp.exp(joined - peak) * pltpu.roll(joined, LANES - query_count, 1)
    total = jnp.sum(scaled, axis=0, keepdims=True)
    total = jnp.where(row_of(total.shape, 1) < query_count, total, 1.0)
    normalizers = peak + jnp.log(total)
    for query in range(query_count):
        picked = jnp.concatenate([exact[pl.ds(shards[query * top_count + k], 1), :] for k in range(top_count)], axis=0)
        lane = row_of(picked.shape, 1)
        candidate = jnp.sum(jnp.where(lane == 2 * query_count + query, picked, 0.0), axis=1, keepdims=True)
        result = candidate - normalizers[:, query : query + 1] + shift
        result = jnp.sum(jnp.where(lane == row_of(picked.shape, 0), result, 0.0), axis=0, keepdims=True)
        found[query : query + 1, :] = result[:, :top_count]

    for load in loads[1:]:
        load.wait()
    stores = []
    for chunk in range(chunks):
        first = chunk * queries
        for entry in range(chunk * entries, (chunk + 1) * entries):
            fetch(entry, chunk).wait()
        for k in range(entries):
            for j in range(body // rows):
                gathered[chunk, k * rows : (k + 1) * rows, j * LANES : (j + 1) * LANES] = back[
                    chunk * entries + k, j * rows : (j + 1) * rows, :
                ]
        mixed = jnp.dot(gathered[chunk], w_out[...], preferred_element_type=jnp.float32)
        states = text[first : first + queries].astype(jnp.float32).reshape(queries, 1, rows, width)
        summed = mixed.reshape(queries, top_count, rows, width) + states
        mean = jnp.mean(summed, axis=-1, keepdims=True)
        centred = summed - mean
        variance = jnp.mean(centred * centred, axis=-1, keepdims=True)
        normed = centred * lax.rsqrt(variance + EPSILON) * gain[...].reshape(1, 1, 1, width)
        out[first : first + queries] = normed.astype(jnp.bfloat16)
        store = pltpu.make_async_copy(
            out.at[pl.ds(first, queries)], out_hbm.at[pl.ds(first, queries)], sems.at[chunks + 4 + chunk]
        )
        store.start()
        stores.append(store)
    for store in stores:
        store.wait()


def finish(shards, place, back, text, w_out, gain, top_count, shift):
    query_count, rows, width = text.shape
    chunks = 2
    body = back.shape[1] - EXTRA
    entries = query_count * top_count
    return pl.pallas_call(
        functools.partial(finish_kernel, top_count=top_count, query_count=query_count, chunks=chunks, shift=shift),
        grid_spec=pltpu.PrefetchScalarGridSpec(
            num_scalar_prefetch=2,
            grid=(1,),
            in_specs=[pl.BlockSpec(memory_space=pltpu.HBM)] * 4,
            out_specs=[
                pl.BlockSpec((query_count, top_count), lambda i, *_: (0, 0)),
                pl.BlockSpec(memory_space=pltpu.HBM),
            ],
            scratch_shapes=[
                pltpu.VMEM((back.shape[0], LANES), jnp.float32),
                pltpu.VMEM((chunks, entries // chunks * rows, width), jnp.bfloat16),
                pltpu.VMEM((entries, body, LANES), jnp.bfloat16),
                pltpu.VMEM((back.shape[0], EXTRA, LANES), jnp.bfloat16),
                pltpu.VMEM(text.shape, text.dtype),
                pltpu.VMEM(w_out.shape, w_out.dtype),
                pltpu.VMEM(gain.shape, gain.dtype),
                pltpu.VMEM((query_count, top_count, rows, width), jnp.bfloat16),
                pltpu.SemaphoreType.DMA((2 * chunks + 4,)),
            ],
        ),
        out_shape=[
            jax.ShapeDtypeStruct((query_count, top_count), jnp.float32),
            pltpu.HBM((query_count, top_count, rows, width), jnp.bfloat16),
        ],
        compiler_params=pltpu.CompilerParams(vmem_limit_bytes=VMEM_LIMIT),
        cost_estimate=pl.CostEstimate(
            flops=2 * entries * rows * width * width, bytes_accessed=7 << 20, transcendentals=0
        ),
        name="finish",
    )(shards, place, in_hbm(back), in_hbm(text), in_hbm(w_out), in_hbm(gain))


def project_rows(rows_in, weight):
    return jnp.einsum("spc,cd->spd", rows_in, weight, preferred_element_type=jnp.float32).astype(jnp.bfloat16)


def on_device(queries, slab, cand_ids, patches, text_states, w_query, w_key, w_value, w_out, norm_gain):
    shard_count = lax.axis_size("shard")
    shard_here = lax.axis_index("shard")
    core = lax.axis_index("rep")
    grid_y, depth, grid_x = GRIDS[shard_count]
    query_count = queries.shape[0]
    slab_count = slab.shape[0]
    top_count = cand_ids.shape[1]
    list_length = query_count * top_count
    text_count, model_width = text_states.shape[1:]
    head_size = model_width // HEADS
    here_x, here_z, here_y = shard_here % grid_x, shard_here // grid_x % depth, shard_here // (grid_x * depth)
    owned = depth // PAIR
    pairs = [
        [
            (y * depth + k * PAIR + in_pair) * grid_x + x
            for in_pair in range(PAIR)
            for y in range(grid_y)
            for x in range(grid_x)
        ]
        for k in range(owned)
    ]
    swap = [(0, 1), (1, 0)]
    w_query_other = lax.ppermute(w_query, "rep", swap)
    own_list = cand_ids.reshape(list_length)
    own_anchor = own_list // slab_count
    sent = pack(cand_ids, text_states.reshape(query_count * text_count, model_width), queries, slab_count)
    owners = [sent]
    for o in range(1, owned):
        moves = [
            (
                (y * depth + z) * grid_x + x,
                (y * depth + (z + o * PAIR) % depth) * grid_x + x,
            )
            for y in range(grid_y)
            for z in range(depth)
            for x in range(grid_x)
        ]
        owners.append(lax.ppermute(sent, "shard", moves))
    request = make_request(
        jnp.stack([here_z // PAIR * PAIR, here_z // PAIR]),
        owners,
        w_query,
        w_query_other,
        grid_y,
        grid_x,
        text_count,
        query_count,
        top_count,
    )
    got = lax.all_to_all(request, "shard", split_axis=0, concat_axis=0, tiled=True, axis_index_groups=pairs)

    keys = project_rows(patches, jnp.concatenate([w_key, lax.ppermute(w_key, "rep", swap)], axis=1))
    values = project_rows(patches, jnp.concatenate([w_value, lax.ppermute(w_value, "rep", swap)], axis=1))
    w_out_other = lax.ppermute(w_out, "rep", swap)
    half = model_width // 2
    w_out_whole = jnp.where(
        core == 0,
        jnp.concatenate([w_out, w_out_other], axis=1),
        jnp.concatenate(
            [
                jnp.concatenate([w_out_other[half:], w_out[half:]], axis=1),
                jnp.concatenate([w_out_other[:half], w_out[:half]], axis=1),
            ],
            axis=0,
        ),
    )

    context = serve(
        got, slab, keys, values, grid_y, grid_x, owned, text_count, query_count, top_count, head_size
    )
    back = lax.all_to_all(context, "shard", split_axis=0, concat_axis=0, tiled=True)

    source = (here_z % PAIR * grid_y + here_y) * grid_x + here_x
    place = (source * owned + here_z // PAIR) % (LANES // query_count)
    retrieval, attended = finish(
        own_anchor,
        place.reshape(1),
        back,
        text_states,
        w_out_whole,
        norm_gain.reshape(1, model_width),
        top_count,
        math.log(slab_count * shard_count),
    )
    return (retrieval, attended)


def solution(mesh):
    in_specs = (
        P(("shard", "rep"), None),
        P("shard", None),
        P(("shard", "rep"), None),
        P("shard", None, None),
        P(("shard", "rep"), None, None),
        P(None, "rep"),
        P(None, "rep"),
        P(None, "rep"),
        P(None, "rep"),
        P(),
    )
    out_specs = (P(("shard", "rep"), None), P(("shard", "rep"), None, None, None))
    return jax.shard_map(
        on_device, mesh=mesh, in_specs=in_specs, out_specs=out_specs, check_vma=False
    )
```

```python
import functools
import math

import jax
import jax.numpy as jnp
from jax import lax
from jax.experimental import pallas as pl
from jax.experimental.pallas import tpu as pltpu
from jax.sharding import PartitionSpec as P

HEADS = 12
SCALE = 100.0
EPSILON = 1e-06
LANES = 128
EXTRA = 8
UNROLL = 16
PAIR = 2
GRIDS = {128: (4, 8, 4), 8: (2, 2, 2)}
VMEM_LIMIT = 48 * 1024 * 1024


def row_of(shape, dim):
    return lax.broadcasted_iota(jnp.int32, shape, dim)


def split_source(source, grid_y, grid_x):
    if isinstance(source, int):
        return source // (grid_y * grid_x), source // grid_x % grid_y, source % grid_x
    return lax.div(source, grid_y * grid_x), lax.rem(lax.div(source, grid_x), grid_y), lax.rem(source, grid_x)


def owner_of(source, k, grid_y, grid_x, owned):
    in_pair, y, x = split_source(source, grid_y, grid_x)
    return (y * owned * PAIR + k * PAIR + in_pair) * grid_x + x


def in_hbm(array):
    return pltpu.with_memory_space_constraint(array, pltpu.HBM)


def pack_kernel(ids_hbm, text_hbm, queries_hbm, out, ids, queries, sems, *, slab_count):
    rows = text_hbm.shape[0]
    copies = [
        pltpu.make_async_copy(ids_hbm, ids, sems.at[0]),
        pltpu.make_async_copy(queries_hbm, queries, sems.at[1]),
        pltpu.make_async_copy(text_hbm, out.at[pl.ds(0, rows), :], sems.at[2]),
    ]
    for copy in copies:
        copy.start()
    count, width = queries.shape
    lane = row_of((EXTRA, LANES), 1)
    image = jnp.full((EXTRA, LANES), -1, jnp.int32)
    listed = image
    copies[0].wait()
    for entry in range(ids.shape[0] * ids.shape[1]):
        row = ids[entry // ids.shape[1], entry % ids.shape[1]]
        here = lane == lax.div(row, slab_count)
        image = jnp.where(here, lax.rem(row, slab_count), image)
        listed = jnp.where(here, entry, listed)
    copies[1].wait()
    pieces = [queries[...].astype(jnp.float32)]
    if count < EXTRA:
        pieces.append(jnp.zeros((EXTRA - count, width), jnp.float32))
    code = [image.astype(jnp.float32), listed.astype(jnp.float32)]
    code.append(jnp.zeros((EXTRA, width - 2 * LANES), jnp.float32))
    pieces.append(jnp.concatenate(code, axis=1))
    out[rows:, :] = jnp.concatenate(pieces, axis=0).astype(jnp.bfloat16)
    copies[2].wait()


def pack(ids, text, queries, slab_count):
    rows, width = text.shape
    return pl.pallas_call(
        functools.partial(pack_kernel, slab_count=slab_count),
        in_specs=[pl.BlockSpec(memory_space=pltpu.HBM)] * 3,
        out_specs=pl.BlockSpec(memory_space=pltpu.VMEM),
        scratch_shapes=[
            pltpu.SMEM(ids.shape, ids.dtype),
            pltpu.VMEM(queries.shape, queries.dtype),
            pltpu.SemaphoreType.DMA((3,)),
        ],
        out_shape=jax.ShapeDtypeStruct((rows + 2 * EXTRA, width), jnp.bfloat16),
        compiler_params=pltpu.CompilerParams(vmem_limit_bytes=VMEM_LIMIT),
        cost_estimate=pl.CostEstimate(flops=1 << 20, bytes_accessed=1 << 18, transcendentals=0),
        name="pack",
    )(in_hbm(ids), in_hbm(text), in_hbm(queries))


def to_scalars(vectors, decoded, table, sem):
    decoded[...] = vectors
    copy = pltpu.make_async_copy(decoded, table, sem)
    copy.start()
    copy.wait()


def request_kernel(
    place, owners, w_own, w_other, out, decoded, table, projected, shared, sem,
    *, grid_y, grid_x, rows, query_count, top_count
):
    step = pl.program_id(0)
    depth, height, width = owners.shape
    texts = height - 2 * EXTRA
    body = projected.shape[1]
    tile_row = row_of((EXTRA, LANES), 0)

    @pl.when(step == 0)
    def _():
        found = [jnp.zeros((EXTRA, LANES), jnp.float32) for _ in range(2)]
        for z in range(depth):
            code = owners[z, texts + EXTRA :, : 2 * LANES].astype(jnp.float32)
            found = [jnp.where(tile_row == z, code[:, i * LANES : (i + 1) * LANES], found[i]) for i in range(2)]
        decoded[...] = jnp.concatenate(found, axis=0).astype(jnp.int32)
        copy = pltpu.make_async_copy(decoded, table, sem)
        copy.start()
        states = owners[:, :texts, :].reshape(depth * texts, width)
        at = 0
        for weight in (w_own, w_other):
            half = jnp.dot(states, weight[...], preferred_element_type=jnp.float32).astype(jnp.bfloat16)
            for c in range(half.shape[1] // LANES):
                for t in range(depth * query_count):
                    projected[t, at : at + rows, :] = half[t * rows : (t + 1) * rows, c * LANES : (c + 1) * LANES]
                at += rows
        picked = [owners[z, texts : texts + EXTRA, :].astype(jnp.float32)[:query_count] for z in range(depth)]
        picked = jnp.concatenate(picked, axis=0).astype(jnp.bfloat16)
        for c in range(width // LANES):
            size = depth * query_count
            shared[c * size : (c + 1) * size, :] = picked[:, c * LANES : (c + 1) * LANES]
        copy.wait()

    lane = row_of((EXTRA, LANES), 1)
    for i in range(out.shape[0]):
        target = step * out.shape[0] + i
        in_pair, y, x = split_source(target, grid_y, grid_x)
        shard = (y * depth * PAIR + place[0] + in_pair) * grid_x + x
        code = jnp.full((EXTRA, LANES), -1.0, jnp.float32)
        for z in range(depth):
            image, listed = table[z, shard], table[EXTRA + z, shard]
            query = lax.div(jnp.maximum(listed, 0), top_count)
            out[i, z * body : (z + 1) * body, :] = projected[z * query_count + query]
            code = jnp.where(lane == z, image.astype(jnp.float32), code)
            code = jnp.where(lane == EXTRA + z, listed.astype(jnp.float32), code)
        out[i, depth * body : depth * body + shared.shape[0], :] = shared[...]
        out[i, depth * body + shared.shape[0] :, :] = code.astype(jnp.bfloat16)


def make_request(place, owners, w_own, w_other, grid_y, grid_x, rows, query_count, top_count):
    depth, height, width = owners.shape
    body = width // LANES * rows
    shared_rows = depth * query_count * (width // LANES)
    total = depth * body + shared_rows + EXTRA
    targets = PAIR * grid_y * grid_x
    block = min(8, targets)
    whole = lambda a: pl.BlockSpec(a.shape, lambda i, *_: (0,) * a.ndim)
    return pl.pallas_call(
        functools.partial(
            request_kernel,
            grid_y=grid_y,
            grid_x=grid_x,
            rows=rows,
            query_count=query_count,
            top_count=top_count,
        ),
        grid_spec=pltpu.PrefetchScalarGridSpec(
            num_scalar_prefetch=1,
            grid=(targets // block,),
            in_specs=[whole(owners), whole(w_own), whole(w_other)],
            out_specs=pl.BlockSpec((block, total, LANES), lambda i, *_: (i, 0, 0)),
            scratch_shapes=[
                pltpu.VMEM((2 * EXTRA, LANES), jnp.int32),
                pltpu.SMEM((2 * EXTRA, LANES), jnp.int32),
                pltpu.VMEM((depth * query_count, body, LANES), jnp.bfloat16),
                pltpu.VMEM((shared_rows, LANES), jnp.bfloat16),
                pltpu.SemaphoreType.DMA,
            ],
        ),
        out_shape=pltpu.HBM((targets, total, LANES), jnp.bfloat16),
        compiler_params=pltpu.CompilerParams(vmem_limit_bytes=VMEM_LIMIT),
        cost_estimate=pl.CostEstimate(flops=1 << 29, bytes_accessed=6 << 20, transcendentals=0),
        name="request",
    )(place, in_hbm(owners), in_hbm(w_own), w_other)


def index_stats(query, slab, picked, logits):
    count = query.shape[0]
    tile = min(256, slab.shape[0])
    peak = None
    for t in range(slab.shape[0] // tile):
        part = SCALE * lax.dot_general(
            slab[t * tile : (t + 1) * tile, :], query, (((1,), (1,)), ((), ())), preferred_element_type=jnp.float32
        )
        logits[t * tile : (t + 1) * tile, :] = part
        top = jnp.max(part, axis=0, keepdims=True)
        peak = top if peak is None else jnp.maximum(peak, top)
    total = jnp.zeros_like(peak)
    for t in range(slab.shape[0] // tile):
        total = total + jnp.sum(jnp.exp(logits[t * tile : (t + 1) * tile, :] - peak), axis=0, keepdims=True)
    chosen = row_of((tile, count), 0) == picked
    candidate = jnp.sum(jnp.where(chosen, logits[:tile, :], 0.0), axis=0, keepdims=True)
    return peak, total, candidate


def split_rows(exact):
    tile_row = row_of((EXTRA, LANES), 0)
    exact = jnp.broadcast_to(exact, (EXTRA, LANES))
    high = exact.astype(jnp.bfloat16).astype(jnp.float32)
    left = exact - high
    middle = left.astype(jnp.bfloat16).astype(jnp.float32)
    parts = jnp.where(tile_row == 0, high, jnp.where(tile_row == 1, middle, left - middle))
    return jnp.where(tile_row < 3, parts, 0.0)


def serve_kernel(
    got_hbm, slab_hbm, keys_hbm, values_hbm, out_hbm,
    out, got, slab, keys, values, logits, decoded, table, listed, sems, *, grid_y, grid_x, depth, rows, query_count, top_count, head_size
):
    sources = got.shape[0]
    slots = sources * depth
    columns = keys.shape[2]
    body = columns // LANES * rows
    slot_rows = depth * body
    late = got.shape[1] - slot_rows
    copies = [
        pltpu.make_async_copy(source, target, sems.at[i])
        for i, (source, target) in enumerate(
            [
                (got_hbm.at[:, pl.ds(slot_rows, late), :], got.at[:, pl.ds(slot_rows, late), :]),
                (slab_hbm, slab),
                (got_hbm.at[:, pl.ds(0, slot_rows), :], got.at[:, pl.ds(0, slot_rows), :]),
                (keys_hbm, keys),
                (values_hbm, values),
            ]
        )
    ]
    for copy in copies:
        copy.start()
    size = depth * query_count
    shared_rows = size * (columns // LANES)
    per_chunk = LANES // query_count
    lane = row_of((EXTRA, LANES), 1)
    tile_row = row_of((EXTRA, LANES), 0)

    copies[0].wait()
    found = [jnp.zeros((EXTRA, LANES), jnp.float32) for _ in range(-(-sources // EXTRA))]
    for source in range(sources):
        code = got[source, slot_rows + shared_rows :, :LANES].astype(jnp.float32)
        found[source // EXTRA] = jnp.where(tile_row == source % EXTRA, code, found[source // EXTRA])
    found = found[0] if len(found) == 1 else jnp.concatenate(found, axis=0)
    to_scalars(found.astype(jnp.int32), decoded, table, sems.at[5])

    count = 0
    chunks = [jnp.full((EXTRA, LANES), -1, jnp.int32) for _ in range(-(-slots // per_chunk))]
    for slot in range(slots):
        image, entry = table[slot // depth, slot % depth], table[slot // depth, EXTRA + slot % depth]
        query = lax.div(jnp.maximum(entry, 0), top_count)
        at = slot % per_chunk * query_count + query
        chunks[slot // per_chunk] = jnp.where(lane == at, image, chunks[slot // per_chunk])
        listed[count] = slot
        count = count + jnp.where(image >= 0, 1, 0)
    last = listed[jnp.maximum(count - 1, 0)]
    for g in range(UNROLL):
        listed[count + g] = last

    queries = jnp.concatenate(
        [
            jnp.concatenate(
                [
                    got[source, slot_rows + c * size : slot_rows + (c + 1) * size, :]
                    for c in range(columns // LANES)
                ],
                axis=1,
            )
            for source in range(sources)
        ],
        axis=0,
    )
    missing = len(chunks) * LANES - queries.shape[0]
    if missing:
        queries = jnp.concatenate([queries, jnp.zeros((missing, queries.shape[1]), queries.dtype)], axis=0)
    copies[1].wait()
    stats = index_stats(queries, slab, jnp.concatenate([chunk[:1] for chunk in chunks], axis=1), logits)
    for c in range(len(chunks)):
        tiles = [split_rows(stat[:, c * LANES : (c + 1) * LANES]) for stat in stats]
        tiles = [tiles[0], pltpu.roll(tiles[1], query_count, 1), pltpu.roll(tiles[2], 2 * query_count, 1)]
        for slot in range(c * per_chunk, min((c + 1) * per_chunk, slots)):
            source, z = slot // depth, slot % depth
            at = slot % per_chunk
            owner = owner_of(source, z, grid_y, grid_x, depth)
            place = lane // query_count
            tile = jnp.where(place == at, tiles[0], jnp.where(place == (at + 1) % per_chunk, tiles[1], tiles[2]))
            out[owner, body:, :] = tile.astype(jnp.bfloat16)

    stats_out = pltpu.make_async_copy(
        out.at[:, pl.ds(body, EXTRA), :], out_hbm.at[:, pl.ds(body, EXTRA), :], sems.at[6]
    )
    stats_out.start()

    def send(owner):
        return pltpu.make_async_copy(out.at[owner, pl.ds(0, body), :], out_hbm.at[owner, pl.ds(0, body), :], sems.at[7])

    copies[2].wait()
    copies[3].wait()
    copies[4].wait()
    spans = []
    at = 0
    while at < columns:
        width = min(2 * LANES, columns - at)
        lane_head = row_of((rows, width), 1) // head_size
        spans.append((at, width, [jnp.where(lane_head == h, 1.0, 0.0) for h in range(width // head_size)]))
        at += width

    def group(index, carry):
        chosen = [listed[index * UNROLL + g] for g in range(UNROLL)]
        places = [(lax.div(slot, depth), lax.rem(slot, depth)) for slot in chosen]
        images = [table[source, z] for source, z in places]
        owners = [owner_of(source, z, grid_y, grid_x, depth) for source, z in places]
        work = [(g, span) for g in range(UNROLL) for span in spans]
        scores = []
        for g, (at, width, masks) in work:
            source, z = places[g]
            pieces = [
                got[source, pl.ds(pl.multiple_of(z * body + c * rows, rows), rows), :]
                for c in range(at // LANES, (at + width) // LANES)
            ]
            query = pieces[0] if len(pieces) == 1 else jnp.concatenate(pieces, axis=1)
            spread = jnp.concatenate([query * mask.astype(query.dtype) for mask in masks], axis=0)
            scores.append(
                lax.dot_general(
                    spread,
                    keys[images[g], :, at : at + width],
                    (((1,), (1,)), ((), ())),
                    preferred_element_type=jnp.float32,
                )
            )
        scores = [score * head_size ** (-0.5) for score in scores]
        highest = [jnp.max(score, axis=-1, keepdims=True) for score in scores]
        powers = [jnp.exp(score - top) for score, top in zip(scores, highest)]
        totals = [jnp.sum(power, axis=-1, keepdims=True) for power in powers]
        weights = [(power / total).astype(jnp.bfloat16) for power, total in zip(powers, totals)]
        mixed = [
            jnp.dot(weight, values[images[g], :, at : at + width], preferred_element_type=jnp.float32)
            for weight, (g, (at, width, _)) in zip(weights, work)
        ]
        for mix, (g, (at, width, masks)) in zip(mixed, work):
            context = mix[:rows] * masks[0]
            for h in range(1, len(masks)):
                context = context + mix[h * rows : (h + 1) * rows] * masks[h]
            context = context.astype(jnp.bfloat16)
            for c in range(width // LANES):
                out[owners[g], (at // LANES + c) * rows : (at // LANES + c + 1) * rows, :] = context[
                    :, c * LANES : (c + 1) * LANES
                ]
        for owner in owners:
            send(owner).start()
        return carry

    def drain(index, carry):
        for _ in range(UNROLL):
            send(0).wait()
        return carry

    groups = lax.div(count + UNROLL - 1, UNROLL)
    lax.fori_loop(0, groups, group, 0)
    lax.fori_loop(0, groups, drain, 0)
    stats_out.wait()


def serve(got, slab, keys, values, grid_y, grid_x, depth, rows, query_count, top_count, head_size):
    sources = got.shape[0]
    slots = sources * depth
    body = keys.shape[2] // LANES * rows
    lanes = -(-slots * query_count // LANES) * LANES
    operands = [got, slab, keys, values]
    codes = (-(-sources // EXTRA) * EXTRA, LANES)
    return pl.pallas_call(
        functools.partial(
            serve_kernel,
            grid_y=grid_y,
            grid_x=grid_x,
            depth=depth,
            rows=rows,
            query_count=query_count,
            top_count=top_count,
            head_size=head_size,
        ),
        grid=(1,),
        in_specs=[pl.BlockSpec(memory_space=pltpu.HBM)] * 4,
        out_specs=pl.BlockSpec(memory_space=pltpu.HBM),
        scratch_shapes=[pltpu.VMEM((slots, body + EXTRA, LANES), jnp.bfloat16)]
        + [pltpu.VMEM(a.shape, a.dtype) for a in operands]
        + [
            pltpu.VMEM((slab.shape[0], lanes), jnp.float32),
            pltpu.VMEM(codes, jnp.int32),
            pltpu.SMEM(codes, jnp.int32),
            pltpu.SMEM((slots + UNROLL,), jnp.int32),
            pltpu.SemaphoreType.DMA((8,)),
        ],
        out_shape=pltpu.HBM((slots, body + EXTRA, LANES), jnp.bfloat16),
        compiler_params=pltpu.CompilerParams(vmem_limit_bytes=VMEM_LIMIT),
        cost_estimate=pl.CostEstimate(flops=8 << 30, bytes_accessed=14 << 20, transcendentals=2 << 20),
        name="serve",
    )(*[in_hbm(a) for a in operands])


def finish_kernel(
    shards, place, back_hbm, text_hbm, w_out_hbm, gain_hbm, found, out_hbm,
    exact, gathered, back, sent, text, w_out, gain, out, sems, *, top_count, query_count, chunks, shift
):
    rows, width = text.shape[1:]
    body = back.shape[1]
    entries = query_count * top_count // chunks
    queries = query_count // chunks

    def fetch(entry, chunk):
        return pltpu.make_async_copy(back_hbm.at[shards[entry], pl.ds(0, body), :], back.at[entry], sems.at[chunk])

    loads = [
        pltpu.make_async_copy(source, target, sems.at[chunks + i])
        for i, (source, target) in enumerate(
            [
                (back_hbm.at[:, pl.ds(body, EXTRA), :], sent),
                (w_out_hbm, w_out),
                (text_hbm, text),
                (gain_hbm, gain),
            ]
        )
    ]
    for load in loads:
        load.start()
    for chunk in range(chunks):
        for entry in range(chunk * entries, (chunk + 1) * entries):
            fetch(entry, chunk).start()

    loads[0].wait()
    parts = sent[...].astype(jnp.float32)
    joined = jnp.sum(jnp.where(row_of(parts.shape, 1) < 3, parts, 0.0), axis=1)
    joined = pltpu.roll(joined, lax.rem(LANES - place[0] * query_count, LANES), 1)
    exact[...] = joined
    peak = jnp.max(joined, axis=0, keepdims=True)
    scaled = jnp.exp(joined - peak) * pltpu.roll(joined, LANES - query_count, 1)
    total = jnp.sum(scaled, axis=0, keepdims=True)
    total = jnp.where(row_of(total.shape, 1) < query_count, total, 1.0)
    normalizers = peak + jnp.log(total)
    for query in range(query_count):
        picked = jnp.concatenate([exact[pl.ds(shards[query * top_count + k], 1), :] for k in range(top_count)], axis=0)
        lane = row_of(picked.shape, 1)
        candidate = jnp.sum(jnp.where(lane == 2 * query_count + query, picked, 0.0), axis=1, keepdims=True)
        result = candidate - normalizers[:, query : query + 1] + shift
        result = jnp.sum(jnp.where(lane == row_of(picked.shape, 0), result, 0.0), axis=0, keepdims=True)
        found[query : query + 1, :] = result[:, :top_count]

    for load in loads[1:]:
        load.wait()
    stores = []
    for chunk in range(chunks):
        first = chunk * queries
        for entry in range(chunk * entries, (chunk + 1) * entries):
            fetch(entry, chunk).wait()
        for k in range(entries):
            for j in range(body // rows):
                gathered[chunk, k * rows : (k + 1) * rows, j * LANES : (j + 1) * LANES] = back[
                    chunk * entries + k, j * rows : (j + 1) * rows, :
                ]
        mixed = jnp.dot(gathered[chunk], w_out[...], preferred_element_type=jnp.float32)
        states = text[first : first + queries].astype(jnp.float32).reshape(queries, 1, rows, width)
        summed = mixed.reshape(queries, top_count, rows, width) + states
        mean = jnp.mean(summed, axis=-1, keepdims=True)
        centred = summed - mean
        variance = jnp.mean(centred * centred, axis=-1, keepdims=True)
        normed = centred * lax.rsqrt(variance + EPSILON) * gain[...].reshape(1, 1, 1, width)
        out[first : first + queries] = normed.astype(jnp.bfloat16)
        store = pltpu.make_async_copy(
            out.at[pl.ds(first, queries)], out_hbm.at[pl.ds(first, queries)], sems.at[chunks + 4 + chunk]
        )
        store.start()
        stores.append(store)
    for store in stores:
        store.wait()


def finish(shards, place, back, text, w_out, gain, top_count, shift):
    query_count, rows, width = text.shape
    chunks = 2
    body = back.shape[1] - EXTRA
    entries = query_count * top_count
    return pl.pallas_call(
        functools.partial(finish_kernel, top_count=top_count, query_count=query_count, chunks=chunks, shift=shift),
        grid_spec=pltpu.PrefetchScalarGridSpec(
            num_scalar_prefetch=2,
            grid=(1,),
            in_specs=[pl.BlockSpec(memory_space=pltpu.HBM)] * 4,
            out_specs=[
                pl.BlockSpec((query_count, top_count), lambda i, *_: (0, 0)),
                pl.BlockSpec(memory_space=pltpu.HBM),
            ],
            scratch_shapes=[
                pltpu.VMEM((back.shape[0], LANES), jnp.float32),
                pltpu.VMEM((chunks, entries // chunks * rows, width), jnp.bfloat16),
                pltpu.VMEM((entries, body, LANES), jnp.bfloat16),
                pltpu.VMEM((back.shape[0], EXTRA, LANES), jnp.bfloat16),
                pltpu.VMEM(text.shape, text.dtype),
                pltpu.VMEM(w_out.shape, w_out.dtype),
                pltpu.VMEM(gain.shape, gain.dtype),
                pltpu.VMEM((query_count, top_count, rows, width), jnp.bfloat16),
                pltpu.SemaphoreType.DMA((2 * chunks + 4,)),
            ],
        ),
        out_shape=[
            jax.ShapeDtypeStruct((query_count, top_count), jnp.float32),
            pltpu.HBM((query_count, top_count, rows, width), jnp.bfloat16),
        ],
        compiler_params=pltpu.CompilerParams(vmem_limit_bytes=VMEM_LIMIT),
        cost_estimate=pl.CostEstimate(
            flops=2 * entries * rows * width * width, bytes_accessed=7 << 20, transcendentals=0
        ),
        name="finish",
    )(shards, place, in_hbm(back), in_hbm(text), in_hbm(w_out), in_hbm(gain))


def project_rows(rows_in, weight):
    return jnp.einsum("spc,cd->spd", rows_in, weight, preferred_element_type=jnp.float32).astype(jnp.bfloat16)


def on_device(queries, slab, cand_ids, patches, text_states, w_query, w_key, w_value, w_out, norm_gain):
    shard_count = lax.axis_size("shard")
    shard_here = lax.axis_index("shard")
    core = lax.axis_index("rep")
    grid_y, depth, grid_x = GRIDS[shard_count]
    query_count = queries.shape[0]
    slab_count = slab.shape[0]
    top_count = cand_ids.shape[1]
    list_length = query_count * top_count
    text_count, model_width = text_states.shape[1:]
    head_size = model_width // HEADS
    here_x, here_z, here_y = shard_here % grid_x, shard_here // grid_x % depth, shard_here // (grid_x * depth)
    owned = depth // PAIR
    columns = [
        [(y * depth + k * PAIR + in_pair) * grid_x + x for k in range(owned)]
        for y in range(grid_y)
        for x in range(grid_x)
        for in_pair in range(PAIR)
    ]
    pairs = [
        [
            (y * depth + k * PAIR + in_pair) * grid_x + x
            for in_pair in range(PAIR)
            for y in range(grid_y)
            for x in range(grid_x)
        ]
        for k in range(owned)
    ]
    swap = [(0, 1), (1, 0)]
    w_query_other = lax.ppermute(w_query, "rep", swap)
    own_list = cand_ids.reshape(list_length)
    own_anchor = own_list // slab_count
    sent = pack(cand_ids, text_states.reshape(query_count * text_count, model_width), queries, slab_count)
    owners = lax.all_gather(sent, "shard", axis=0, tiled=True, axis_index_groups=columns)
    request = make_request(
        (here_z // PAIR * PAIR).reshape(1),
        owners.reshape(owned, sent.shape[0], model_width),
        w_query,
        w_query_other,
        grid_y,
        grid_x,
        text_count,
        query_count,
        top_count,
    )
    got = lax.all_to_all(request, "shard", split_axis=0, concat_axis=0, tiled=True, axis_index_groups=pairs)

    keys = project_rows(patches, jnp.concatenate([w_key, lax.ppermute(w_key, "rep", swap)], axis=1))
    values = project_rows(patches, jnp.concatenate([w_value, lax.ppermute(w_value, "rep", swap)], axis=1))
    w_out_other = lax.ppermute(w_out, "rep", swap)
    half = model_width // 2
    w_out_whole = jnp.where(
        core == 0,
        jnp.concatenate([w_out, w_out_other], axis=1),
        jnp.concatenate(
            [
                jnp.concatenate([w_out_other[half:], w_out[half:]], axis=1),
                jnp.concatenate([w_out_other[:half], w_out[:half]], axis=1),
            ],
            axis=0,
        ),
    )

    context = serve(
        got, slab, keys, values, grid_y, grid_x, owned, text_count, query_count, top_count, head_size
    )
    back = lax.all_to_all(context, "shard", split_axis=0, concat_axis=0, tiled=True)

    source = (here_z % PAIR * grid_y + here_y) * grid_x + here_x
    place = (source * owned + here_z // PAIR) % (LANES // query_count)
    retrieval, attended = finish(
        own_anchor,
        place.reshape(1),
        back,
        text_states,
        w_out_whole,
        norm_gain.reshape(1, model_width),
        top_count,
        math.log(slab_count * shard_count),
    )
    return (retrieval, attended)


def solution(mesh):
    in_specs = (
        P(("shard", "rep"), None),
        P("shard", None),
        P(("shard", "rep"), None),
        P("shard", None, None),
        P(("shard", "rep"), None, None),
        P(None, "rep"),
        P(None, "rep"),
        P(None, "rep"),
        P(None, "rep"),
        P(),
    )
    out_specs = (P(("shard", "rep"), None), P(("shard", "rep"), None, None, None))
    return jax.shard_map(
        on_device, mesh=mesh, in_specs=in_specs, out_specs=out_specs, check_vma=False
    )
```

```python
import functools
import math

import jax
import jax.numpy as jnp
from jax import lax
from jax.experimental import pallas as pl
from jax.experimental.pallas import tpu as pltpu
from jax.sharding import PartitionSpec as P

HEADS = 12
SCALE = 100.0
EPSILON = 1e-06
LANES = 128
EXTRA = 8
UNROLL = 16
PAIR = 2
GRIDS = {128: (4, 8, 4), 8: (2, 2, 2)}
VMEM_LIMIT = 40 * 1024 * 1024


def row_of(shape, dim):
    return lax.broadcasted_iota(jnp.int32, shape, dim)


def split_source(source, grid_y, grid_x):
    if isinstance(source, int):
        return source // (grid_y * grid_x), source // grid_x % grid_y, source % grid_x
    return lax.div(source, grid_y * grid_x), lax.rem(lax.div(source, grid_x), grid_y), lax.rem(source, grid_x)


def owner_of(source, k, grid_y, grid_x, owned):
    in_pair, y, x = split_source(source, grid_y, grid_x)
    return (y * owned * PAIR + k * PAIR + in_pair) * grid_x + x


def in_vmem(array):
    return pltpu.with_memory_space_constraint(array, pltpu.VMEM)


def in_hbm(array):
    return pltpu.with_memory_space_constraint(array, pltpu.HBM)


def pack_kernel(ids_hbm, text_hbm, queries_hbm, out, ids, queries, sems, *, slab_count):
    rows = text_hbm.shape[0]
    copies = [
        pltpu.make_async_copy(ids_hbm, ids, sems.at[0]),
        pltpu.make_async_copy(queries_hbm, queries, sems.at[1]),
        pltpu.make_async_copy(text_hbm, out.at[pl.ds(0, rows), :], sems.at[2]),
    ]
    for copy in copies:
        copy.start()
    count, width = queries.shape
    lane = row_of((EXTRA, LANES), 1)
    image = jnp.full((EXTRA, LANES), -1, jnp.int32)
    listed = image
    copies[0].wait()
    for entry in range(ids.shape[0] * ids.shape[1]):
        row = ids[entry // ids.shape[1], entry % ids.shape[1]]
        here = lane == lax.div(row, slab_count)
        image = jnp.where(here, lax.rem(row, slab_count), image)
        listed = jnp.where(here, entry, listed)
    copies[1].wait()
    pieces = [queries[...].astype(jnp.float32)]
    if count < EXTRA:
        pieces.append(jnp.zeros((EXTRA - count, width), jnp.float32))
    code = [image.astype(jnp.float32), listed.astype(jnp.float32)]
    code.append(jnp.zeros((EXTRA, width - 2 * LANES), jnp.float32))
    pieces.append(jnp.concatenate(code, axis=1))
    out[rows:, :] = jnp.concatenate(pieces, axis=0).astype(jnp.bfloat16)
    copies[2].wait()


def pack(ids, text, queries, slab_count):
    rows, width = text.shape
    return pl.pallas_call(
        functools.partial(pack_kernel, slab_count=slab_count),
        in_specs=[pl.BlockSpec(memory_space=pltpu.HBM)] * 3,
        out_specs=pl.BlockSpec(memory_space=pltpu.VMEM),
        scratch_shapes=[
            pltpu.SMEM(ids.shape, ids.dtype),
            pltpu.VMEM(queries.shape, queries.dtype),
            pltpu.SemaphoreType.DMA((3,)),
        ],
        out_shape=jax.ShapeDtypeStruct((rows + 2 * EXTRA, width), jnp.bfloat16),
        compiler_params=pltpu.CompilerParams(vmem_limit_bytes=VMEM_LIMIT),
        cost_estimate=pl.CostEstimate(flops=1 << 20, bytes_accessed=1 << 18, transcendentals=0),
        name="pack",
    )(in_hbm(ids), in_hbm(text), in_hbm(queries))


def to_scalars(vectors, decoded, table, sem):
    decoded[...] = vectors
    copy = pltpu.make_async_copy(decoded, table, sem)
    copy.start()
    copy.wait()


def request_kernel(
    place, owners, w_own, w_other, out, decoded, table, projected, shared, sem,
    *, grid_y, grid_x, rows, query_count, top_count
):
    step = pl.program_id(0)
    depth, height, width = owners.shape
    texts = height - 2 * EXTRA
    body = projected.shape[1]
    tile_row = row_of((EXTRA, LANES), 0)

    @pl.when(step == 0)
    def _():
        found = [jnp.zeros((EXTRA, LANES), jnp.float32) for _ in range(2)]
        for z in range(depth):
            code = owners[z, texts + EXTRA :, : 2 * LANES].astype(jnp.float32)
            found = [jnp.where(tile_row == z, code[:, i * LANES : (i + 1) * LANES], found[i]) for i in range(2)]
        decoded[...] = jnp.concatenate(found, axis=0).astype(jnp.int32)
        copy = pltpu.make_async_copy(decoded, table, sem)
        copy.start()
        states = owners[:, :texts, :].reshape(depth * texts, width)
        at = 0
        for weight in (w_own, w_other):
            half = jnp.dot(states, weight[...], preferred_element_type=jnp.float32).astype(jnp.bfloat16)
            for c in range(half.shape[1] // LANES):
                for t in range(depth * query_count):
                    projected[t, at : at + rows, :] = half[t * rows : (t + 1) * rows, c * LANES : (c + 1) * LANES]
                at += rows
        picked = [owners[z, texts : texts + EXTRA, :].astype(jnp.float32)[:query_count] for z in range(depth)]
        picked = jnp.concatenate(picked, axis=0).astype(jnp.bfloat16)
        for c in range(width // LANES):
            size = depth * query_count
            shared[c * size : (c + 1) * size, :] = picked[:, c * LANES : (c + 1) * LANES]
        copy.wait()

    lane = row_of((EXTRA, LANES), 1)
    for i in range(out.shape[0]):
        target = step * out.shape[0] + i
        in_pair, y, x = split_source(target, grid_y, grid_x)
        shard = (y * depth * PAIR + place[0] + in_pair) * grid_x + x
        code = jnp.full((EXTRA, LANES), -1.0, jnp.float32)
        for z in range(depth):
            image, listed = table[z, shard], table[EXTRA + z, shard]
            query = lax.div(jnp.maximum(listed, 0), top_count)
            out[i, z * body : (z + 1) * body, :] = projected[z * query_count + query]
            code = jnp.where(lane == z, image.astype(jnp.float32), code)
            code = jnp.where(lane == EXTRA + z, listed.astype(jnp.float32), code)
        out[i, depth * body : depth * body + shared.shape[0], :] = shared[...]
        out[i, depth * body + shared.shape[0] :, :] = code.astype(jnp.bfloat16)


def make_request(place, owners, w_own, w_other, grid_y, grid_x, rows, query_count, top_count):
    depth, height, width = owners.shape
    body = width // LANES * rows
    shared_rows = depth * query_count * (width // LANES)
    total = depth * body + shared_rows + EXTRA
    targets = PAIR * grid_y * grid_x
    block = min(8, targets)
    whole = lambda a: pl.BlockSpec(a.shape, lambda i, *_: (0,) * a.ndim)
    return pl.pallas_call(
        functools.partial(
            request_kernel,
            grid_y=grid_y,
            grid_x=grid_x,
            rows=rows,
            query_count=query_count,
            top_count=top_count,
        ),
        grid_spec=pltpu.PrefetchScalarGridSpec(
            num_scalar_prefetch=1,
            grid=(targets // block,),
            in_specs=[whole(owners), whole(w_own), whole(w_other)],
            out_specs=pl.BlockSpec((block, total, LANES), lambda i, *_: (i, 0, 0)),
            scratch_shapes=[
                pltpu.VMEM((2 * EXTRA, LANES), jnp.int32),
                pltpu.SMEM((2 * EXTRA, LANES), jnp.int32),
                pltpu.VMEM((depth * query_count, body, LANES), jnp.bfloat16),
                pltpu.VMEM((shared_rows, LANES), jnp.bfloat16),
                pltpu.SemaphoreType.DMA,
            ],
        ),
        out_shape=pltpu.HBM((targets, total, LANES), jnp.bfloat16),
        compiler_params=pltpu.CompilerParams(vmem_limit_bytes=VMEM_LIMIT),
        cost_estimate=pl.CostEstimate(flops=1 << 29, bytes_accessed=6 << 20, transcendentals=0),
        name="request",
    )(place, in_hbm(owners), in_hbm(w_own), w_other)


def index_stats(query, slab, picked, logits):
    count = query.shape[0]
    tile = min(256, slab.shape[0])
    peak = None
    for t in range(slab.shape[0] // tile):
        part = SCALE * lax.dot_general(
            slab[t * tile : (t + 1) * tile, :], query, (((1,), (1,)), ((), ())), preferred_element_type=jnp.float32
        )
        logits[t * tile : (t + 1) * tile, :] = part
        top = jnp.max(part, axis=0, keepdims=True)
        peak = top if peak is None else jnp.maximum(peak, top)
    total = jnp.zeros_like(peak)
    for t in range(slab.shape[0] // tile):
        total = total + jnp.sum(jnp.exp(logits[t * tile : (t + 1) * tile, :] - peak), axis=0, keepdims=True)
    chosen = row_of((tile, count), 0) == picked
    candidate = jnp.sum(jnp.where(chosen, logits[:tile, :], 0.0), axis=0, keepdims=True)
    return peak, total, candidate


def split_rows(exact):
    tile_row = row_of((EXTRA, LANES), 0)
    exact = jnp.broadcast_to(exact, (EXTRA, LANES))
    high = exact.astype(jnp.bfloat16).astype(jnp.float32)
    left = exact - high
    middle = left.astype(jnp.bfloat16).astype(jnp.float32)
    parts = jnp.where(tile_row == 0, high, jnp.where(tile_row == 1, middle, left - middle))
    return jnp.where(tile_row < 3, parts, 0.0)


def serve_kernel(
    got, slab_hbm, keys_hbm, values_hbm, out_hbm,
    out, slab, keys, values, logits, decoded, table, listed, sems, *, grid_y, grid_x, depth, rows, query_count, top_count, head_size
):
    sources = got.shape[0]
    slots = sources * depth
    columns = keys.shape[2]
    body = columns // LANES * rows
    slot_rows = depth * body
    copies = [
        pltpu.make_async_copy(source, target, sems.at[i])
        for i, (source, target) in enumerate(
            [(slab_hbm, slab), (keys_hbm, keys), (values_hbm, values)]
        )
    ]
    for copy in copies:
        copy.start()
    size = depth * query_count
    shared_rows = size * (columns // LANES)
    per_chunk = LANES // query_count
    lane = row_of((EXTRA, LANES), 1)
    tile_row = row_of((EXTRA, LANES), 0)

    found = [jnp.zeros((EXTRA, LANES), jnp.float32) for _ in range(-(-sources // EXTRA))]
    for source in range(sources):
        code = got[source, slot_rows + shared_rows :, :LANES].astype(jnp.float32)
        found[source // EXTRA] = jnp.where(tile_row == source % EXTRA, code, found[source // EXTRA])
    found = found[0] if len(found) == 1 else jnp.concatenate(found, axis=0)
    to_scalars(found.astype(jnp.int32), decoded, table, sems.at[5])

    count = 0
    chunks = [jnp.full((EXTRA, LANES), -1, jnp.int32) for _ in range(-(-slots // per_chunk))]
    for slot in range(slots):
        image, entry = table[slot // depth, slot % depth], table[slot // depth, EXTRA + slot % depth]
        query = lax.div(jnp.maximum(entry, 0), top_count)
        at = slot % per_chunk * query_count + query
        chunks[slot // per_chunk] = jnp.where(lane == at, image, chunks[slot // per_chunk])
        listed[count] = slot
        count = count + jnp.where(image >= 0, 1, 0)
    last = listed[jnp.maximum(count - 1, 0)]
    for g in range(UNROLL):
        listed[count + g] = last

    queries = jnp.concatenate(
        [
            jnp.concatenate(
                [
                    got[source, slot_rows + c * size : slot_rows + (c + 1) * size, :]
                    for c in range(columns // LANES)
                ],
                axis=1,
            )
            for source in range(sources)
        ],
        axis=0,
    )
    missing = len(chunks) * LANES - queries.shape[0]
    if missing:
        queries = jnp.concatenate([queries, jnp.zeros((missing, queries.shape[1]), queries.dtype)], axis=0)
    copies[0].wait()
    stats = index_stats(queries, slab, jnp.concatenate([chunk[:1] for chunk in chunks], axis=1), logits)
    for c in range(len(chunks)):
        tiles = [split_rows(stat[:, c * LANES : (c + 1) * LANES]) for stat in stats]
        tiles = [tiles[0], pltpu.roll(tiles[1], query_count, 1), pltpu.roll(tiles[2], 2 * query_count, 1)]
        for slot in range(c * per_chunk, min((c + 1) * per_chunk, slots)):
            source, z = slot // depth, slot % depth
            at = slot % per_chunk
            owner = owner_of(source, z, grid_y, grid_x, depth)
            place = lane // query_count
            tile = jnp.where(place == at, tiles[0], jnp.where(place == (at + 1) % per_chunk, tiles[1], tiles[2]))
            out[owner, body:, :] = tile.astype(jnp.bfloat16)

    stats_out = pltpu.make_async_copy(
        out.at[:, pl.ds(body, EXTRA), :], out_hbm.at[:, pl.ds(body, EXTRA), :], sems.at[6]
    )
    stats_out.start()

    def send(owner):
        return pltpu.make_async_copy(out.at[owner, pl.ds(0, body), :], out_hbm.at[owner, pl.ds(0, body), :], sems.at[7])

    copies[1].wait()
    copies[2].wait()
    spans = []
    at = 0
    while at < columns:
        width = min(2 * LANES, columns - at)
        lane_head = row_of((rows, width), 1) // head_size
        spans.append((at, width, [jnp.where(lane_head == h, 1.0, 0.0) for h in range(width // head_size)]))
        at += width

    def group(index, carry):
        chosen = [listed[index * UNROLL + g] for g in range(UNROLL)]
        places = [(lax.div(slot, depth), lax.rem(slot, depth)) for slot in chosen]
        images = [table[source, z] for source, z in places]
        owners = [owner_of(source, z, grid_y, grid_x, depth) for source, z in places]
        work = [(g, span) for g in range(UNROLL) for span in spans]
        scores = []
        for g, (at, width, masks) in work:
            source, z = places[g]
            pieces = [
                got[source, pl.ds(pl.multiple_of(z * body + c * rows, rows), rows), :]
                for c in range(at // LANES, (at + width) // LANES)
            ]
            query = pieces[0] if len(pieces) == 1 else jnp.concatenate(pieces, axis=1)
            spread = jnp.concatenate([query * mask.astype(query.dtype) for mask in masks], axis=0)
            scores.append(
                lax.dot_general(
                    spread,
                    keys[images[g], :, at : at + width],
                    (((1,), (1,)), ((), ())),
                    preferred_element_type=jnp.float32,
                )
            )
        scores = [score * head_size ** (-0.5) for score in scores]
        highest = [jnp.max(score, axis=-1, keepdims=True) for score in scores]
        powers = [jnp.exp(score - top) for score, top in zip(scores, highest)]
        totals = [jnp.sum(power, axis=-1, keepdims=True) for power in powers]
        inverses = [1.0 / total for total in totals]
        weights = [(power * inverse).astype(jnp.bfloat16) for power, inverse in zip(powers, inverses)]
        mixed = [
            jnp.dot(weight, values[images[g], :, at : at + width], preferred_element_type=jnp.float32)
            for weight, (g, (at, width, _)) in zip(weights, work)
        ]
        for mix, (g, (at, width, masks)) in zip(mixed, work):
            context = mix[:rows]
            for h in range(1, len(masks)):
                context = jnp.where(masks[h] > 0.5, mix[h * rows : (h + 1) * rows], context)
            context = context.astype(jnp.bfloat16)
            for c in range(width // LANES):
                out[owners[g], (at // LANES + c) * rows : (at // LANES + c + 1) * rows, :] = context[
                    :, c * LANES : (c + 1) * LANES
                ]
        for owner in owners:
            send(owner).start()
        return carry

    def drain(index, carry):
        for _ in range(UNROLL):
            send(0).wait()
        return carry

    groups = lax.div(count + UNROLL - 1, UNROLL)
    lax.fori_loop(0, groups, group, 0)
    lax.fori_loop(0, groups, drain, 0)
    stats_out.wait()


def serve(got, slab, keys, values, grid_y, grid_x, depth, rows, query_count, top_count, head_size):
    sources = got.shape[0]
    slots = sources * depth
    body = keys.shape[2] // LANES * rows
    lanes = -(-slots * query_count // LANES) * LANES
    operands = [got, slab, keys, values]
    codes = (-(-sources // EXTRA) * EXTRA, LANES)
    return pl.pallas_call(
        functools.partial(
            serve_kernel,
            grid_y=grid_y,
            grid_x=grid_x,
            depth=depth,
            rows=rows,
            query_count=query_count,
            top_count=top_count,
            head_size=head_size,
        ),
        grid=(1,),
        in_specs=[pl.BlockSpec(memory_space=pltpu.VMEM)] + [pl.BlockSpec(memory_space=pltpu.HBM)] * 3,
        out_specs=pl.BlockSpec(memory_space=pltpu.HBM),
        scratch_shapes=[pltpu.VMEM((slots, body + EXTRA, LANES), jnp.bfloat16)]
        + [pltpu.VMEM(a.shape, a.dtype) for a in operands[1:]]
        + [
            pltpu.VMEM((slab.shape[0], lanes), jnp.float32),
            pltpu.VMEM(codes, jnp.int32),
            pltpu.SMEM(codes, jnp.int32),
            pltpu.SMEM((slots + UNROLL,), jnp.int32),
            pltpu.SemaphoreType.DMA((8,)),
        ],
        out_shape=pltpu.HBM((slots, body + EXTRA, LANES), jnp.bfloat16),
        compiler_params=pltpu.CompilerParams(vmem_limit_bytes=VMEM_LIMIT),
        cost_estimate=pl.CostEstimate(flops=8 << 30, bytes_accessed=14 << 20, transcendentals=2 << 20),
        name="serve",
    )(in_vmem(got), *[in_hbm(a) for a in operands[1:]])


def finish_kernel(
    shards, place, back, text_hbm, w_out_hbm, gain_hbm, found, out_hbm,
    exact, gathered, text, w_out, gain, out, sems, *, top_count, query_count, chunks, shift
):
    rows, width = text.shape[1:]
    body = back.shape[1] - EXTRA
    entries = query_count * top_count // chunks
    queries = query_count // chunks

    loads = [
        pltpu.make_async_copy(source, target, sems.at[i])
        for i, (source, target) in enumerate([(w_out_hbm, w_out), (text_hbm, text), (gain_hbm, gain)])
    ]
    for load in loads:
        load.start()
    parts = back[:, body:, :].astype(jnp.float32)
    joined = jnp.sum(jnp.where(row_of(parts.shape, 1) < 3, parts, 0.0), axis=1)
    joined = pltpu.roll(joined, lax.rem(LANES - place[0] * query_count, LANES), 1)
    exact[...] = joined
    peak = jnp.max(joined, axis=0, keepdims=True)
    scaled = jnp.exp(joined - peak) * pltpu.roll(joined, LANES - query_count, 1)
    total = jnp.sum(scaled, axis=0, keepdims=True)
    total = jnp.where(row_of(total.shape, 1) < query_count, total, 1.0)
    normalizers = peak + jnp.log(total)
    for query in range(query_count):
        picked = jnp.concatenate([exact[pl.ds(shards[query * top_count + k], 1), :] for k in range(top_count)], axis=0)
        lane = row_of(picked.shape, 1)
        candidate = jnp.sum(jnp.where(lane == 2 * query_count + query, picked, 0.0), axis=1, keepdims=True)
        result = candidate - normalizers[:, query : query + 1] + shift
        result = jnp.sum(jnp.where(lane == row_of(picked.shape, 0), result, 0.0), axis=0, keepdims=True)
        found[query : query + 1, :] = result[:, :top_count]

    for load in loads:
        load.wait()
    stores = []
    for chunk in range(chunks):
        first = chunk * queries
        for k in range(entries):
            shard = shards[chunk * entries + k]
            for j in range(body // rows):
                gathered[chunk, k * rows : (k + 1) * rows, j * LANES : (j + 1) * LANES] = back[
                    shard, j * rows : (j + 1) * rows, :
                ]
        mixed = jnp.dot(gathered[chunk], w_out[...], preferred_element_type=jnp.float32)
        states = text[first : first + queries].astype(jnp.float32).reshape(queries, 1, rows, width)
        summed = mixed.reshape(queries, top_count, rows, width) + states
        mean = jnp.mean(summed, axis=-1, keepdims=True)
        centred = summed - mean
        variance = jnp.mean(centred * centred, axis=-1, keepdims=True)
        normed = centred * lax.rsqrt(variance + EPSILON) * gain[...].reshape(1, 1, 1, width)
        out[first : first + queries] = normed.astype(jnp.bfloat16)
        store = pltpu.make_async_copy(
            out.at[pl.ds(first, queries)], out_hbm.at[pl.ds(first, queries)], sems.at[3 + chunk]
        )
        store.start()
        stores.append(store)
    for store in stores:
        store.wait()


def finish(shards, place, back, text, w_out, gain, top_count, shift):
    query_count, rows, width = text.shape
    chunks = 2
    body = back.shape[1] - EXTRA
    entries = query_count * top_count
    return pl.pallas_call(
        functools.partial(finish_kernel, top_count=top_count, query_count=query_count, chunks=chunks, shift=shift),
        grid_spec=pltpu.PrefetchScalarGridSpec(
            num_scalar_prefetch=2,
            grid=(1,),
            in_specs=[pl.BlockSpec(memory_space=pltpu.VMEM)] + [pl.BlockSpec(memory_space=pltpu.HBM)] * 3,
            out_specs=[
                pl.BlockSpec((query_count, top_count), lambda i, *_: (0, 0)),
                pl.BlockSpec(memory_space=pltpu.HBM),
            ],
            scratch_shapes=[
                pltpu.VMEM((back.shape[0], LANES), jnp.float32),
                pltpu.VMEM((chunks, entries // chunks * rows, width), jnp.bfloat16),
                pltpu.VMEM(text.shape, text.dtype),
                pltpu.VMEM(w_out.shape, w_out.dtype),
                pltpu.VMEM(gain.shape, gain.dtype),
                pltpu.VMEM((query_count, top_count, rows, width), jnp.bfloat16),
                pltpu.SemaphoreType.DMA((chunks + 3,)),
            ],
        ),
        out_shape=[
            jax.ShapeDtypeStruct((query_count, top_count), jnp.float32),
            pltpu.HBM((query_count, top_count, rows, width), jnp.bfloat16),
        ],
        compiler_params=pltpu.CompilerParams(vmem_limit_bytes=VMEM_LIMIT),
        cost_estimate=pl.CostEstimate(
            flops=2 * entries * rows * width * width, bytes_accessed=7 << 20, transcendentals=0
        ),
        name="finish",
    )(shards, place, in_vmem(back), in_hbm(text), in_hbm(w_out), in_hbm(gain))


def project_rows(rows_in, weight):
    return jnp.einsum("spc,cd->spd", rows_in, weight, preferred_element_type=jnp.float32).astype(jnp.bfloat16)


def on_device(queries, slab, cand_ids, patches, text_states, w_query, w_key, w_value, w_out, norm_gain):
    shard_count = lax.axis_size("shard")
    shard_here = lax.axis_index("shard")
    core = lax.axis_index("rep")
    grid_y, depth, grid_x = GRIDS[shard_count]
    query_count = queries.shape[0]
    slab_count = slab.shape[0]
    top_count = cand_ids.shape[1]
    list_length = query_count * top_count
    text_count, model_width = text_states.shape[1:]
    head_size = model_width // HEADS
    here_x, here_z, here_y = shard_here % grid_x, shard_here // grid_x % depth, shard_here // (grid_x * depth)
    owned = depth // PAIR
    columns = [
        [(y * depth + k * PAIR + in_pair) * grid_x + x for k in range(owned)]
        for y in range(grid_y)
        for x in range(grid_x)
        for in_pair in range(PAIR)
    ]
    pairs = [
        [
            (y * depth + k * PAIR + in_pair) * grid_x + x
            for in_pair in range(PAIR)
            for y in range(grid_y)
            for x in range(grid_x)
        ]
        for k in range(owned)
    ]
    swap = [(0, 1), (1, 0)]
    w_query_other = lax.ppermute(w_query, "rep", swap)
    own_list = cand_ids.reshape(list_length)
    own_anchor = own_list // slab_count
    sent = pack(cand_ids, text_states.reshape(query_count * text_count, model_width), queries, slab_count)
    owners = lax.all_gather(sent, "shard", axis=0, tiled=True, axis_index_groups=columns)
    request = make_request(
        (here_z // PAIR * PAIR).reshape(1),
        owners.reshape(owned, sent.shape[0], model_width),
        w_query,
        w_query_other,
        grid_y,
        grid_x,
        text_count,
        query_count,
        top_count,
    )
    got = lax.all_to_all(request, "shard", split_axis=0, concat_axis=0, tiled=True, axis_index_groups=pairs)

    keys = project_rows(patches, jnp.concatenate([w_key, lax.ppermute(w_key, "rep", swap)], axis=1))
    values = project_rows(patches, jnp.concatenate([w_value, lax.ppermute(w_value, "rep", swap)], axis=1))
    w_out_other = lax.ppermute(w_out, "rep", swap)
    half = model_width // 2
    w_out_whole = jnp.where(
        core == 0,
        jnp.concatenate([w_out, w_out_other], axis=1),
        jnp.concatenate(
            [
                jnp.concatenate([w_out_other[half:], w_out[half:]], axis=1),
                jnp.concatenate([w_out_other[:half], w_out[:half]], axis=1),
            ],
            axis=0,
        ),
    )

    context = serve(
        got, slab, keys, values, grid_y, grid_x, owned, text_count, query_count, top_count, head_size
    )
    back = lax.all_to_all(context, "shard", split_axis=0, concat_axis=0, tiled=True)

    source = (here_z % PAIR * grid_y + here_y) * grid_x + here_x
    place = (source * owned + here_z // PAIR) % (LANES // query_count)
    retrieval, attended = finish(
        own_anchor,
        place.reshape(1),
        back,
        text_states,
        w_out_whole,
        norm_gain.reshape(1, model_width),
        top_count,
        math.log(slab_count * shard_count),
    )
    return (retrieval, attended)


def solution(mesh):
    in_specs = (
        P(("shard", "rep"), None),
        P("shard", None),
        P(("shard", "rep"), None),
        P("shard", None, None),
        P(("shard", "rep"), None, None),
        P(None, "rep"),
        P(None, "rep"),
        P(None, "rep"),
        P(None, "rep"),
        P(),
    )
    out_specs = (P(("shard", "rep"), None), P(("shard", "rep"), None, None, None))
    return jax.shard_map(
        on_device, mesh=mesh, in_specs=in_specs, out_specs=out_specs, check_vma=False
    )
```

```python
import functools
import math

import jax
import jax.numpy as jnp
from jax import lax
from jax.experimental import pallas as pl
from jax.experimental.pallas import tpu as pltpu
from jax.sharding import PartitionSpec as P

HEADS = 12
SCALE = 100.0
EPSILON = 1e-06
LANES = 128
EXTRA = 8
UNROLL = 16
PAIR = 2
GRIDS = {128: (4, 8, 4), 8: (2, 2, 2)}
VMEM_LIMIT = 48 * 1024 * 1024


def row_of(shape, dim):
    return lax.broadcasted_iota(jnp.int32, shape, dim)


def split_source(source, grid_y, grid_x):
    if isinstance(source, int):
        return source // (grid_y * grid_x), source // grid_x % grid_y, source % grid_x
    return lax.div(source, grid_y * grid_x), lax.rem(lax.div(source, grid_x), grid_y), lax.rem(source, grid_x)


def owner_of(source, k, grid_y, grid_x, owned):
    in_pair, y, x = split_source(source, grid_y, grid_x)
    return (y * owned * PAIR + k * PAIR + in_pair) * grid_x + x


def in_hbm(array):
    return pltpu.with_memory_space_constraint(array, pltpu.HBM)


def pack_kernel(ids_hbm, text_hbm, queries_hbm, out, ids, queries, sems, *, slab_count):
    rows = text_hbm.shape[0]
    copies = [
        pltpu.make_async_copy(ids_hbm, ids, sems.at[0]),
        pltpu.make_async_copy(queries_hbm, queries, sems.at[1]),
        pltpu.make_async_copy(text_hbm, out.at[pl.ds(0, rows), :], sems.at[2]),
    ]
    for copy in copies:
        copy.start()
    count, width = queries.shape
    lane = row_of((EXTRA, LANES), 1)
    image = jnp.full((EXTRA, LANES), -1, jnp.int32)
    listed = image
    copies[0].wait()
    for entry in range(ids.shape[0] * ids.shape[1]):
        row = ids[entry // ids.shape[1], entry % ids.shape[1]]
        here = lane == lax.div(row, slab_count)
        image = jnp.where(here, lax.rem(row, slab_count), image)
        listed = jnp.where(here, entry, listed)
    copies[1].wait()
    pieces = [queries[...].astype(jnp.float32)]
    if count < EXTRA:
        pieces.append(jnp.zeros((EXTRA - count, width), jnp.float32))
    code = [image.astype(jnp.float32), listed.astype(jnp.float32)]
    code.append(jnp.zeros((EXTRA, width - 2 * LANES), jnp.float32))
    pieces.append(jnp.concatenate(code, axis=1))
    out[rows:, :] = jnp.concatenate(pieces, axis=0).astype(jnp.bfloat16)
    copies[2].wait()


def pack(ids, text, queries, slab_count):
    rows, width = text.shape
    return pl.pallas_call(
        functools.partial(pack_kernel, slab_count=slab_count),
        in_specs=[pl.BlockSpec(memory_space=pltpu.HBM)] * 3,
        out_specs=pl.BlockSpec(memory_space=pltpu.VMEM),
        scratch_shapes=[
            pltpu.SMEM(ids.shape, ids.dtype),
            pltpu.VMEM(queries.shape, queries.dtype),
            pltpu.SemaphoreType.DMA((3,)),
        ],
        out_shape=jax.ShapeDtypeStruct((rows + 2 * EXTRA, width), jnp.bfloat16),
        compiler_params=pltpu.CompilerParams(vmem_limit_bytes=VMEM_LIMIT),
        cost_estimate=pl.CostEstimate(flops=1 << 20, bytes_accessed=1 << 18, transcendentals=0),
        name="pack",
    )(in_hbm(ids), in_hbm(text), in_hbm(queries))


def to_scalars(vectors, decoded, table, sem):
    decoded[...] = vectors
    copy = pltpu.make_async_copy(decoded, table, sem)
    copy.start()
    copy.wait()


def request_kernel(
    place, owners, w_own, w_other, out, decoded, table, projected, shared, sem,
    *, grid_y, grid_x, rows, query_count, top_count
):
    step = pl.program_id(0)
    depth, height, width = owners.shape
    texts = height - 2 * EXTRA
    body = projected.shape[1]
    tile_row = row_of((EXTRA, LANES), 0)

    @pl.when(step == 0)
    def _():
        found = [jnp.zeros((EXTRA, LANES), jnp.float32) for _ in range(2)]
        for z in range(depth):
            code = owners[z, texts + EXTRA :, : 2 * LANES].astype(jnp.float32)
            found = [jnp.where(tile_row == z, code[:, i * LANES : (i + 1) * LANES], found[i]) for i in range(2)]
        decoded[...] = jnp.concatenate(found, axis=0).astype(jnp.int32)
        copy = pltpu.make_async_copy(decoded, table, sem)
        copy.start()
        states = owners[:, :texts, :].reshape(depth * texts, width)
        at = 0
        for weight in (w_own, w_other):
            half = jnp.dot(states, weight[...], preferred_element_type=jnp.float32).astype(jnp.bfloat16)
            for c in range(half.shape[1] // LANES):
                for t in range(depth * query_count):
                    projected[t, at : at + rows, :] = half[t * rows : (t + 1) * rows, c * LANES : (c + 1) * LANES]
                at += rows
        picked = [owners[z, texts : texts + EXTRA, :].astype(jnp.float32)[:query_count] for z in range(depth)]
        picked = jnp.concatenate(picked, axis=0).astype(jnp.bfloat16)
        for c in range(width // LANES):
            size = depth * query_count
            shared[c * size : (c + 1) * size, :] = picked[:, c * LANES : (c + 1) * LANES]
        copy.wait()

    lane = row_of((EXTRA, LANES), 1)
    for i in range(out.shape[0]):
        target = step * out.shape[0] + i
        in_pair, y, x = split_source(target, grid_y, grid_x)
        shard = (y * depth * PAIR + place[0] + in_pair) * grid_x + x
        code = jnp.full((EXTRA, LANES), -1.0, jnp.float32)
        for z in range(depth):
            image, listed = table[z, shard], table[EXTRA + z, shard]
            query = lax.div(jnp.maximum(listed, 0), top_count)
            out[i, z * body : (z + 1) * body, :] = projected[z * query_count + query]
            code = jnp.where(lane == z, image.astype(jnp.float32), code)
            code = jnp.where(lane == EXTRA + z, listed.astype(jnp.float32), code)
        out[i, depth * body : depth * body + shared.shape[0], :] = shared[...]
        out[i, depth * body + shared.shape[0] :, :] = code.astype(jnp.bfloat16)


def make_request(place, owners, w_own, w_other, grid_y, grid_x, rows, query_count, top_count):
    depth, height, width = owners.shape
    body = width // LANES * rows
    shared_rows = depth * query_count * (width // LANES)
    total = depth * body + shared_rows + EXTRA
    targets = PAIR * grid_y * grid_x
    block = min(8, targets)
    whole = lambda a: pl.BlockSpec(a.shape, lambda i, *_: (0,) * a.ndim)
    return pl.pallas_call(
        functools.partial(
            request_kernel,
            grid_y=grid_y,
            grid_x=grid_x,
            rows=rows,
            query_count=query_count,
            top_count=top_count,
        ),
        grid_spec=pltpu.PrefetchScalarGridSpec(
            num_scalar_prefetch=1,
            grid=(targets // block,),
            in_specs=[whole(owners), whole(w_own), whole(w_other)],
            out_specs=pl.BlockSpec((block, total, LANES), lambda i, *_: (i, 0, 0)),
            scratch_shapes=[
                pltpu.VMEM((2 * EXTRA, LANES), jnp.int32),
                pltpu.SMEM((2 * EXTRA, LANES), jnp.int32),
                pltpu.VMEM((depth * query_count, body, LANES), jnp.bfloat16),
                pltpu.VMEM((shared_rows, LANES), jnp.bfloat16),
                pltpu.SemaphoreType.DMA,
            ],
        ),
        out_shape=pltpu.HBM((targets, total, LANES), jnp.bfloat16),
        compiler_params=pltpu.CompilerParams(vmem_limit_bytes=VMEM_LIMIT),
        cost_estimate=pl.CostEstimate(flops=1 << 29, bytes_accessed=6 << 20, transcendentals=0),
        name="request",
    )(place, in_hbm(owners), in_hbm(w_own), w_other)


def index_stats(query, slab, picked, logits):
    count = query.shape[0]
    tile = min(256, slab.shape[0])
    peak = None
    for t in range(slab.shape[0] // tile):
        part = SCALE * lax.dot_general(
            slab[t * tile : (t + 1) * tile, :], query, (((1,), (1,)), ((), ())), preferred_element_type=jnp.float32
        )
        logits[t * tile : (t + 1) * tile, :] = part
        top = jnp.max(part, axis=0, keepdims=True)
        peak = top if peak is None else jnp.maximum(peak, top)
    total = jnp.zeros_like(peak)
    for t in range(slab.shape[0] // tile):
        total = total + jnp.sum(jnp.exp(logits[t * tile : (t + 1) * tile, :] - peak), axis=0, keepdims=True)
    chosen = row_of((tile, count), 0) == picked
    candidate = jnp.sum(jnp.where(chosen, logits[:tile, :], 0.0), axis=0, keepdims=True)
    return peak, total, candidate


def split_rows(exact):
    tile_row = row_of((EXTRA, LANES), 0)
    exact = jnp.broadcast_to(exact, (EXTRA, LANES))
    high = exact.astype(jnp.bfloat16).astype(jnp.float32)
    left = exact - high
    middle = left.astype(jnp.bfloat16).astype(jnp.float32)
    parts = jnp.where(tile_row == 0, high, jnp.where(tile_row == 1, middle, left - middle))
    return jnp.where(tile_row < 3, parts, 0.0)


def serve_kernel(
    got_hbm, slab_hbm, keys_hbm, values_hbm, out_hbm,
    out, got, slab, keys, values, logits, decoded, table, listed, sems, *, grid_y, grid_x, depth, rows, query_count, top_count, head_size
):
    sources = got.shape[0]
    slots = sources * depth
    columns = keys.shape[2]
    body = columns // LANES * rows
    slot_rows = depth * body
    copies = [
        pltpu.make_async_copy(source, target, sems.at[i])
        for i, (source, target) in enumerate(
            [
                (got_hbm, got),
                (slab_hbm, slab),
                (keys_hbm, keys),
                (values_hbm, values),
            ]
        )
    ]
    for copy in copies:
        copy.start()
    size = depth * query_count
    shared_rows = size * (columns // LANES)
    per_chunk = LANES // query_count
    lane = row_of((EXTRA, LANES), 1)
    tile_row = row_of((EXTRA, LANES), 0)

    copies[0].wait()
    found = [jnp.zeros((EXTRA, LANES), jnp.float32) for _ in range(-(-sources // EXTRA))]
    for source in range(sources):
        code = got[source, slot_rows + shared_rows :, :LANES].astype(jnp.float32)
        found[source // EXTRA] = jnp.where(tile_row == source % EXTRA, code, found[source // EXTRA])
    found = found[0] if len(found) == 1 else jnp.concatenate(found, axis=0)
    to_scalars(found.astype(jnp.int32), decoded, table, sems.at[5])

    count = 0
    chunks = [jnp.full((EXTRA, LANES), -1, jnp.int32) for _ in range(-(-slots // per_chunk))]
    for slot in range(slots):
        image, entry = table[slot // depth, slot % depth], table[slot // depth, EXTRA + slot % depth]
        query = lax.div(jnp.maximum(entry, 0), top_count)
        at = slot % per_chunk * query_count + query
        chunks[slot // per_chunk] = jnp.where(lane == at, image, chunks[slot // per_chunk])
        listed[count] = slot
        count = count + jnp.where(image >= 0, 1, 0)
    last = listed[jnp.maximum(count - 1, 0)]
    for g in range(UNROLL):
        listed[count + g] = last

    queries = jnp.concatenate(
        [
            jnp.concatenate(
                [
                    got[source, slot_rows + c * size : slot_rows + (c + 1) * size, :]
                    for c in range(columns // LANES)
                ],
                axis=1,
            )
            for source in range(sources)
        ],
        axis=0,
    )
    missing = len(chunks) * LANES - queries.shape[0]
    if missing:
        queries = jnp.concatenate([queries, jnp.zeros((missing, queries.shape[1]), queries.dtype)], axis=0)
    copies[1].wait()
    stats = index_stats(queries, slab, jnp.concatenate([chunk[:1] for chunk in chunks], axis=1), logits)
    for c in range(len(chunks)):
        tiles = [split_rows(stat[:, c * LANES : (c + 1) * LANES]) for stat in stats]
        tiles = [tiles[0], pltpu.roll(tiles[1], query_count, 1), pltpu.roll(tiles[2], 2 * query_count, 1)]
        for slot in range(c * per_chunk, min((c + 1) * per_chunk, slots)):
            source, z = slot // depth, slot % depth
            at = slot % per_chunk
            owner = owner_of(source, z, grid_y, grid_x, depth)
            place = lane // query_count
            tile = jnp.where(place == at, tiles[0], jnp.where(place == (at + 1) % per_chunk, tiles[1], tiles[2]))
            out[owner, body:, :] = tile.astype(jnp.bfloat16)

    copies[2].wait()
    copies[3].wait()
    spans = []
    at = 0
    while at < columns:
        width = min(2 * LANES, columns - at)
        lane_head = row_of((rows, width), 1) // head_size
        spans.append((at, width, [jnp.where(lane_head == h, 1.0, 0.0) for h in range(width // head_size)]))
        at += width

    def group(index, carry):
        chosen = [listed[index * UNROLL + g] for g in range(UNROLL)]
        places = [(lax.div(slot, depth), lax.rem(slot, depth)) for slot in chosen]
        images = [table[source, z] for source, z in places]
        owners = [owner_of(source, z, grid_y, grid_x, depth) for source, z in places]
        work = [(g, span) for g in range(UNROLL) for span in spans]
        scores = []
        for g, (at, width, masks) in work:
            source, z = places[g]
            pieces = [
                got[source, pl.ds(pl.multiple_of(z * body + c * rows, rows), rows), :]
                for c in range(at // LANES, (at + width) // LANES)
            ]
            query = pieces[0] if len(pieces) == 1 else jnp.concatenate(pieces, axis=1)
            spread = jnp.concatenate([query * mask.astype(query.dtype) for mask in masks], axis=0)
            scores.append(
                lax.dot_general(
                    spread,
                    keys[images[g], :, at : at + width],
                    (((1,), (1,)), ((), ())),
                    preferred_element_type=jnp.float32,
                )
            )
        scores = [score * head_size ** (-0.5) for score in scores]
        highest = [jnp.max(score, axis=-1, keepdims=True) for score in scores]
        powers = [jnp.exp(score - top) for score, top in zip(scores, highest)]
        totals = [jnp.sum(power, axis=-1, keepdims=True) for power in powers]
        weights = [(power / total).astype(jnp.bfloat16) for power, total in zip(powers, totals)]
        mixed = [
            jnp.dot(weight, values[images[g], :, at : at + width], preferred_element_type=jnp.float32)
            for weight, (g, (at, width, _)) in zip(weights, work)
        ]
        for mix, (g, (at, width, masks)) in zip(mixed, work):
            context = mix[:rows] * masks[0]
            for h in range(1, len(masks)):
                context = context + mix[h * rows : (h + 1) * rows] * masks[h]
            context = context.astype(jnp.bfloat16)
            for c in range(width // LANES):
                out[owners[g], (at // LANES + c) * rows : (at // LANES + c + 1) * rows, :] = context[
                    :, c * LANES : (c + 1) * LANES
                ]
        return carry

    lax.fori_loop(0, lax.div(count + UNROLL - 1, UNROLL), group, 0)
    copy = pltpu.make_async_copy(out, out_hbm, sems.at[6])
    copy.start()
    copy.wait()


def serve(got, slab, keys, values, grid_y, grid_x, depth, rows, query_count, top_count, head_size):
    sources = got.shape[0]
    slots = sources * depth
    body = keys.shape[2] // LANES * rows
    lanes = -(-slots * query_count // LANES) * LANES
    operands = [got, slab, keys, values]
    codes = (-(-sources // EXTRA) * EXTRA, LANES)
    return pl.pallas_call(
        functools.partial(
            serve_kernel,
            grid_y=grid_y,
            grid_x=grid_x,
            depth=depth,
            rows=rows,
            query_count=query_count,
            top_count=top_count,
            head_size=head_size,
        ),
        grid=(1,),
        in_specs=[pl.BlockSpec(memory_space=pltpu.HBM)] * 4,
        out_specs=pl.BlockSpec(memory_space=pltpu.HBM),
        scratch_shapes=[pltpu.VMEM((slots, body + EXTRA, LANES), jnp.bfloat16)]
        + [pltpu.VMEM(a.shape, a.dtype) for a in operands]
        + [
            pltpu.VMEM((slab.shape[0], lanes), jnp.float32),
            pltpu.VMEM(codes, jnp.int32),
            pltpu.SMEM(codes, jnp.int32),
            pltpu.SMEM((slots + UNROLL,), jnp.int32),
            pltpu.SemaphoreType.DMA((8,)),
        ],
        out_shape=pltpu.HBM((slots, body + EXTRA, LANES), jnp.bfloat16),
        compiler_params=pltpu.CompilerParams(vmem_limit_bytes=VMEM_LIMIT),
        cost_estimate=pl.CostEstimate(flops=8 << 30, bytes_accessed=14 << 20, transcendentals=2 << 20),
        name="serve",
    )(*[in_hbm(a) for a in operands])


def finish_kernel(
    shards, place, back_hbm, text_hbm, w_out_hbm, gain_hbm, found, out_hbm,
    exact, gathered, back, text, w_out, gain, out, sems, *, top_count, query_count, chunks, shift
):
    rows, width = text.shape[1:]
    body = back.shape[1] - EXTRA
    entries = query_count * top_count // chunks
    queries = query_count // chunks

    loads = [
        pltpu.make_async_copy(source, target, sems.at[chunks + i])
        for i, (source, target) in enumerate(
            [
                (back_hbm, back),
                (w_out_hbm, w_out),
                (text_hbm, text),
                (gain_hbm, gain),
            ]
        )
    ]
    for load in loads:
        load.start()
    loads[0].wait()
    parts = back[:, body:, :].astype(jnp.float32)
    joined = jnp.sum(jnp.where(row_of(parts.shape, 1) < 3, parts, 0.0), axis=1)
    joined = pltpu.roll(joined, lax.rem(LANES - place[0] * query_count, LANES), 1)
    exact[...] = joined
    peak = jnp.max(joined, axis=0, keepdims=True)
    scaled = jnp.exp(joined - peak) * pltpu.roll(joined, LANES - query_count, 1)
    total = jnp.sum(scaled, axis=0, keepdims=True)
    total = jnp.where(row_of(total.shape, 1) < query_count, total, 1.0)
    normalizers = peak + jnp.log(total)
    for query in range(query_count):
        picked = jnp.concatenate([exact[pl.ds(shards[query * top_count + k], 1), :] for k in range(top_count)], axis=0)
        lane = row_of(picked.shape, 1)
        candidate = jnp.sum(jnp.where(lane == 2 * query_count + query, picked, 0.0), axis=1, keepdims=True)
        result = candidate - normalizers[:, query : query + 1] + shift
        result = jnp.sum(jnp.where(lane == row_of(picked.shape, 0), result, 0.0), axis=0, keepdims=True)
        found[query : query + 1, :] = result[:, :top_count]

    for load in loads[1:]:
        load.wait()
    stores = []
    for chunk in range(chunks):
        first = chunk * queries
        for k in range(entries):
            shard = shards[chunk * entries + k]
            for j in range(body // rows):
                gathered[chunk, k * rows : (k + 1) * rows, j * LANES : (j + 1) * LANES] = back[
                    shard, j * rows : (j + 1) * rows, :
                ]
        mixed = jnp.dot(gathered[chunk], w_out[...], preferred_element_type=jnp.float32)
        states = text[first : first + queries].astype(jnp.float32).reshape(queries, 1, rows, width)
        summed = mixed.reshape(queries, top_count, rows, width) + states
        mean = jnp.mean(summed, axis=-1, keepdims=True)
        centred = summed - mean
        variance = jnp.mean(centred * centred, axis=-1, keepdims=True)
        normed = centred * lax.rsqrt(variance + EPSILON) * gain[...].reshape(1, 1, 1, width)
        out[first : first + queries] = normed.astype(jnp.bfloat16)
        store = pltpu.make_async_copy(
            out.at[pl.ds(first, queries)], out_hbm.at[pl.ds(first, queries)], sems.at[chunks + 4 + chunk]
        )
        store.start()
        stores.append(store)
    for store in stores:
        store.wait()


def finish(shards, place, back, text, w_out, gain, top_count, shift):
    query_count, rows, width = text.shape
    chunks = 2
    body = back.shape[1] - EXTRA
    entries = query_count * top_count
    return pl.pallas_call(
        functools.partial(finish_kernel, top_count=top_count, query_count=query_count, chunks=chunks, shift=shift),
        grid_spec=pltpu.PrefetchScalarGridSpec(
            num_scalar_prefetch=2,
            grid=(1,),
            in_specs=[pl.BlockSpec(memory_space=pltpu.HBM)] * 4,
            out_specs=[
                pl.BlockSpec((query_count, top_count), lambda i, *_: (0, 0)),
                pl.BlockSpec(memory_space=pltpu.HBM),
            ],
            scratch_shapes=[
                pltpu.VMEM((back.shape[0], LANES), jnp.float32),
                pltpu.VMEM((chunks, entries // chunks * rows, width), jnp.bfloat16),
                pltpu.VMEM(back.shape, back.dtype),
                pltpu.VMEM(text.shape, text.dtype),
                pltpu.VMEM(w_out.shape, w_out.dtype),
                pltpu.VMEM(gain.shape, gain.dtype),
                pltpu.VMEM((query_count, top_count, rows, width), jnp.bfloat16),
                pltpu.SemaphoreType.DMA((2 * chunks + 4,)),
            ],
        ),
        out_shape=[
            jax.ShapeDtypeStruct((query_count, top_count), jnp.float32),
            pltpu.HBM((query_count, top_count, rows, width), jnp.bfloat16),
        ],
        compiler_params=pltpu.CompilerParams(vmem_limit_bytes=VMEM_LIMIT),
        cost_estimate=pl.CostEstimate(
            flops=2 * entries * rows * width * width, bytes_accessed=7 << 20, transcendentals=0
        ),
        name="finish",
    )(shards, place, in_hbm(back), in_hbm(text), in_hbm(w_out), in_hbm(gain))


def project_rows(rows_in, weight):
    return jnp.einsum("spc,cd->spd", rows_in, weight, preferred_element_type=jnp.float32).astype(jnp.bfloat16)


def on_device(queries, slab, cand_ids, patches, text_states, w_query, w_key, w_value, w_out, norm_gain):
    shard_count = lax.axis_size("shard")
    shard_here = lax.axis_index("shard")
    core = lax.axis_index("rep")
    grid_y, depth, grid_x = GRIDS[shard_count]
    query_count = queries.shape[0]
    slab_count = slab.shape[0]
    top_count = cand_ids.shape[1]
    list_length = query_count * top_count
    text_count, model_width = text_states.shape[1:]
    head_size = model_width // HEADS
    here_x, here_z, here_y = shard_here % grid_x, shard_here // grid_x % depth, shard_here // (grid_x * depth)
    owned = depth // PAIR
    columns = [
        [(y * depth + k * PAIR + in_pair) * grid_x + x for k in range(owned)]
        for y in range(grid_y)
        for x in range(grid_x)
        for in_pair in range(PAIR)
    ]
    pairs = [
        [
            (y * depth + k * PAIR + in_pair) * grid_x + x
            for in_pair in range(PAIR)
            for y in range(grid_y)
            for x in range(grid_x)
        ]
        for k in range(owned)
    ]
    swap = [(0, 1), (1, 0)]
    w_query_other = lax.ppermute(w_query, "rep", swap)
    own_list = cand_ids.reshape(list_length)
    own_anchor = own_list // slab_count
    sent = pack(cand_ids, text_states.reshape(query_count * text_count, model_width), queries, slab_count)
    owners = lax.all_gather(sent, "shard", axis=0, tiled=True, axis_index_groups=columns)
    request = make_request(
        (here_z // PAIR * PAIR).reshape(1),
        owners.reshape(owned, sent.shape[0], model_width),
        w_query,
        w_query_other,
        grid_y,
        grid_x,
        text_count,
        query_count,
        top_count,
    )
    got = lax.all_to_all(request, "shard", split_axis=0, concat_axis=0, tiled=True, axis_index_groups=pairs)

    keys = project_rows(patches, jnp.concatenate([w_key, lax.ppermute(w_key, "rep", swap)], axis=1))
    values = project_rows(patches, jnp.concatenate([w_value, lax.ppermute(w_value, "rep", swap)], axis=1))
    w_out_other = lax.ppermute(w_out, "rep", swap)
    half = model_width // 2
    w_out_whole = jnp.where(
        core == 0,
        jnp.concatenate([w_out, w_out_other], axis=1),
        jnp.concatenate(
            [
                jnp.concatenate([w_out_other[half:], w_out[half:]], axis=1),
                jnp.concatenate([w_out_other[:half], w_out[:half]], axis=1),
            ],
            axis=0,
        ),
    )

    context = serve(
        got, slab, keys, values, grid_y, grid_x, owned, text_count, query_count, top_count, head_size
    )
    back = lax.all_to_all(context, "shard", split_axis=0, concat_axis=0, tiled=True)

    source = (here_z % PAIR * grid_y + here_y) * grid_x + here_x
    place = (source * owned + here_z // PAIR) % (LANES // query_count)
    retrieval, attended = finish(
        own_anchor,
        place.reshape(1),
        back,
        text_states,
        w_out_whole,
        norm_gain.reshape(1, model_width),
        top_count,
        math.log(slab_count * shard_count),
    )
    return (retrieval, attended)


def solution(mesh):
    in_specs = (
        P(("shard", "rep"), None),
        P("shard", None),
        P(("shard", "rep"), None),
        P("shard", None, None),
        P(("shard", "rep"), None, None),
        P(None, "rep"),
        P(None, "rep"),
        P(None, "rep"),
        P(None, "rep"),
        P(),
    )
    out_specs = (P(("shard", "rep"), None), P(("shard", "rep"), None, None, None))
    return jax.shard_map(
        on_device, mesh=mesh, in_specs=in_specs, out_specs=out_specs, check_vma=False
    )
```
